32 devices in a mesh: dp: 16 (over z, y, core), tensor: 2 (over x).
Axes of the slice: x: 2, y: 2, z: 4, core: 2. Of those that a mesh axis runs over, the one named last changes fastest.
Arguments:
- tokens: bfloat16 [32, 709, 768], P(('dp', 'tensor')), may hold values from -6 to 6
- text_len: int32 [32], P(('dp', 'tensor')), may hold values from 40 to 512, as said below
- box_coords: int32 [32, 2, 709], P(('dp', 'tensor')), may hold values from 0 to 1000
- w_query: bfloat16 [768, 768], P(None, 'tensor'), may hold values from -0.21875 to 0.21875
- b_query: bfloat16 [768], P('tensor'), may hold values from -3 to 3
- w_key: bfloat16 [768, 768], P(None, 'tensor'), may hold values from -0.21875 to 0.21875
- w_value: bfloat16 [768, 768], P(None, 'tensor'), may hold values from -0.21875 to 0.21875
- b_value: bfloat16 [768], P('tensor'), may hold values from -3 to 3
- w_out: bfloat16 [768, 768], P('tensor'), may hold values from -0.625 to 0.625
- b_out: bfloat16 [768], replicated, may hold values from -3 to 3
- table_seq: bfloat16 [12, 32], P('tensor'), may hold values from -3.5 to 3.5
- table_x: bfloat16 [12, 64], P('tensor'), may hold values from -3.5 to 3.5
- table_y: bfloat16 [12, 64], P('tensor'), may hold values from -3.5 to 3.5
- gain_attn: bfloat16 [768], replicated, may hold values from 0.099609375 to 1.8984375
- shift_attn: bfloat16 [768], replicated, may hold values from -1.75 to 1.75
- w_up: bfloat16 [768, 3072], P(None, 'tensor'), may hold values from -0.21875 to 0.21875
- b_up: bfloat16 [3072], P('tensor'), may hold values from -3 to 3
- w_down: bfloat16 [3072, 768], P('tensor'), may hold values from -0.21875 to 0.21875
- b_down: bfloat16 [768], replicated, may hold values from -3 to 3
- gain_ffn: bfloat16 [768], replicated, may hold values from 0.099609375 to 1.8984375
- shift_ffn: bfloat16 [768], replicated, may hold values from -1.75 to 1.75
- cotangent: bfloat16 [32, 709, 768], P(('dp', 'tensor')), may hold values from -6 to 6
Outputs:
- output: bfloat16 [32, 709, 768], P(('dp', 'tensor'))
- grad_tokens: float32 [32, 709, 768], P(('dp', 'tensor'))
- grad_w_query: float32 [768, 768], P(None, 'tensor')
- grad_b_query: float32 [768], P('tensor')
- grad_w_key: float32 [768, 768], P(None, 'tensor')
- grad_w_value: float32 [768, 768], P(None, 'tensor')
- grad_b_value: float32 [768], P('tensor')
- grad_w_out: float32 [768, 768], P('tensor')
- grad_b_out: float32 [768], replicated
- grad_table_seq: float32 [12, 32], P('tensor')
- grad_table_x: float32 [12, 64], P('tensor')
- grad_table_y: float32 [12, 64], P('tensor')
- grad_gain_attn: float32 [768], replicated
- grad_shift_attn: float32 [768], replicated
- grad_w_up: float32 [768, 3072], P(None, 'tensor')
- grad_b_up: float32 [3072], P('tensor')
- grad_w_down: float32 [3072, 768], P('tensor')
- grad_b_down: float32 [768], replicated
- grad_gain_ffn: float32 [768], replicated
- grad_shift_ffn: float32 [768], replicated
The draws below stay inside these ranges and needn't reach their ends.
Inputs may be any that keep to these rules, and one draw needn't show every extreme that they name: `text_len`: text slots in use in each item, the rest are padding; in every draw some item uses all 512 and some only 40.
All inputs are finite; a program needn't handle non-finite values.
Results may differ from the reference program's by a relative error of at most 0.014.
The reference program's roundings to bfloat16 on the way count: a program that leaves them out, or rounds other values in their place, can miss the bound.
Values may be sent and summed in bfloat16 or wider, within the bound.
No kernel may reach another device: no remote copies, remote signals or barrier semaphores. Data moves between devices by JAX's collectives and lax.ppermute only.
A program may use at most 192 MiB of HBM per device.

```python
import math
from functools import partial
import jax
import jax.numpy as jnp
from jax import lax

D = 768
HEADS = 12
HEAD_DIM = 64
FF = 3072
BUCKETS = 32
MAX_DIST = 128
BUCKETS_2D = 64
MAX_DIST_2D = 256
TEXT = 512
SHORT = 40
SEQ = 709
ITEMS = 32


def draw_text_len(key, part):
    key = jax.random.fold_in(key, 11)
    key_lengths, key_long, key_short = jax.random.split(key, 3)
    lengths = jax.random.randint(key_lengths, (ITEMS,), SHORT, TEXT + 1)
    longest = jax.random.randint(key_long, (), 0, ITEMS)
    shortest = (longest + 1 + jax.random.randint(key_short, (), 0, ITEMS - 1)) % ITEMS
    lengths = lengths.at[longest].set(TEXT).at[shortest].set(SHORT)
    return lengths.astype(jnp.int32)


def with_ends(array, rng, least, top_value):
    extent = array.shape
    spot = [jax.random.randint(jax.random.fold_in(rng, axis), (), 0, extent[axis]) for axis in range(len(extent))]
    array = array.at[tuple(spot)].set(least)
    longest = extent.index(max(extent))
    spot[longest] = (spot[longest] + 1) % extent[longest]
    return array.at[tuple(spot)].set(top_value)


def steps_of(own_key, dims, pieces, low, high):
    loudness, own = 1.0, jax.random.fold_in(own_key, 6)
    for position, shards_of in pieces:
        draws = jnp.exp(jax.random.uniform(jax.random.fold_in(own, position), (shards_of,), jnp.float32, low / len(pieces), high / len(pieces)))
        loudness = loudness * jnp.repeat(draws, dims[position] // shards_of).reshape([-1 if axis == position else 1 for axis in range(len(dims))])
    return loudness


def centred(key, dims, scale, reach, cuts=(), held_as=jnp.bfloat16):
    factor_of = steps_of(key, dims, cuts, -0.22, 0.18) if cuts else 1.0
    array = jax.random.normal(key, dims, jnp.float32) * scale * factor_of
    return jnp.minimum(jnp.maximum(array, -reach), reach).astype(held_as)


def setup_inputs(seed: int = 0) -> dict:
    seeds = jax.random.split(jax.random.key(seed), 23)
    tokens = centred(seeds[0], (ITEMS, SEQ, D), 1.0, 6.0, ((0, 32),))
    text_len = draw_text_len(jax.random.fold_in(seeds[22], 71), 0)
    box_coords = with_ends(jax.random.randint(seeds[2], (ITEMS, 2, SEQ), 0, 1001), jax.random.fold_in(seeds[2], 1), 0, 1000).astype(jnp.int32)
    w_query = centred(seeds[3], (D, D), D ** -0.5, 0.21875, ((1, 2),))
    b_query = centred(seeds[4], (D,), 0.5, 3.0, ((0, 2),))
    w_key = centred(seeds[5], (D, D), D ** -0.5, 0.21875, ((1, 2),))
    w_value = centred(seeds[6], (D, D), D ** -0.5, 0.21875, ((1, 2),))
    b_value = centred(seeds[7], (D,), 0.5, 3.0, ((0, 2),))
    w_out = centred(seeds[8], (D, D), (D // 8) ** -0.5, 0.625, ((0, 2),))
    b_out = centred(seeds[9], (D,), 0.5, 3.0)
    table_seq = centred(seeds[10], (HEADS, BUCKETS), 0.6, 3.5, ((0, 2),))
    table_x = centred(seeds[11], (HEADS, BUCKETS_2D), 0.6, 3.5, ((0, 2),))
    table_y = centred(seeds[12], (HEADS, BUCKETS_2D), 0.6, 3.5, ((0, 2),))
    gain_attn = jnp.clip(1.0 + 0.18 * jax.random.normal(seeds[13], (D,), jnp.float32), 0.099609375, 1.8984375).astype(jnp.bfloat16)
    shift_attn = centred(seeds[14], (D,), 0.3, 1.75)
    w_up = centred(seeds[15], (D, FF), D ** -0.5, 0.21875, ((1, 2),))
    b_up = centred(seeds[16], (FF,), 0.5, 3.0, ((0, 2),))
    w_down = centred(seeds[17], (FF, D), (FF // 4) ** -0.5, 0.21875, ((0, 2),))
    b_down = centred(seeds[18], (D,), 0.5, 3.0)
    gain_ffn = jnp.clip(1.0 + 0.18 * jax.random.normal(seeds[19], (D,), jnp.float32), 0.099609375, 1.8984375).astype(jnp.bfloat16)
    shift_ffn = centred(seeds[20], (D,), 0.3, 1.75)
    cotangent = centred(seeds[21], (ITEMS, SEQ, D), 1.0, 6.0, ((0, 32),))
    return dict(tokens=tokens, text_len=text_len, box_coords=box_coords, w_query=w_query, b_query=b_query, w_key=w_key, w_value=w_value, b_value=b_value, w_out=w_out, b_out=b_out, table_seq=table_seq, table_x=table_x, table_y=table_y, gain_attn=gain_attn, shift_attn=shift_attn, w_up=w_up, b_up=b_up, w_down=w_down, b_down=b_down, gain_ffn=gain_ffn, shift_ffn=shift_ffn, cotangent=cotangent)


layer_eps = 1e-05
masked_score = -1000000000.0

@jax.custom_vjp
def low(v):
    return lax.optimization_barrier(v.astype(jnp.bfloat16)).astype(jnp.float32)

@jax.custom_vjp
def low_back(v):
    return v

def low_keep(v):
    return (low(v), None)

def low_pass(kept, grad):
    return (grad,)

def back_keep(v):
    return (v, None)

def back_low(kept, grad):
    return (low(grad),)
low.defvjp(low_keep, low_pass)
low_back.defvjp(back_keep, back_low)

def bucket_edges(buckets, farthest):
    half_count = buckets // 2
    exact_count = half_count // 2
    result = list(range(1, exact_count + 1))
    for degree in range(1, exact_count):
        result.append(int(math.ceil(exact_count * (farthest / exact_count) ** (degree / exact_count) - 1e-09)))
    return result

def bucket_index(relative, buckets, farthest):
    distance = jnp.abs(relative)
    counted = (relative > 0).astype(jnp.int32) * (buckets // 2)
    for border in bucket_edges(buckets, farthest):
        counted = counted + (distance >= border).astype(jnp.int32)
    return counted

def item_buckets(box_item):
    places = jnp.arange(box_item.shape[1], dtype=jnp.int32)
    along_seq = bucket_index(places[None, :] - places[:, None], BUCKETS, MAX_DIST)
    across = box_item[0]
    along_x = bucket_index(across[None, :] - across[:, None], BUCKETS_2D, MAX_DIST_2D)
    upward = box_item[1]
    along_y = bucket_index(upward[None, :] - upward[:, None], BUCKETS_2D, MAX_DIST_2D)
    return (along_seq, along_x, along_y)

def product(left, right):
    return jnp.dot(left, right, precision=lax.Precision.HIGHEST)

def layer_norm(values, gain, shift):
    center = values - lax.optimization_barrier(jnp.mean(values, axis=-1, keepdims=True))
    spread = lax.optimization_barrier(jnp.mean(center * center, axis=-1, keepdims=True))
    return center * lax.rsqrt(spread + layer_eps) * gain + shift

def attend_item(tables, packed):
    queries, keys_in, values_in, length_now, box_item = packed
    scores = jnp.einsum('qhd,khd->hqk', queries, keys_in, precision=lax.Precision.HIGHEST) * HEAD_DIM ** (-0.5)
    for bucket, bias_table in zip(item_buckets(box_item), tables):
        scores = scores + jnp.take(bias_table, bucket, axis=1)
    scores = low_back(scores)
    places = jnp.arange(SEQ, dtype=jnp.int32)
    usable = (places < length_now) | (places >= TEXT)
    scores = jnp.where(usable[None, None, :], scores, masked_score)
    chances = low(jax.nn.softmax(scores, axis=-1))
    return jnp.einsum('hqk,khd->qhd', chances, values_in, precision=lax.Precision.HIGHEST)

def forward(params, inputs, text_len, box_coords):
    w_query, b_query, w_key, w_value, b_value, w_out, b_out, table_seq, table_x, table_y, gain_attn, shift_attn, w_up, b_up, w_down, b_down, gain_ffn, shift_ffn = params
    shaped = (ITEMS, SEQ, HEADS, HEAD_DIM)
    queries = low(low_back(product(inputs, w_query) + b_query)).reshape(shaped)
    keys_all = low(low_back(product(inputs, w_key))).reshape(shaped)
    values_all = low(low_back(product(inputs, w_value) + b_value)).reshape(shaped)
    tables = (table_seq, table_x, table_y)
    context = lax.map(jax.checkpoint(partial(attend_item, tables)), (queries, keys_all, values_all, text_len, box_coords))
    context = low(low_back(context.reshape(ITEMS, SEQ, HEADS * HEAD_DIM)))
    attn = low_back(product(context, w_out) + b_out)
    normed = layer_norm(inputs + attn, gain_attn, shift_attn)
    hidden_pre = low_back(product(low(normed), w_up) + b_up)
    activated = low(jax.nn.gelu(hidden_pre, approximate=False))
    branch = low_back(product(activated, w_down) + b_down)
    return layer_norm(normed + branch, gain_ffn, shift_ffn)

def reference(tokens, text_len, box_coords, w_query, b_query, w_key, w_value, b_value, w_out, b_out, table_seq, table_x, table_y, gain_attn, shift_attn, w_up, b_up, w_down, b_down, gain_ffn, shift_ffn, cotangent):
    params = (w_query.astype(jnp.float32), b_query.astype(jnp.float32), w_key.astype(jnp.float32), w_value.astype(jnp.float32), b_value.astype(jnp.float32), w_out.astype(jnp.float32), b_out.astype(jnp.float32), table_seq.astype(jnp.float32), table_x.astype(jnp.float32), table_y.astype(jnp.float32), gain_attn.astype(jnp.float32), shift_attn.astype(jnp.float32), w_up.astype(jnp.float32), b_up.astype(jnp.float32), w_down.astype(jnp.float32), b_down.astype(jnp.float32), gain_ffn.astype(jnp.float32), shift_ffn.astype(jnp.float32))
    inputs = tokens.astype(jnp.float32)

    def closed(params_in, inputs_in):
        return forward(params_in, inputs_in, text_len, box_coords)
    result, pullback = jax.vjp(closed, params, inputs)
    gradients, grad_in = pullback(cotangent.astype(jnp.float32))
    return (result.astype(jnp.bfloat16), grad_in, gradients[0], gradients[1], gradients[2], gradients[3], gradients[4], gradients[5], gradients[6], gradients[7], gradients[8], gradients[9], gradients[10], gradients[11], gradients[12], gradients[13], gradients[14], gradients[15], gradients[16], gradients[17])
```

```python
from functools import partial
import math

import jax
import jax.numpy as jnp
from jax import lax
from jax.experimental import pallas as pl
from jax.experimental.pallas import tpu as pltpu
from jax.sharding import PartitionSpec as P

HEAD_DIM = 64
BUCKETS = 32
MAX_DIST = 128
BUCKETS_2D = 64
MAX_DIST_2D = 256
TEXT = 512
layer_eps = 1e-05

f32 = jnp.float32
bf = jnp.bfloat16
i16 = jnp.int16
PT = 256
NT = (((1,), (1,)), ((), ()))
VM = 56 << 20

def bucket_edges(buckets, farthest):
    exact=buckets//4
    r=list(range(1,exact+1))
    for k in range(1,exact):
        r.append(int(math.ceil(exact*(farthest/exact)**(k/exact)-1e-09)))
    return r
def lane_gather(table, index):
    dn=lax.GatherDimensionNumbers(offset_dims=(),collapsed_slice_dims=(1,),start_index_map=(1,),operand_batching_dims=(0,),start_indices_batching_dims=(0,))
    return lax.gather(table,index[...,None],dn,(1,1),mode=lax.GatherScatterMode.PROMISE_IN_BOUNDS)

def prep_kernel(len_ref, box_ref, boxt_ref, tseq_ref, idx_ref, toep_ref, *, buckets2, dist2, buckets1, dist1, seq):
    rows, lanes = idx_ref.shape[1:]
    edges=bucket_edges(buckets2,dist2)
    near=[e for e in edges if e<128]; far=[e for e in edges if e>=128]
    half=buckets2//2
    n=len_ref[0]
    rb=16
    lane=lax.broadcasted_iota(jnp.int32,(rb,128),1)
    tab=jnp.zeros((rb,128),jnp.int32)
    for e in near: tab=tab+jnp.where(lane>=e,1,0)
    def body(i,_):
        r0=pl.multiple_of(i*rb,rb)
        r=pl.ds(r0,rb)
        place=lax.broadcasted_iota(jnp.int32,(rb,128),0)+r0
        ok=((place<n)|(place>=TEXT))&(place<seq)
        for ax in range(2):
            col=jnp.broadcast_to(boxt_ref[ax,r,:],(rb,128))
            for c in range(lanes//128):
                cs=slice(c*128,(c+1)*128)
                d=col-box_ref[ax:ax+1,cs]
                a=jnp.abs(d)
                b=lane_gather(tab,jnp.minimum(a,127))
                for e in far: b=b+jnp.where(a>=e,1,0)
                b=b+jnp.where(d>0,half,0)
                if ax==1: b=jnp.where(ok,b,buckets2)
                idx_ref[ax,r,cs]=b.astype(i16)
        return 0
    lax.fori_loop(0,rows//rb,body,0)
    edges1=bucket_edges(buckets1,dist1)
    for j in range(5):
        d=lax.broadcasted_iota(jnp.int32,(128,128),0)-lax.broadcasted_iota(jnp.int32,(128,128),1)+128*(j-2)
        a=jnp.abs(d)
        b=jnp.zeros_like(d)
        for e in edges1: b=b+jnp.where(a>=e,1,0)
        b=(b+jnp.where(d>0,buckets1//2,0)).astype(i16)
        for h in range(tseq_ref.shape[0]):
            toep_ref[h,j*128:(j+1)*128,:]=lane_gather(jnp.broadcast_to(tseq_ref[h:h+1,:],(128,128)),b)

def prep(length, box, tseq, *, rows, lanes, seq, buckets2=BUCKETS_2D, dist2=MAX_DIST_2D, buckets1=BUCKETS, dist1=MAX_DIST):
    H=tseq.shape[0]
    boxp=jnp.pad(box,((0,0),(0,lanes-seq)))
    boxt=boxp[:,:rows,None]
    ts=jnp.pad(tseq,((0,0),(0,128-tseq.shape[1])))
    return pl.pallas_call(partial(prep_kernel,buckets2=buckets2,dist2=dist2,buckets1=buckets1,dist1=dist1,seq=seq),
        out_shape=(jax.ShapeDtypeStruct((2,rows,lanes),i16),jax.ShapeDtypeStruct((H,640,128),bf)),
        in_specs=[pl.BlockSpec(memory_space=pltpu.SMEM)]+[pl.BlockSpec(memory_space=pltpu.VMEM)]*3,
        out_specs=(pl.BlockSpec(memory_space=pltpu.VMEM),)*2,
        compiler_params=pltpu.CompilerParams(vmem_limit_bytes=VM),name="buckets",
    )(length,boxp,boxt,ts)

def keep_rows(x,first_row,limit):
    rr=lax.broadcasted_iota(jnp.int32,(x.shape[0],1),0)+first_row
    return jnp.where(rr<limit,x,jnp.zeros_like(x))

def fwd_kernel(q_ref,k_ref,v_ref,idx_ref,toep_ref,tx_ref,ty_ref,ctx_ref,p_ref,s_ref):
    H,rows,PT=p_ref.shape
    nch=PT//128
    tile=pl.program_id(0)
    lane=lax.broadcasted_iota(jnp.int32,(1,128),1)
    first=lane<HEAD_DIM
    for hp in range(H//2):
        hs=slice(hp*128,(hp+1)*128)
        q=keep_rows(q_ref[:,hs],tile*PT,rows)*jnp.asarray(HEAD_DIM**-0.5,bf)
        for h in range(2):
            qm=jnp.where(first if h==0 else ~first,q,jnp.zeros_like(q))
            s_ref[2*hp+h]=lax.dot_general(k_ref[:,hs],qm,NT,preferred_element_type=f32)
    tabs=[(jnp.broadcast_to(tx_ref[h:h+1,:],(16,128)),jnp.broadcast_to(ty_ref[h:h+1,:],(16,128))) for h in range(H)]
    cuts=[(h,c) for c in range(nch) for h in range(H)]
    def pass1(g,ms):
        r0=pl.multiple_of(g*16,16); r=pl.ds(r0,16)
        sb=r0//128; off=r0%128
        out=[]
        for c in range(nch):
            cs=slice(c*128,(c+1)*128)
            ix=idx_ref[0,r,cs]; iy=idx_ref[1,r,cs]
            tr=pl.ds(pl.multiple_of((jnp.clip(sb-(tile*nch+c),-2,2)+2)*128+off,16),16)
            for h in range(H):
                s=s_ref[h,r,cs]+lane_gather(tabs[h][0],ix).astype(f32)+lane_gather(tabs[h][1],iy).astype(f32)+toep_ref[h,tr,:].astype(f32)
                s_ref[h,r,cs]=s
                out.append(jnp.maximum(ms[c*H+h],jnp.maximum(s[:8],s[8:])))
        return tuple(out)
    ms=lax.fori_loop(0,rows//16,pass1,tuple(jnp.full((8,128),-jnp.inf,f32) for _ in cuts))
    ms=[jnp.max(m,axis=0,keepdims=True) for m in ms]
    def pass2(g,ls):
        r=pl.ds(pl.multiple_of(g*16,16),16)
        out=[]
        for i,(h,c) in enumerate(cuts):
            cs=slice(c*128,(c+1)*128)
            e=jnp.exp(s_ref[h,r,cs]-ms[i])
            s_ref[h,r,cs]=e
            out.append(ls[i]+(e[:8]+e[8:]))
        return tuple(out)
    ls=lax.fori_loop(0,rows//16,pass2,tuple(jnp.zeros((8,128),f32) for _ in cuts))
    inv=[1.0/jnp.sum(l,axis=0,keepdims=True) for l in ls]
    def pass3(g,_):
        r=pl.ds(pl.multiple_of(g*16,16),16)
        for i,(h,c) in enumerate(cuts):
            cs=slice(c*128,(c+1)*128)
            p_ref[h,r,cs]=(s_ref[h,r,cs]*inv[i]).astype(bf)
        return 0
    lax.fori_loop(0,rows//16,pass3,0)
    for hp in range(H//2):
        hs=slice(hp*128,(hp+1)*128)
        vt=v_ref[:,hs].T
        o=[jnp.dot(vt[h*64:(h+1)*64],p_ref[2*hp+h],preferred_element_type=f32) for h in range(2)]
        ctx_ref[:,hs]=jnp.concatenate(o,0).T.astype(bf)

def attn_fwd(qkv,idx,toep,tx,ty):
    rows=qkv.shape[0]; W=qkv.shape[1]//3; H=W//HEAD_DIM; lanes=idx.shape[2]
    tx=jnp.pad(tx,((0,0),(0,128-tx.shape[1])))
    ty=jnp.concatenate([ty,jnp.full((H,128-ty.shape[1]),-1e9,bf)],1)
    whole=lambda shape: pl.BlockSpec(shape,lambda i:(0,)*len(shape))
    return pl.pallas_call(fwd_kernel,
        grid=(lanes//PT,),
        in_specs=[pl.BlockSpec((PT,W),lambda i:(i,0)),pl.BlockSpec((rows,W),lambda i:(0,1)),pl.BlockSpec((rows,W),lambda i:(0,2)),
                  pl.BlockSpec((2,rows,PT),lambda i:(0,0,i)),whole(toep.shape),whole(tx.shape),whole(ty.shape)],
        out_specs=(pl.BlockSpec((PT,W),lambda i:(i,0)),pl.BlockSpec((H,rows,PT),lambda i:(0,0,i))),
        out_shape=(jax.ShapeDtypeStruct((rows,W),bf),jax.ShapeDtypeStruct((H,rows,lanes),bf)),
        scratch_shapes=[pltpu.VMEM((H,rows,PT),f32)],
        compiler_params=pltpu.CompilerParams(vmem_limit_bytes=VM),name="attn_fwd",
        cost_estimate=pl.CostEstimate(flops=H*rows*lanes*256,bytes_accessed=H*rows*lanes*2,transcendentals=H*rows*lanes),
    )(qkv,qkv,qkv,idx,toep,tx,ty)

def bwd_kernel(q_ref,k_ref,v_ref,do_ref,p_ref,dq_ref,dk_ref,dv_ref,gs_ref,dp_ref,dka,dva):
    H,rows,PT=p_ref.shape
    nch=PT//128
    tile=pl.program_id(0); last=pl.num_programs(0)-1
    lane=lax.broadcasted_iota(jnp.int32,(1,128),1)
    first=lane<HEAD_DIM
    scale=HEAD_DIM**-0.5
    cuts=[(h,c) for c in range(nch) for h in range(H)]
    split=lambda x: (jnp.where(first,x,jnp.zeros_like(x)),jnp.where(first,jnp.zeros_like(x),x))
    for hp in range(H//2):
        hs=slice(hp*128,(hp+1)*128)
        dm=split(keep_rows(do_ref[:,hs],tile*PT,rows))
        for h in range(2):
            dp_ref[2*hp+h]=lax.dot_general(v_ref[:,hs],dm[h],NT,preferred_element_type=f32)
    def pass1(g,ds):
        r=pl.ds(pl.multiple_of(g*16,16),16)
        out=[]
        for i,(h,c) in enumerate(cuts):
            cs=slice(c*128,(c+1)*128)
            t=p_ref[h,r,cs].astype(f32)*dp_ref[h,r,cs]
            out.append(ds[i]+(t[:8]+t[8:]))
        return tuple(out)
    ds=lax.fori_loop(0,rows//16,pass1,tuple(jnp.zeros((8,128),f32) for _ in cuts))
    ds=[jnp.sum(d,axis=0,keepdims=True) for d in ds]
    def pass2(g,_):
        r=pl.ds(pl.multiple_of(g*16,16),16)
        for i,(h,c) in enumerate(cuts):
            cs=slice(c*128,(c+1)*128)
            gs_ref[h,r,cs]=(p_ref[h,r,cs].astype(f32)*(dp_ref[h,r,cs]-ds[i])).astype(bf)
        return 0
    lax.fori_loop(0,rows//16,pass2,0)
    @pl.when(tile==0)
    def _():
        dka[...]=jnp.zeros_like(dka); dva[...]=jnp.zeros_like(dva)
    for hp in range(H//2):
        hs=slice(hp*128,(hp+1)*128)
        kt=k_ref[:,hs].T
        o=[jnp.dot(kt[h*64:(h+1)*64],gs_ref[2*hp+h],preferred_element_type=f32) for h in range(2)]
        dq_ref[:,hs]=(jnp.concatenate(o,0)*scale).T.astype(bf)
        qm=split(keep_rows(q_ref[:,hs],tile*PT,rows))
        dm=split(keep_rows(do_ref[:,hs],tile*PT,rows))
        dka[:,hs]+=jnp.dot(gs_ref[2*hp],qm[0],preferred_element_type=f32)+jnp.dot(gs_ref[2*hp+1],qm[1],preferred_element_type=f32)
        dva[:,hs]+=jnp.dot(p_ref[2*hp],dm[0],preferred_element_type=f32)+jnp.dot(p_ref[2*hp+1],dm[1],preferred_element_type=f32)
    @pl.when(tile==last)
    def _():
        dk_ref[...]=(dka[...]*scale).astype(bf)
        dv_ref[...]=dva[...].astype(bf)

def attn_bwd(qkv,do,p):
    rows=qkv.shape[0]; W=qkv.shape[1]//3; H=W//HEAD_DIM; lanes=p.shape[2]
    tilew=pl.BlockSpec((PT,W),lambda i:(i,0))
    whole=lambda k: pl.BlockSpec((rows,W),lambda i,k=k:(0,k))
    big=pl.BlockSpec((H,rows,PT),lambda i:(0,0,i))
    o=jax.ShapeDtypeStruct((rows,W),bf)
    return pl.pallas_call(bwd_kernel,
        grid=(lanes//PT,),
        in_specs=[tilew,whole(1),whole(2),tilew,big],
        out_specs=(tilew,whole(0),whole(0),big),
        out_shape=(o,o,o,jax.ShapeDtypeStruct((H,rows,lanes),bf)),
        scratch_shapes=[pltpu.VMEM((H,rows,PT),f32),pltpu.VMEM((rows,W),f32),pltpu.VMEM((rows,W),f32)],
        compiler_params=pltpu.CompilerParams(vmem_limit_bytes=VM),name="attn_bwd",
        cost_estimate=pl.CostEstimate(flops=H*rows*lanes*640,bytes_accessed=H*rows*lanes*4,transcendentals=0),
    )(qkv,qkv,qkv,do,p)

def hist_kernel(gs_ref, go_ref, idx_ref, out_ref, toep_ref, acc, accT, *, buckets2):
    H, rows, lanes = gs_ref.shape
    step = pl.program_id(0)
    SB = 16
    heads = 2 * H

    @pl.when(step == 0)
    def _():
        acc[...] = jnp.zeros_like(acc)
        accT[...] = jnp.zeros_like(accT)

    iota = lax.broadcasted_iota(jnp.int32, (buckets2, lanes), 0).astype(i16)
    one = jnp.ones((buckets2, lanes), bf)
    zero = jnp.zeros((buckets2, lanes), bf)

    def body(i, _):
        r = pl.ds(pl.multiple_of(i * SB, SB), SB)
        s0 = step * rows + i * SB
        sb = s0 // 128
        off = pl.multiple_of(s0 % 128, SB)
        both = [gs_ref[:, r, :], go_ref[:, r, :]]
        for k in range(2):
            for h in range(H):
                for c in range(lanes // 128):
                    at = pl.ds(pl.multiple_of((jnp.clip(sb - c, -2, 2) + 2) * 128 + off, SB), SB)
                    accT[k * H + h, at, :] += both[k][h, :, c * 128:(c + 1) * 128].astype(f32)
        G = jnp.concatenate(both, 0).reshape(heads * SB, lanes)
        O = []
        for ax in range(2):
            ix = idx_ref[ax, r, :]
            for p in range(SB):
                O.append(jnp.where(iota == ix[p:p + 1, :], one, zero))
        acc[...] += lax.dot_general(jnp.concatenate(O, 0), G, NT, preferred_element_type=f32)
        return 0

    lax.fori_loop(0, rows // SB, body, 0)

    @pl.when(step == pl.num_programs(0) - 1)
    def _():
        lane = lax.broadcasted_iota(jnp.int32, (buckets2, heads * SB), 1) % SB
        for ax in range(2):
            t = jnp.zeros((buckets2, heads * SB), f32)
            for p in range(SB):
                at = (ax * SB + p) * buckets2
                t = t + jnp.where(lane == p, acc[at:at + buckets2, :], 0.0)
            out_ref[ax] = t
        m = lax.broadcasted_iota(jnp.int32, (128, 128), 1)
        turned = m + lax.broadcasted_iota(jnp.int32, (128, 128), 0)
        wraps = turned >= 128
        turned = jnp.where(wraps, turned - 128, turned)
        for h in range(heads):
            for j in (-1, 0, 1):
                x = lane_gather(accT[h, (j + 2) * 128:(j + 3) * 128, :], turned)
                at = 2 * (j + 1)
                toep_ref[h, at:at + 1, :] = jnp.sum(jnp.where(wraps, 0.0, x), axis=0, keepdims=True)
                toep_ref[h, at + 1:at + 2, :] = jnp.sum(jnp.where(wraps, x, 0.0), axis=0, keepdims=True)
            toep_ref[h, 6:7, :] = jnp.sum(accT[h, 0:128, :], axis=0, keepdims=True)
            toep_ref[h, 7:8, :] = jnp.sum(accT[h, 512:640, :], axis=0, keepdims=True)


def hist(gs, go, idx, SB=240):
    H, rows, lanes = gs.shape
    big = pl.BlockSpec((H, SB, lanes), lambda i: (0, i, 0))
    out, toep = pl.pallas_call(
        partial(hist_kernel, buckets2=BUCKETS_2D),
        grid=(rows // SB,),
        in_specs=[big, big, pl.BlockSpec((2, SB, lanes), lambda i: (0, i, 0))],
        out_specs=(pl.BlockSpec((2, BUCKETS_2D, 2 * H * 16), lambda i: (0, 0, 0)), pl.BlockSpec((2 * H, 8, 128), lambda i: (0, 0, 0))),
        out_shape=(jax.ShapeDtypeStruct((2, BUCKETS_2D, 2 * H * 16), f32), jax.ShapeDtypeStruct((2 * H, 8, 128), f32)),
        scratch_shapes=[pltpu.VMEM((32 * BUCKETS_2D, 2 * H * 16), f32), pltpu.VMEM((2 * H, 640, 128), f32)],
        compiler_params=pltpu.CompilerParams(vmem_limit_bytes=VM),
        name="table_sums",
        cost_estimate=pl.CostEstimate(flops=rows * 128 * lanes * 2 * H * 32, bytes_accessed=4 * H * rows * lanes, transcendentals=0),
    )(gs, go, idx)
    xy = out.reshape(2, BUCKETS_2D, 2 * H, 16).sum(3).transpose(0, 2, 1)
    line = toep.reshape(2 * H, 1024)
    base = jnp.array([-128, 0, 0, 128, 128, 256, -MAX_DIST - 128, MAX_DIST + 256])
    d = (base[:, None] - jnp.arange(128)).reshape(1024)
    b = jnp.zeros_like(d)
    for e in bucket_edges(BUCKETS, MAX_DIST):
        b = b + (jnp.abs(d) >= e)
    b = b + (d > 0) * (BUCKETS // 2)
    seq = jnp.dot(line, (b[:, None] == jnp.arange(BUCKETS)).astype(f32), precision=lax.Precision.HIGHEST)
    return seq, xy[0], xy[1]


def swap(value, axis, bit):
    count = lax.axis_size(axis)
    return lax.ppermute(value, axis, [(i, i ^ bit) for i in range(count)])


def side(axis, bit):
    return (lax.axis_index(axis) // bit) % 2


def half_of(value, axis, which):
    size = value.shape[axis] // 2
    return lax.dynamic_slice_in_dim(value, which * size, size, axis)


def join(mine, theirs, which, axis):
    low = jnp.where(which == 0, mine, theirs)
    high = jnp.where(which == 0, theirs, mine)
    return jnp.concatenate([low, high], axis)


def fetch(own):
    core = side("dp", 1)
    got = swap(half_of(own, 0, core), "tensor", 1)
    return join(got, swap(got, "dp", 1), core, 0)


def dp_bits():
    count = lax.axis_size("dp")
    bits = []
    bit = 1
    while bit < count:
        bits.append(bit)
        bit *= 2
    return bits


def add_low(a, b):
    return (a.astype(f32) + b.astype(f32)).astype(bf)


def reduce_weight(own, other):
    bits = dp_bits()
    core = side("dp", 1)
    both = jnp.stack([own, other])
    got = swap(half_of(both, 1, 1 - core), "dp", 1)
    both = add_low(half_of(both, 1, core), got)
    total = add_low(both[0], swap(both[1], "tensor", 1))
    for bit in bits[1:]:
        at = side("dp", bit)
        got = swap(half_of(total, 0, 1 - at), "dp", bit)
        total = add_low(half_of(total, 0, at), got)
    for bit in bits[::-1]:
        total = join(total, swap(total, "dp", bit), side("dp", bit), 0)
    return total.astype(f32)


def reduce_small(own, other):
    total = own + swap(other, "tensor", 1)
    for bit in dp_bits():
        total = total + swap(total, "dp", bit)
    return total


def norm_parts(values):
    center = values - jnp.mean(values, axis=1, keepdims=True)
    inverse = lax.rsqrt(jnp.mean(center * center, axis=1, keepdims=True) + layer_eps)
    return center * inverse, inverse


def norm_back(grad_scaled, scaled, inverse):
    return inverse * (
        grad_scaled
        - jnp.mean(grad_scaled, axis=1, keepdims=True)
        - scaled * jnp.mean(grad_scaled * scaled, axis=1, keepdims=True)
    )


def gelu_parts(v):
    cdf = 0.5 * (1.0 + lax.erf(v * (0.5 ** 0.5)))
    pdf = jnp.exp(-0.5 * v * v) * (1.0 / math.sqrt(2.0 * math.pi))
    return v * cdf, cdf + v * pdf


def mm(a, b):
    return jnp.dot(a, b, preferred_element_type=f32)


def mm_nt(a, b):
    return lax.dot_general(a, b, (((1,), (1,)), ((), ())), preferred_element_type=f32)


def mm_tn(a, b):
    return lax.dot_general(a, b, (((0,), (0,)), ((), ())), preferred_element_type=f32)


def per_device(
    tokens, text_len, box_coords, w_query, b_query, w_key, w_value, b_value, w_out, b_out,
    table_seq, table_x, table_y, gain_attn, shift_attn, w_up, b_up, w_down, b_down,
    gain_ffn, shift_ffn, cotangent,
):
    seq, width = tokens.shape[1:]
    rows = -(-seq // 240) * 240
    lanes = -(-rows // PT) * PT
    local = w_query.shape[1]
    heads = local // HEAD_DIM
    hidden = w_up.shape[1]

    smalls = [b_query, b_value, b_up, table_seq.reshape(-1), table_x.reshape(-1), table_y.reshape(-1)]
    small_other = swap(jnp.concatenate(smalls), "tensor", 1)
    others = []
    at = 0
    for piece in smalls:
        others.append(small_other[at:at + piece.shape[0]])
        at += piece.shape[0]
    bq_o, bv_o, bu_o = others[:3]
    ts_o, tx_o, ty_o = others[3].reshape(heads, -1), others[4].reshape(heads, -1), others[5].reshape(heads, -1)

    w_qkv = jnp.concatenate([w_query, w_key, w_value], 1)
    w_qkv_o = fetch(w_qkv)
    w_out_o = fetch(w_out)
    w_up_o = fetch(w_up)
    w_down_o = fetch(w_down)

    x = jnp.pad(tokens[0], ((0, rows - seq), (0, 0)))
    g = jnp.pad(cotangent[0], ((0, rows - seq), (0, 0)))

    def bias_of(bq, bv):
        return jnp.concatenate([bq, jnp.zeros((local,), bf), bv]).astype(f32)

    idx, toep = prep(text_len, box_coords[0], jnp.concatenate([table_seq, ts_o], 0), rows=rows, lanes=lanes, seq=seq)
    qkv = (mm(x, w_qkv) + bias_of(b_query, b_value)).astype(bf)
    ctx, prob = attn_fwd(qkv, idx, toep[:heads], table_x, table_y)
    qkv_o = (mm(x, w_qkv_o) + bias_of(bq_o, bv_o)).astype(bf)
    ctx_o, prob_o = attn_fwd(qkv_o, idx, toep[heads:], tx_o, ty_o)

    attn = mm(ctx, w_out) + mm(ctx_o, w_out_o) + b_out.astype(f32)
    n1, inv1 = norm_parts(x.astype(f32) + attn)
    normed = n1 * gain_attn.astype(f32) + shift_attn.astype(f32)
    low = normed.astype(bf)
    act, slope = gelu_parts(mm(low, w_up) + b_up.astype(f32))
    act_o, slope_o = gelu_parts(mm(low, w_up_o) + bu_o.astype(f32))
    act, act_o = act.astype(bf), act_o.astype(bf)
    slope, slope_o = slope.astype(bf), slope_o.astype(bf)
    branch = mm(act, w_down) + mm(act_o, w_down_o) + b_down.astype(f32)
    n2, inv2 = norm_parts(normed + branch)
    output = (n2 * gain_ffn.astype(f32) + shift_ffn.astype(f32)).astype(bf)[:seq][None]

    gf = g.astype(f32)
    grad_gain_ffn = jnp.sum(gf * n2, axis=0)
    grad_shift_ffn = jnp.sum(gf, axis=0)
    grad_mid = norm_back(gf * gain_ffn.astype(f32), n2, inv2)
    gb = grad_mid.astype(bf)
    grad_b_down = jnp.sum(gb.astype(f32), axis=0)
    grad_w_down = reduce_weight(mm_tn(act, gb).astype(bf), mm_tn(act_o, gb).astype(bf))
    gh = (mm_nt(gb, w_down) * slope.astype(f32)).astype(bf)
    gh_o = (mm_nt(gb, w_down_o) * slope_o.astype(f32)).astype(bf)
    grad_b_up = jnp.sum(gh.astype(f32), axis=0)
    grad_b_up_o = jnp.sum(gh_o.astype(f32), axis=0)
    grad_w_up = reduce_weight(mm_tn(low, gh).astype(bf), mm_tn(low, gh_o).astype(bf))
    grad_normed = mm_nt(gh, w_up) + mm_nt(gh_o, w_up_o) + grad_mid
    grad_gain_attn = jnp.sum(grad_normed * n1, axis=0)
    grad_shift_attn = jnp.sum(grad_normed, axis=0)
    grad_first = norm_back(grad_normed * gain_attn.astype(f32), n1, inv1)
    ga = grad_first.astype(bf)
    grad_b_out = jnp.sum(ga.astype(f32), axis=0)
    grad_w_out = reduce_weight(mm_tn(ctx, ga).astype(bf), mm_tn(ctx_o, ga).astype(bf))
    gc = mm_nt(ga, w_out).astype(bf)
    gc_o = mm_nt(ga, w_out_o).astype(bf)
    dq, dk, dv, gs = attn_bwd(qkv, gc, prob)
    dq_o, dk_o, dv_o, gs_o = attn_bwd(qkv_o, gc_o, prob_o)
    dqkv = jnp.concatenate([dq, dk, dv], 1)
    dqkv_o = jnp.concatenate([dq_o, dk_o, dv_o], 1)
    grad_w_qkv = reduce_weight(mm_tn(x, dqkv).astype(bf), mm_tn(x, dqkv_o).astype(bf))
    grad_tokens = (grad_first + mm_nt(dqkv, w_qkv) + mm_nt(dqkv_o, w_qkv_o))[:seq][None]
    t_seq, t_x, t_y = hist(gs, gs_o, idx)

    sums = jnp.sum(dqkv.astype(f32), axis=0)
    sums_o = jnp.sum(dqkv_o.astype(f32), axis=0)
    shared = [grad_b_out, grad_gain_attn, grad_shift_attn, grad_b_down, grad_gain_ffn, grad_shift_ffn]

    def packed(bias_sums, up, at):
        tables = [t[at:at + heads].reshape(-1) for t in (t_seq, t_x, t_y)]
        return jnp.concatenate([bias_sums[:local], bias_sums[2 * local:], up] + tables + shared)

    small = reduce_small(packed(sums, grad_b_up, 0), packed(sums_o, grad_b_up_o, heads))
    shapes = [(local,), (local,), (hidden,), table_seq.shape, table_x.shape, table_y.shape] + [(width,)] * 6
    pieces = []
    at = 0
    for shape in shapes:
        size = math.prod(shape)
        pieces.append(small[at:at + size].reshape(shape))
        at += size
    g_bq, g_bv, g_bu, g_ts, g_tx, g_ty, g_bo, g_ga, g_sa, g_bd, g_gf, g_sf = pieces
    return (
        output, grad_tokens,
        grad_w_qkv[:, :local], g_bq, grad_w_qkv[:, local:2 * local], grad_w_qkv[:, 2 * local:], g_bv,
        grad_w_out, g_bo, g_ts, g_tx, g_ty, g_ga, g_sa, grad_w_up, g_bu, grad_w_down, g_bd, g_gf, g_sf,
    )


def solution(mesh):
    item = P(("dp", "tensor"), None, None)
    column, row, split, copied = P(None, "tensor"), P("tensor", None), P("tensor"), P()
    return jax.shard_map(
        per_device,
        mesh=mesh,
        in_specs=(
            item, P(("dp", "tensor")), item, column, split, column, column, split, row, copied,
            row, row, row, copied, copied, column, split, row, copied, copied, copied, item,
        ),
        out_specs=(
            item, item, column, split, column, column, split, row, copied, row, row, row,
            copied, copied, column, split, row, copied, copied, copied,
        ),
        check_vma=False,
    )
```

```python
from functools import partial
import math

import jax
import jax.numpy as jnp
from jax import lax
from jax.experimental import pallas as pl
from jax.experimental.pallas import tpu as pltpu
from jax.sharding import PartitionSpec as P

HEAD_DIM = 64
BUCKETS = 32
MAX_DIST = 128
BUCKETS_2D = 64
MAX_DIST_2D = 256
TEXT = 512
layer_eps = 1e-05

f32 = jnp.float32
bf = jnp.bfloat16
i16 = jnp.int16
PT = 256
NT = (((1,), (1,)), ((), ()))
VM = 56 << 20

def bucket_edges(buckets, farthest):
    exact=buckets//4
    r=list(range(1,exact+1))
    for k in range(1,exact):
        r.append(int(math.ceil(exact*(farthest/exact)**(k/exact)-1e-09)))
    return r
def lane_gather(table, index):
    dn=lax.GatherDimensionNumbers(offset_dims=(),collapsed_slice_dims=(1,),start_index_map=(1,),operand_batching_dims=(0,),start_indices_batching_dims=(0,))
    return lax.gather(table,index[...,None],dn,(1,1),mode=lax.GatherScatterMode.PROMISE_IN_BOUNDS)

def prep_kernel(len_ref, box_ref, own_ref, oth_ref, idx_ref, toep_ref, toep_o_ref, line_ref, col_ref, *, seq):
    rows, lanes = idx_ref.shape[1:]
    heads = toep_ref.shape[0]
    edges = bucket_edges(BUCKETS_2D, MAX_DIST_2D)
    near = [e for e in edges if e < 128]
    far = [e for e in edges if e >= 128]
    n = len_ref[0]
    rb = 16
    line_ref[...] = jnp.zeros_like(line_ref)
    line_ref[0:2, 0:seq] = box_ref[...].astype(f32)
    col_ref[...] = line_ref[...].T
    lane = lax.broadcasted_iota(jnp.int32, (rb, 128), 1)
    tab = jnp.zeros((rb, 128), jnp.int32)
    for e in near:
        tab = tab + jnp.where(lane >= e, 1, 0)
    tab = tab.astype(i16)

    def body(i, _):
        r = pl.ds(pl.multiple_of(i * rb, rb), rb)
        place = lax.broadcasted_iota(jnp.int32, (rb, 128), 0) + i * rb
        ok = ((place < n) | (place >= TEXT)) & (place < seq)
        for ax in range(2):
            col = jnp.broadcast_to(col_ref[r, ax:ax + 1], (rb, 128))
            for c in range(lanes // 128):
                cs = slice(c * 128, (c + 1) * 128)
                d = col - line_ref[ax:ax + 1, cs]
                a = jnp.abs(d)
                b = jnp.where(d > 0, float(BUCKETS_2D // 2), 0.0)
                for e in far:
                    b = b + jnp.where(a >= e, 1.0, 0.0)
                b = b.astype(jnp.int32).astype(i16) + lane_gather(tab, jnp.minimum(a, 127.0).astype(jnp.int32).astype(i16))
                if ax == 1:
                    b = jnp.where(ok, b.astype(jnp.int32), BUCKETS_2D).astype(i16)
                idx_ref[ax, r, cs] = b
        return 0

    lax.fori_loop(0, rows // rb, body, 0, unroll=5)
    for j in range(5):
        d = lax.broadcasted_iota(jnp.int32, (128, 128), 0) - lax.broadcasted_iota(jnp.int32, (128, 128), 1) + 128 * (j - 2)
        a = jnp.abs(d)
        b = jnp.zeros_like(d)
        for e in bucket_edges(BUCKETS, MAX_DIST):
            b = b + jnp.where(a >= e, 1, 0)
        b = (b + jnp.where(d > 0, BUCKETS // 2, 0)).astype(i16)
        for src, dst in ((own_ref, toep_ref), (oth_ref, toep_o_ref)):
            for h in range(heads):
                dst[h, j * 128:(j + 1) * 128, :] = lane_gather(jnp.broadcast_to(src[2 + h:3 + h, 0:128], (128, 128)), b)


VMEM = pl.BlockSpec(memory_space=pltpu.VMEM)
SMEM = pl.BlockSpec(memory_space=pltpu.SMEM)
ANY = pl.BlockSpec(memory_space=pl.ANY)


def prep(length, box, own, oth, heads, rows, lanes):
    seq = box.shape[1]
    toep = jax.ShapeDtypeStruct((heads, 640, 128), bf)
    return pl.pallas_call(
        partial(prep_kernel, seq=seq),
        out_shape=(jax.ShapeDtypeStruct((2, rows, lanes), i16), toep, toep),
        in_specs=[SMEM, VMEM, VMEM, VMEM],
        out_specs=(VMEM,) * 3,
        scratch_shapes=[pltpu.VMEM((8, lanes), f32), pltpu.VMEM((lanes, 8), f32)],
        compiler_params=pltpu.CompilerParams(vmem_limit_bytes=VM),
        name="buckets",
    )(length, box, own, oth)


def pack_kernel(bq, bv, bu, ts, tx, ty, bo, ga, sa, bd, gf, sf, small_ref, wide_ref):
    local = bq.shape[0]
    heads = ts.shape[0]
    hidden = bu.shape[0]
    small_ref[...] = jnp.zeros_like(small_ref)
    small_ref[0:1, 0:hidden] = bu[...][None]
    small_ref[1:2, 0:local] = bq[...][None]
    small_ref[1:2, 2 * local:3 * local] = bv[...][None]
    small_ref[2:2 + heads, 0:ts.shape[1]] = ts[...]
    small_ref[2:2 + heads, 128:128 + tx.shape[1]] = tx[...]
    small_ref[2:2 + heads, 256:384] = jnp.full((heads, 128), -1e9, bf)
    small_ref[2:2 + heads, 256:256 + ty.shape[1]] = ty[...]
    wide_ref[...] = jnp.zeros_like(wide_ref)
    for i, v in enumerate((bo, ga, sa, bd, gf, sf)):
        wide_ref[i:i + 1, :] = v[...].astype(f32)[None]


def pack(split, copied, width, hidden):
    return pl.pallas_call(
        pack_kernel,
        out_shape=(jax.ShapeDtypeStruct((16, hidden), bf), jax.ShapeDtypeStruct((8, width), f32)),
        in_specs=[VMEM] * 12,
        out_specs=(VMEM,) * 2,
        name="pack",
    )(*split, *copied)


def keep_rows(x,first_row,limit):
    rr=lax.broadcasted_iota(jnp.int32,(x.shape[0],1),0)+first_row
    return jnp.where(rr<limit,x,jnp.zeros_like(x))

def fwd_kernel(q_ref, k_ref, v_ref, idx_ref, toep_ref, small_ref, ctx_ref, p_ref, s_ref):
    H,rows,PT=p_ref.shape
    nch=PT//128
    tile=pl.program_id(0)
    lane=lax.broadcasted_iota(jnp.int32,(1,128),1)
    first=lane<HEAD_DIM
    for hp in range(H//2):
        hs=slice(hp*128,(hp+1)*128)
        q=keep_rows(q_ref[:,hs],tile*PT,rows)*jnp.asarray(HEAD_DIM**-0.5,bf)
        for h in range(2):
            qm=jnp.where(first if h==0 else ~first,q,jnp.zeros_like(q))
            s_ref[2*hp+h]=lax.dot_general(k_ref[:,hs],qm,NT,preferred_element_type=f32)
    tabs=[(jnp.broadcast_to(small_ref[2+h:3+h,128:256],(16,128)),jnp.broadcast_to(small_ref[2+h:3+h,256:384],(16,128))) for h in range(H)]
    cuts=[(h,c) for c in range(nch) for h in range(H)]
    def pass1(g,ms):
        r0=pl.multiple_of(g*16,16); r=pl.ds(r0,16)
        sb=r0//128; off=r0%128
        out=[]
        for c in range(nch):
            cs=slice(c*128,(c+1)*128)
            ix=idx_ref[0,r,cs]; iy=idx_ref[1,r,cs]
            tr=pl.ds(pl.multiple_of((jnp.clip(sb-(tile*nch+c),-2,2)+2)*128+off,16),16)
            gx=[lane_gather(tabs[h][0],ix) for h in range(H)]
            gy=[lane_gather(tabs[h][1],iy) for h in range(H)]
            for h in range(H):
                s=s_ref[h,r,cs]+gx[h].astype(f32)+gy[h].astype(f32)+toep_ref[h,tr,:].astype(f32)
                s_ref[h,r,cs]=s
                out.append(jnp.maximum(ms[c*H+h],jnp.maximum(s[:8],s[8:])))
        return tuple(out)
    ms=lax.fori_loop(0,rows//16,pass1,tuple(jnp.full((8,128),-jnp.inf,f32) for _ in cuts),unroll=9)
    ms=[jnp.max(m,axis=0,keepdims=True) for m in ms]
    def pass2(g,ls):
        r=pl.ds(pl.multiple_of(g*16,16),16)
        out=[]
        for i,(h,c) in enumerate(cuts):
            cs=slice(c*128,(c+1)*128)
            e=jnp.exp(s_ref[h,r,cs]-ms[i])
            s_ref[h,r,cs]=e
            out.append(ls[i]+(e[:8]+e[8:]))
        return tuple(out)
    ls=lax.fori_loop(0,rows//16,pass2,tuple(jnp.zeros((8,128),f32) for _ in cuts),unroll=5)
    inv=[1.0/jnp.sum(l,axis=0,keepdims=True) for l in ls]
    def pass3(g,_):
        r=pl.ds(pl.multiple_of(g*16,16),16)
        for i,(h,c) in enumerate(cuts):
            cs=slice(c*128,(c+1)*128)
            p_ref[h,r,cs]=(s_ref[h,r,cs]*inv[i]).astype(bf)
        return 0
    lax.fori_loop(0,rows//16,pass3,0,unroll=5)
    for hp in range(H//2):
        hs=slice(hp*128,(hp+1)*128)
        vt=v_ref[:,hs].T
        o=[jnp.dot(vt[h*64:(h+1)*64],p_ref[2*hp+h],preferred_element_type=f32) for h in range(2)]
        ctx_ref[:,hs]=jnp.concatenate(o,0).T.astype(bf)

def attn_fwd(q, k, v, idx, toep, small):
    rows, W = q.shape
    H = W // HEAD_DIM
    lanes = idx.shape[2]
    whole = lambda shape: pl.BlockSpec(shape, lambda i: (0,) * len(shape))
    return pl.pallas_call(
        fwd_kernel,
        grid=(lanes // PT,),
        in_specs=[pl.BlockSpec((PT, W), lambda i: (i, 0)), whole((rows, W)), whole((rows, W)), pl.BlockSpec((2, rows, PT), lambda i: (0, 0, i)), whole(toep.shape), whole(small.shape)],
        out_specs=(pl.BlockSpec((PT, W), lambda i: (i, 0)), pl.BlockSpec((H, rows, PT), lambda i: (0, 0, i))),
        out_shape=(jax.ShapeDtypeStruct((rows, W), bf), jax.ShapeDtypeStruct((H, rows, lanes), bf)),
        scratch_shapes=[pltpu.VMEM((H, rows, PT), f32)],
        compiler_params=pltpu.CompilerParams(vmem_limit_bytes=VM),
        name="attn_fwd",
        cost_estimate=pl.CostEstimate(flops=H * rows * lanes * 4096, bytes_accessed=H * rows * lanes * 2, transcendentals=H * rows * lanes),
    )(q, k, v, idx, toep, small)


def skip_refs(kernel, first, count, *refs):
    kernel(*refs[:first], *refs[first + count:])


def bwd_kernel(q_ref,k_ref,v_ref,do_ref,p_ref,dq_ref,dk_ref,dv_ref,gs_ref,dp_ref,dka,dva):
    H,rows,PT=p_ref.shape
    nch=PT//128
    tile=pl.program_id(0); last=pl.num_programs(0)-1
    lane=lax.broadcasted_iota(jnp.int32,(1,128),1)
    first=lane<HEAD_DIM
    scale=HEAD_DIM**-0.5
    cuts=[(h,c) for c in range(nch) for h in range(H)]
    split=lambda x: (jnp.where(first,x,jnp.zeros_like(x)),jnp.where(first,jnp.zeros_like(x),x))
    for hp in range(H//2):
        hs=slice(hp*128,(hp+1)*128)
        dm=split(keep_rows(do_ref[:,hs],tile*PT,rows))
        for h in range(2):
            dp_ref[2*hp+h]=lax.dot_general(v_ref[:,hs],dm[h],NT,preferred_element_type=f32)
    def pass1(g,ds):
        r=pl.ds(pl.multiple_of(g*16,16),16)
        out=[]
        for i,(h,c) in enumerate(cuts):
            cs=slice(c*128,(c+1)*128)
            t=p_ref[h,r,cs].astype(f32)*dp_ref[h,r,cs]
            out.append(ds[i]+(t[:8]+t[8:]))
        return tuple(out)
    ds=lax.fori_loop(0,rows//16,pass1,tuple(jnp.zeros((8,128),f32) for _ in cuts),unroll=9)
    ds=[jnp.sum(d,axis=0,keepdims=True) for d in ds]
    def pass2(g,_):
        r=pl.ds(pl.multiple_of(g*16,16),16)
        for i,(h,c) in enumerate(cuts):
            cs=slice(c*128,(c+1)*128)
            gs_ref[h,r,cs]=(p_ref[h,r,cs].astype(f32)*(dp_ref[h,r,cs]-ds[i])).astype(bf)
        return 0
    lax.fori_loop(0,rows//16,pass2,0,unroll=9)
    @pl.when(tile==0)
    def _():
        dka[...]=jnp.zeros_like(dka); dva[...]=jnp.zeros_like(dva)
    for hp in range(H//2):
        hs=slice(hp*128,(hp+1)*128)
        kt=k_ref[:,hs].T
        o=[jnp.dot(kt[h*64:(h+1)*64],gs_ref[2*hp+h],preferred_element_type=f32) for h in range(2)]
        dq_ref[:,hs]=(jnp.concatenate(o,0)*scale).T.astype(bf)
        qm=split(keep_rows(q_ref[:,hs],tile*PT,rows))
        dm=split(keep_rows(do_ref[:,hs],tile*PT,rows))
        dka[:,hs]+=jnp.dot(gs_ref[2*hp],qm[0],preferred_element_type=f32)+jnp.dot(gs_ref[2*hp+1],qm[1],preferred_element_type=f32)
        dva[:,hs]+=jnp.dot(p_ref[2*hp],dm[0],preferred_element_type=f32)+jnp.dot(p_ref[2*hp+1],dm[1],preferred_element_type=f32)
    @pl.when(tile==last)
    def _():
        dk_ref[...]=(dka[...]*scale).astype(bf)
        dv_ref[...]=dva[...].astype(bf)

def attn_bwd(q, k, v, do, p, after=()):
    rows, W = q.shape
    H = W // HEAD_DIM
    lanes = p.shape[2]
    tilew = pl.BlockSpec((PT, W), lambda i: (i, 0))
    whole = pl.BlockSpec((rows, W), lambda i: (0, 0))
    big = pl.BlockSpec((H, rows, PT), lambda i: (0, 0, i))
    o = jax.ShapeDtypeStruct((rows, W), bf)
    return pl.pallas_call(
        partial(skip_refs, bwd_kernel, 5, len(after)),
        grid=(lanes // PT,),
        in_specs=[tilew, whole, whole, tilew, big] + [ANY] * len(after),
        out_specs=(tilew, whole, whole, big),
        out_shape=(o, o, o, jax.ShapeDtypeStruct((H, rows, lanes), bf)),
        scratch_shapes=[pltpu.VMEM((H, rows, PT), f32), pltpu.VMEM((rows, W), f32), pltpu.VMEM((rows, W), f32)],
        compiler_params=pltpu.CompilerParams(vmem_limit_bytes=VM),
        name="attn_bwd",
        cost_estimate=pl.CostEstimate(flops=H * rows * lanes * 4096, bytes_accessed=H * rows * lanes * 4, transcendentals=0),
    )(q, k, v, do, p, *after)


def hist_kernel(gs_ref, go_ref, idx_ref, out_ref, toep_ref, acc, accT, *, part):
    H, rows, lanes = gs_ref.shape
    SB = 16
    heads = 2 * H
    near = BUCKETS_2D // 2
    step = pl.program_id(0)

    @pl.when(step == 0)
    def _():
        acc[...] = jnp.zeros_like(acc)
        accT[...] = jnp.zeros_like(accT)

    iota = lax.broadcasted_iota(jnp.int32, (near, lanes), 0).astype(i16)
    one = jnp.ones((near, lanes), bf)
    zero = jnp.zeros((near, lanes), bf)

    def body(i, _):
        r = pl.ds(pl.multiple_of(i * SB, SB), SB)
        s0 = (part + step) * rows + i * SB
        sb = s0 // 128
        off = pl.multiple_of(s0 % 128, SB)
        idx = [idx_ref[ax, r, :] for ax in range(2)]
        positive = [(x >= near).astype(i16).astype(jnp.int32) > 0 for x in idx]
        cols = [[], []]
        for ref in (gs_ref, go_ref):
            for h in range(H):
                full = ref[h, r, :].astype(f32)
                k = len(cols[0])
                for c in range(lanes // 128):
                    at = pl.ds(pl.multiple_of((jnp.clip(sb - c, -2, 2) + 2) * 128 + off, SB), SB)
                    accT[k, at, :] += full[:, c * 128:(c + 1) * 128]
                for ax in range(2):
                    some = jnp.where(positive[ax], full, 0.0)
                    cols[ax].append([jnp.concatenate([full[t:t + 8], some[t:t + 8]], 0).astype(bf) for t in (0, 8)])
        for ax in range(2):
            ix = jnp.bitwise_and(idx[ax], jnp.asarray(near - 1, i16))
            left = []
            right = []
            for t in range(2):
                left.append(jnp.concatenate([jnp.where(iota == ix[t * 8 + p:t * 8 + p + 1, :], one, zero) for p in range(8)], 0))
                right.append(jnp.concatenate([x[t] for x in cols[ax]], 0))
            acc[ax] += lax.dot_general(jnp.concatenate(left, 1), jnp.concatenate(right, 1), NT, preferred_element_type=f32)
        return 0

    lax.fori_loop(0, rows // SB, body, 0, unroll=3)

    @pl.when(step == pl.num_programs(0) - 1)
    def _():
        lane = lax.broadcasted_iota(jnp.int32, (near, heads * SB), 1) % 8
        for ax in range(2):
            t = jnp.zeros((near, heads * SB), f32)
            for p in range(8):
                t = t + jnp.where(lane == p, acc[ax, p * near:(p + 1) * near, :], 0.0)
            out_ref[ax] = t
        m = lax.broadcasted_iota(jnp.int32, (128, 128), 1)
        turned = m + lax.broadcasted_iota(jnp.int32, (128, 128), 0)
        wraps = turned >= 128
        turned = jnp.where(wraps, turned - 128, turned)
        for h in range(heads):
            for j in (-1, 0, 1):
                x = lane_gather(accT[h, (j + 2) * 128:(j + 3) * 128, :], turned)
                at = 2 * (j + 1)
                toep_ref[h, at:at + 1, :] = jnp.sum(jnp.where(wraps, 0.0, x), axis=0, keepdims=True)
                toep_ref[h, at + 1:at + 2, :] = jnp.sum(jnp.where(wraps, x, 0.0), axis=0, keepdims=True)
            toep_ref[h, 6:7, :] = jnp.sum(accT[h, 0:128, :], axis=0, keepdims=True)
            toep_ref[h, 7:8, :] = jnp.sum(accT[h, 512:640, :], axis=0, keepdims=True)


def hist(gs, go, idx, part, parts, after=()):
    H, rows, lanes = gs.shape
    SB = 48
    steps = rows // SB // parts
    part = part * steps
    near = BUCKETS_2D // 2
    big = pl.BlockSpec((H, SB, lanes), lambda i: (0, part + i, 0))
    return pl.pallas_call(
        partial(skip_refs, partial(hist_kernel, part=part), 3, len(after)),
        grid=(steps,),
        in_specs=[big, big, pl.BlockSpec((2, SB, lanes), lambda i: (0, part + i, 0))] + [ANY] * len(after),
        out_specs=(pl.BlockSpec((2, near, 2 * H * 16), lambda i: (0, 0, 0)), pl.BlockSpec((2 * H, 8, 128), lambda i: (0, 0, 0))),
        out_shape=(jax.ShapeDtypeStruct((2, near, 2 * H * 16), f32), jax.ShapeDtypeStruct((2 * H, 8, 128), f32)),
        scratch_shapes=[pltpu.VMEM((2, 8 * near, 2 * H * 16), f32), pltpu.VMEM((2 * H, 640, 128), f32)],
        compiler_params=pltpu.CompilerParams(vmem_limit_bytes=VM),
        name="table_sums",
        cost_estimate=pl.CostEstimate(flops=steps * SB * 128 * lanes * 2 * H * 32, bytes_accessed=4 * H * steps * SB * lanes, transcendentals=0),
    )(gs, go, idx, *after)


def tables_of(sums):
    out = sum(s[0] for s in sums)
    toep = sum(s[1] for s in sums)
    heads = toep.shape[0]
    xy = out.reshape(2, BUCKETS_2D // 2, heads, 2, 8).sum(4).transpose(0, 2, 3, 1)
    xy = jnp.concatenate([xy[:, :, 0] - xy[:, :, 1], xy[:, :, 1]], 2)
    line = toep.reshape(heads, 1024)
    base = jnp.array([-128, 0, 0, 128, 128, 256, -MAX_DIST - 128, MAX_DIST + 256])
    d = (base[:, None] - jnp.arange(128)).reshape(1024)
    b = jnp.zeros_like(d)
    for e in bucket_edges(BUCKETS, MAX_DIST):
        b = b + (jnp.abs(d) >= e)
    b = b + (d > 0) * (BUCKETS // 2)
    seq = jnp.dot(line, (b[:, None] == jnp.arange(BUCKETS)).astype(f32), precision=lax.Precision.HIGHEST)
    return seq, xy[0], xy[1]


def swap(value, axis, bit=1):
    count = lax.axis_size(axis)
    return lax.ppermute(value, axis, [(i, i ^ bit) for i in range(count)])


def half_of(value, axis, which):
    size = value.shape[axis] // 2
    return lax.dynamic_slice_in_dim(value, which * size, size, axis)


def join(mine, theirs, which, axis):
    low = jnp.where(which == 0, mine, theirs)
    high = jnp.where(which == 0, theirs, mine)
    return jnp.concatenate([low, high], axis)


def far_bits():
    count = lax.axis_size("far")
    bits = []
    bit = 1
    while bit < count:
        bits.append(bit)
        bit *= 2
    return bits


def add_low(a, b):
    return (a.astype(f32) + b.astype(f32)).astype(bf)


def core_sum(own, other):
    core = lax.axis_index("core")
    both = jnp.stack([own, other])
    return add_low(half_of(both, 1, core), swap(half_of(both, 1, 1 - core), "core"))


def tensor_sum(both):
    return add_low(both[0], swap(both[1], "tensor"))


def far_halve(total, bit):
    at = (lax.axis_index("far") // bit) % 2
    return add_low(half_of(total, 0, at), swap(half_of(total, 0, 1 - at), "far", bit))


def far_double(total, bit):
    return join(total, swap(total, "far", bit), (lax.axis_index("far") // bit) % 2, 0)


def core_join(total):
    return join(total, swap(total, "core"), lax.axis_index("core"), 0).astype(f32)


def reduce_small(own, other):
    total = own + swap(other, "tensor")
    total = total + swap(total, "core")
    for bit in far_bits():
        total = total + swap(total, "far", bit)
    return total


def norm_parts(values):
    center = values - jnp.mean(values, axis=1, keepdims=True)
    inverse = lax.rsqrt(jnp.mean(center * center, axis=1, keepdims=True) + layer_eps)
    return center * inverse, inverse


def norm_back(grad_scaled, scaled, inverse):
    return inverse * (
        grad_scaled
        - jnp.mean(grad_scaled, axis=1, keepdims=True)
        - scaled * jnp.mean(grad_scaled * scaled, axis=1, keepdims=True)
    )


def gelu_parts(v):
    cdf = 0.5 * (1.0 + lax.erf(v * (0.5 ** 0.5)))
    pdf = jnp.exp(-0.5 * v * v) * (1.0 / math.sqrt(2.0 * math.pi))
    return v * cdf, cdf + v * pdf


def mm(a, b):
    return jnp.dot(a, b, preferred_element_type=f32)


def mm_nt(a, b):
    return lax.dot_general(a, b, (((1,), (1,)), ((), ())), preferred_element_type=f32)


def mm_tn(a, b):
    return lax.dot_general(a, b, (((0,), (0,)), ((), ())), preferred_element_type=f32)


def per_device(
    tokens, text_len, box_coords, w_query, b_query, w_key, w_value, b_value, w_out, b_out,
    table_seq, table_x, table_y, gain_attn, shift_attn, w_up, b_up, w_down, b_down,
    gain_ffn, shift_ffn, cotangent,
):
    seq, width = tokens.shape[1:]
    rows = -(-seq // 240) * 240
    lanes = -(-rows // PT) * PT
    local = w_query.shape[1]
    heads = local // HEAD_DIM
    hidden = w_up.shape[1]
    core = lax.axis_index("core")

    small, wide = pack(
        [b_query, b_value, b_up, table_seq, table_x, table_y],
        [b_out, gain_attn, shift_attn, b_down, gain_ffn, shift_ffn], width, hidden,
    )
    small_o = swap(small, "tensor")
    b_out, gain_attn, shift_attn, b_down, gain_ffn, shift_ffn = [wide[i:i + 1] for i in range(6)]

    def fetch(mine):
        got = swap(mine, "tensor")
        return join(got, swap(got, "core"), core, mine.ndim - 2)

    wqkv_o = fetch(jnp.stack([half_of(w, 0, core) for w in (w_query, w_key, w_value)]))
    wq_o, wk_o, wv_o = wqkv_o[0], wqkv_o[1], wqkv_o[2]
    wo_o, wu_o, wd_o = [fetch(half_of(w, 0, core)) for w in (w_out, w_up, w_down)]

    x = jnp.pad(tokens[0], ((0, rows - seq), (0, 0)))
    g = jnp.pad(cotangent[0], ((0, rows - seq), (0, 0)))

    def project(wq, wk, wv, vectors):
        bias = vectors[1:2].astype(f32)
        return (
            (mm(x, wq) + bias[:, :local]).astype(bf),
            mm(x, wk).astype(bf),
            (mm(x, wv) + bias[:, 2 * local:3 * local]).astype(bf),
        )

    idx, toep, toep_o = prep(text_len, box_coords[0], small, small_o, heads, rows, lanes)
    q, k, v = project(w_query, w_key, w_value, small)
    ctx, prob = attn_fwd(q, k, v, idx, toep, small)
    q_o, k_o, v_o = project(wq_o, wk_o, wv_o, small_o)
    ctx_o, prob_o = attn_fwd(q_o, k_o, v_o, idx, toep_o, small_o)

    attn = mm(ctx, w_out) + mm(ctx_o, wo_o) + b_out
    n1, inv1 = norm_parts(x.astype(f32) + attn)
    normed = n1 * gain_attn + shift_attn
    low = normed.astype(bf)
    act, slope = gelu_parts(mm(low, w_up) + small[0:1].astype(f32))
    act_o, slope_o = gelu_parts(mm(low, wu_o) + small_o[0:1].astype(f32))
    act, act_o = act.astype(bf), act_o.astype(bf)
    slope, slope_o = slope.astype(bf), slope_o.astype(bf)
    branch = mm(act, w_down) + mm(act_o, wd_o) + b_down
    n2, inv2 = norm_parts(normed + branch)
    output = (n2 * gain_ffn + shift_ffn).astype(bf)[:seq][None]

    gf = g.astype(f32)
    grad_gain_ffn = jnp.sum(gf * n2, axis=0)
    grad_shift_ffn = jnp.sum(gf, axis=0)
    grad_mid = norm_back(gf * gain_ffn, n2, inv2)
    gb = grad_mid.astype(bf)
    grad_b_down = jnp.sum(gb.astype(f32), axis=0)
    down = core_sum(mm_tn(act, gb).astype(bf), mm_tn(act_o, gb).astype(bf))
    gh = (mm_nt(gb, w_down) * slope.astype(f32)).astype(bf)
    gh_o = (mm_nt(gb, wd_o) * slope_o.astype(f32)).astype(bf)
    grad_b_up = jnp.sum(gh.astype(f32), axis=0)
    grad_b_up_o = jnp.sum(gh_o.astype(f32), axis=0)
    grad_normed = mm_nt(gh, w_up) + mm_nt(gh_o, wu_o) + grad_mid
    grad_gain_attn = jnp.sum(grad_normed * n1, axis=0)
    grad_shift_attn = jnp.sum(grad_normed, axis=0)
    grad_first = norm_back(grad_normed * gain_attn, n1, inv1)
    ga = grad_first.astype(bf)
    grad_b_out = jnp.sum(ga.astype(f32), axis=0)
    gc = mm_nt(ga, w_out).astype(bf)
    gc_o = mm_nt(ga, wo_o).astype(bf)
    bits = far_bits()

    def wide_rows(first, second):
        second = second.reshape(-1, first.shape[1])
        extra = -(first.shape[0] + second.shape[0]) % (2 * lax.axis_size("far"))
        return jnp.concatenate([first, second, jnp.zeros((extra, first.shape[1]), bf)], 0)

    up = core_sum(
        wide_rows(mm_tn(low, gh).astype(bf), mm_tn(ctx, ga).astype(bf)),
        wide_rows(mm_tn(low, gh_o).astype(bf), mm_tn(ctx_o, ga).astype(bf)),
    )
    dq, dk, dv, gs = attn_bwd(q, k, v, gc, prob, (up,))
    down = tensor_sum(down)
    dq_o, dk_o, dv_o, gs_o = attn_bwd(q_o, k_o, v_o, gc_o, prob_o, (down,))
    grads = [mm_tn(x, d).astype(bf) for d in (dq, dk, dv, dq_o, dk_o, dv_o)]
    qkv = core_sum(jnp.concatenate(grads[:3], 1), jnp.concatenate(grads[3:], 1))
    up = tensor_sum(up)
    sums = [hist(gs, gs_o, idx, 0, 3, (qkv, up))]
    up = far_halve(up, bits[0])
    sums.append(hist(gs, gs_o, idx, 1, 3, (up,)))
    up = far_halve(up, bits[1])
    qkv = tensor_sum(qkv)
    sums.append(hist(gs, gs_o, idx, 2, 3, (up, qkv)))
    for bit in bits[2:]:
        up = far_halve(up, bit)
    for bit in bits[::-1]:
        up = far_double(up, bit)
    for bit in bits:
        qkv = far_halve(qkv, bit)
    for bit in bits[::-1]:
        qkv = far_double(qkv, bit)
    down = lax.psum(down, "far")
    late = lax.optimization_barrier((sums[-1][0], down, dq, dk, dv, dq_o, dk_o, dv_o))
    grad_w_down = core_join(late[1])
    up = core_join(up)
    grad_w_up = up[:width]
    grad_w_out = up[width:width + w_out.size // hidden].reshape(w_out.shape)
    qkv = core_join(qkv)
    t_seq, t_x, t_y = tables_of(sums)
    grad_tokens = grad_first
    for d, w in zip(late[2:], (w_query, w_key, w_value, wq_o, wk_o, wv_o)):
        grad_tokens = grad_tokens + mm_nt(d, w)
    grad_tokens = grad_tokens[:seq][None]

    bias_sums = [jnp.sum(d.astype(f32), axis=0) for d in (dq, dv, dq_o, dv_o)]
    shared = [grad_b_out, grad_gain_attn, grad_shift_attn, grad_b_down, grad_gain_ffn, grad_shift_ffn]

    def packed(query_sum, value_sum, up_sum, at):
        tables = [t[at:at + heads].reshape(-1) for t in (t_seq, t_x, t_y)]
        return jnp.concatenate([query_sum, value_sum, up_sum] + tables + shared)

    totals = reduce_small(packed(*bias_sums[:2], grad_b_up, 0), packed(*bias_sums[2:], grad_b_up_o, heads))
    shapes = [(local,), (local,), (hidden,), table_seq.shape, table_x.shape, table_y.shape] + [(width,)] * 6
    pieces = []
    at = 0
    for shape in shapes:
        size = math.prod(shape)
        pieces.append(totals[at:at + size].reshape(shape))
        at += size
    g_bq, g_bv, g_bu, g_ts, g_tx, g_ty, g_bo, g_ga, g_sa, g_bd, g_gf, g_sf = pieces
    return (
        output, grad_tokens,
        qkv[:, :local], g_bq, qkv[:, local:2 * local], qkv[:, 2 * local:], g_bv,
        grad_w_out, g_bo, g_ts, g_tx, g_ty, g_ga, g_sa, grad_w_up, g_bu, grad_w_down, g_bd, g_gf, g_sf,
    )


def solution(mesh):
    grid = mesh.devices.shape
    mesh = jax.sharding.Mesh(mesh.devices.reshape(grid[0] // 2, 2, grid[1]), ("far", "core", "tensor"))
    every = ("far", "core", "tensor")
    item = P(every, None, None)
    column, row, split, copied = P(None, "tensor"), P("tensor", None), P("tensor"), P()
    return jax.shard_map(
        per_device,
        mesh=mesh,
        in_specs=(
            item, P(every), item, column, split, column, column, split, row, copied,
            row, row, row, copied, copied, column, split, row, copied, copied, copied, item,
        ),
        out_specs=(
            item, item, column, split, column, column, split, row, copied, row, row, row,
            copied, copied, column, split, row, copied, copied, copied,
        ),
        check_vma=False,
    )
```

```python
from functools import partial
import math

import jax
import jax.numpy as jnp
from jax import lax
from jax.experimental import pallas as pl
from jax.experimental.pallas import tpu as pltpu
from jax.sharding import PartitionSpec as P

HEAD_DIM = 64
BUCKETS = 32
MAX_DIST = 128
BUCKETS_2D = 64
MAX_DIST_2D = 256
TEXT = 512
layer_eps = 1e-05

f32 = jnp.float32
bf = jnp.bfloat16
i16 = jnp.int16
PT = 256
NT = (((1,), (1,)), ((), ()))
VM = 56 << 20

BRIEF = pl.CostEstimate(flops=10_000_000_000, bytes_accessed=1, transcendentals=0)


def bucket_edges(buckets, farthest):
    exact=buckets//4
    r=list(range(1,exact+1))
    for k in range(1,exact):
        r.append(int(math.ceil(exact*(farthest/exact)**(k/exact)-1e-09)))
    return r
def lane_gather(table, index):
    dn=lax.GatherDimensionNumbers(offset_dims=(),collapsed_slice_dims=(1,),start_index_map=(1,),operand_batching_dims=(0,),start_indices_batching_dims=(0,))
    return lax.gather(table,index[...,None],dn,(1,1),mode=lax.GatherScatterMode.PROMISE_IN_BOUNDS)

def prep_kernel(len_ref, box_ref, own_ref, oth_ref, idx_ref, toep_ref, toep_o_ref, line_ref, col_ref, *, seq):
    rows, lanes = idx_ref.shape[1:]
    heads = toep_ref.shape[0]
    edges = bucket_edges(BUCKETS_2D, MAX_DIST_2D)
    near = [e for e in edges if e < 128]
    far = [e for e in edges if e >= 128]
    n = len_ref[0]
    rb = 16
    line_ref[...] = jnp.zeros_like(line_ref)
    line_ref[0:2, 0:seq] = box_ref[...].astype(f32)
    col_ref[...] = line_ref[...].T
    lane = lax.broadcasted_iota(jnp.int32, (rb, 128), 1)
    tab = jnp.zeros((rb, 128), jnp.int32)
    for e in near:
        tab = tab + jnp.where(lane >= e, 1, 0)
    tab = tab.astype(i16)

    def body(i, _):
        r = pl.ds(pl.multiple_of(i * rb, rb), rb)
        place = lax.broadcasted_iota(jnp.int32, (rb, 128), 0) + i * rb
        ok = ((place < n) | (place >= TEXT)) & (place < seq)
        for ax in range(2):
            col = jnp.broadcast_to(col_ref[r, ax:ax + 1], (rb, 128))
            for c in range(lanes // 128):
                cs = slice(c * 128, (c + 1) * 128)
                d = col - line_ref[ax:ax + 1, cs]
                a = jnp.abs(d)
                b = jnp.where(d > 0, float(BUCKETS_2D // 2), 0.0)
                for e in far:
                    b = b + jnp.where(a >= e, 1.0, 0.0)
                b = b.astype(jnp.int32).astype(i16) + lane_gather(tab, jnp.minimum(a, 127.0).astype(jnp.int32).astype(i16))
                if ax == 1:
                    b = jnp.where(ok, b.astype(jnp.int32), BUCKETS_2D).astype(i16)
                idx_ref[ax, r, cs] = b
        return 0

    lax.fori_loop(0, rows // rb, body, 0, unroll=5)
    for j in range(5):
        d = lax.broadcasted_iota(jnp.int32, (128, 128), 0) - lax.broadcasted_iota(jnp.int32, (128, 128), 1) + 128 * (j - 2)
        a = jnp.abs(d)
        b = jnp.zeros_like(d)
        for e in bucket_edges(BUCKETS, MAX_DIST):
            b = b + jnp.where(a >= e, 1, 0)
        b = (b + jnp.where(d > 0, BUCKETS // 2, 0)).astype(i16)
        for src, dst in ((own_ref, toep_ref), (oth_ref, toep_o_ref)):
            for h in range(heads):
                dst[h, j * 128:(j + 1) * 128, :] = lane_gather(jnp.broadcast_to(src[2 + h:3 + h, 0:128], (128, 128)), b)


VMEM = pl.BlockSpec(memory_space=pltpu.VMEM)
SMEM = pl.BlockSpec(memory_space=pltpu.SMEM)
ANY = pl.BlockSpec(memory_space=pl.ANY)


def prep(length, box, own, oth, heads, rows, lanes):
    seq = box.shape[1]
    toep = jax.ShapeDtypeStruct((heads, 640, 128), bf)
    return pl.pallas_call(
        partial(prep_kernel, seq=seq),
        out_shape=(jax.ShapeDtypeStruct((2, rows, lanes), i16), toep, toep),
        in_specs=[SMEM, VMEM, VMEM, VMEM],
        out_specs=(VMEM,) * 3,
        scratch_shapes=[pltpu.VMEM((8, lanes), f32), pltpu.VMEM((lanes, 8), f32)],
        compiler_params=pltpu.CompilerParams(vmem_limit_bytes=VM),
        name="buckets",
        cost_estimate=BRIEF,
    )(length, box, own, oth)


def pack_kernel(bq, bv, bu, ts, tx, ty, bo, ga, sa, bd, gf, sf, small_ref, wide_ref):
    local = bq.shape[0]
    heads = ts.shape[0]
    hidden = bu.shape[0]
    small_ref[...] = jnp.zeros_like(small_ref)
    small_ref[0:1, 0:hidden] = bu[...][None]
    small_ref[1:2, 0:local] = bq[...][None]
    small_ref[1:2, 2 * local:3 * local] = bv[...][None]
    small_ref[2:2 + heads, 0:ts.shape[1]] = ts[...]
    small_ref[2:2 + heads, 128:128 + tx.shape[1]] = tx[...]
    small_ref[2:2 + heads, 256:384] = jnp.full((heads, 128), -1e9, bf)
    small_ref[2:2 + heads, 256:256 + ty.shape[1]] = ty[...]
    wide_ref[...] = jnp.zeros_like(wide_ref)
    for i, v in enumerate((bo, ga, sa, bd, gf, sf)):
        wide_ref[i:i + 1, :] = v[...].astype(f32)[None]


def pack(split, copied, width, hidden):
    return pl.pallas_call(
        pack_kernel,
        out_shape=(jax.ShapeDtypeStruct((16, hidden), bf), jax.ShapeDtypeStruct((8, width), f32)),
        in_specs=[VMEM] * 12,
        out_specs=(VMEM,) * 2,
        name="pack",
        cost_estimate=BRIEF,
    )(*split, *copied)


def keep_rows(x,first_row,limit):
    rr=lax.broadcasted_iota(jnp.int32,(x.shape[0],1),0)+first_row
    return jnp.where(rr<limit,x,jnp.zeros_like(x))

def fwd_kernel(q_ref, k_ref, v_ref, idx_ref, toep_ref, small_ref, ctx_ref, p_ref, s_ref):
    H,rows,PT=p_ref.shape
    nch=PT//128
    tile=pl.program_id(0)
    lane=lax.broadcasted_iota(jnp.int32,(1,128),1)
    first=lane<HEAD_DIM
    for hp in range(H//2):
        hs=slice(hp*128,(hp+1)*128)
        q=keep_rows(q_ref[:,hs],tile*PT,rows)*jnp.asarray(HEAD_DIM**-0.5,bf)
        for h in range(2):
            qm=jnp.where(first if h==0 else ~first,q,jnp.zeros_like(q))
            s_ref[2*hp+h]=lax.dot_general(k_ref[:,hs],qm,NT,preferred_element_type=f32)
    tabs=[(jnp.broadcast_to(small_ref[2+h:3+h,128:256],(16,128)),jnp.broadcast_to(small_ref[2+h:3+h,256:384],(16,128))) for h in range(H)]
    cuts=[(h,c) for c in range(nch) for h in range(H)]
    def pass1(g,ms):
        r0=pl.multiple_of(g*16,16); r=pl.ds(r0,16)
        sb=r0//128; off=r0%128
        out=[]
        for c in range(nch):
            cs=slice(c*128,(c+1)*128)
            ix=idx_ref[0,r,cs]; iy=idx_ref[1,r,cs]
            tr=pl.ds(pl.multiple_of((jnp.clip(sb-(tile*nch+c),-2,2)+2)*128+off,16),16)
            gx=[lane_gather(tabs[h][0],ix) for h in range(H)]
            gy=[lane_gather(tabs[h][1],iy) for h in range(H)]
            for h in range(H):
                s=s_ref[h,r,cs]+gx[h].astype(f32)+gy[h].astype(f32)+toep_ref[h,tr,:].astype(f32)
                s_ref[h,r,cs]=s
                out.append(jnp.maximum(ms[c*H+h],jnp.maximum(s[:8],s[8:])))
        return tuple(out)
    ms=lax.fori_loop(0,rows//16,pass1,tuple(jnp.full((8,128),-jnp.inf,f32) for _ in cuts),unroll=9)
    ms=[jnp.max(m,axis=0,keepdims=True) for m in ms]
    def pass2(g,ls):
        r=pl.ds(pl.multiple_of(g*16,16),16)
        out=[]
        for i,(h,c) in enumerate(cuts):
            cs=slice(c*128,(c+1)*128)
            e=jnp.exp(s_ref[h,r,cs]-ms[i])
            s_ref[h,r,cs]=e
            out.append(ls[i]+(e[:8]+e[8:]))
        return tuple(out)
    ls=lax.fori_loop(0,rows//16,pass2,tuple(jnp.zeros((8,128),f32) for _ in cuts),unroll=5)
    inv=[1.0/jnp.sum(l,axis=0,keepdims=True) for l in ls]
    def pass3(g,_):
        r=pl.ds(pl.multiple_of(g*16,16),16)
        for i,(h,c) in enumerate(cuts):
            cs=slice(c*128,(c+1)*128)
            p_ref[h,r,cs]=(s_ref[h,r,cs]*inv[i]).astype(bf)
        return 0
    lax.fori_loop(0,rows//16,pass3,0,unroll=5)
    for hp in range(H//2):
        hs=slice(hp*128,(hp+1)*128)
        vt=v_ref[:,hs].T
        o=[jnp.dot(vt[h*64:(h+1)*64],p_ref[2*hp+h],preferred_element_type=f32) for h in range(2)]
        ctx_ref[:,hs]=jnp.concatenate(o,0).T.astype(bf)

def attn_fwd(q, k, v, W, idx, toep, small, after=()):
    rows = q[0].shape[0]
    H = W // HEAD_DIM
    lanes = idx.shape[2]
    whole = lambda shape: pl.BlockSpec(shape, lambda i: (0,) * len(shape))
    column = lambda at: pl.BlockSpec((rows, W), lambda i: (0, at))
    return pl.pallas_call(
        partial(skip_refs, fwd_kernel, 6, len(after)),
        grid=(lanes // PT,),
        in_specs=[pl.BlockSpec((PT, W), lambda i: (i, q[1])), column(k[1]), column(v[1]), pl.BlockSpec((2, rows, PT), lambda i: (0, 0, i)), whole(toep.shape), whole(small.shape)] + [ANY] * len(after),
        out_specs=(pl.BlockSpec((PT, W), lambda i: (i, 0)), pl.BlockSpec((H, rows, PT), lambda i: (0, 0, i))),
        out_shape=(jax.ShapeDtypeStruct((rows, W), bf), jax.ShapeDtypeStruct((H, rows, lanes), bf)),
        scratch_shapes=[pltpu.VMEM((H, rows, PT), f32)],
        compiler_params=pltpu.CompilerParams(vmem_limit_bytes=VM),
        name="attn_fwd",
        cost_estimate=BRIEF,
    )(q[0], k[0], v[0], idx, toep, small, *after)


def skip_refs(kernel, first, count, *refs):
    kernel(*refs[:first], *refs[first + count:])


def bwd_kernel(q_ref, k_ref, v_ref, do_ref, p_ref, out_ref, gs_ref, dp_ref, dka, dva):
    H,rows,PT=p_ref.shape
    nch=PT//128
    tile=pl.program_id(0); last=pl.num_programs(0)-1
    lane=lax.broadcasted_iota(jnp.int32,(1,128),1)
    first=lane<HEAD_DIM
    scale=HEAD_DIM**-0.5
    cuts=[(h,c) for c in range(nch) for h in range(H)]
    split=lambda x: (jnp.where(first,x,jnp.zeros_like(x)),jnp.where(first,jnp.zeros_like(x),x))
    for hp in range(H//2):
        hs=slice(hp*128,(hp+1)*128)
        dm=split(keep_rows(do_ref[:,hs],tile*PT,rows))
        for h in range(2):
            dp_ref[2*hp+h]=lax.dot_general(v_ref[:,hs],dm[h],NT,preferred_element_type=f32)
    def pass1(g,ds):
        r=pl.ds(pl.multiple_of(g*16,16),16)
        out=[]
        for i,(h,c) in enumerate(cuts):
            cs=slice(c*128,(c+1)*128)
            t=p_ref[h,r,cs].astype(f32)*dp_ref[h,r,cs]
            out.append(ds[i]+(t[:8]+t[8:]))
        return tuple(out)
    ds=lax.fori_loop(0,rows//16,pass1,tuple(jnp.zeros((8,128),f32) for _ in cuts),unroll=9)
    ds=[jnp.sum(d,axis=0,keepdims=True) for d in ds]
    def pass2(g,_):
        r=pl.ds(pl.multiple_of(g*16,16),16)
        for i,(h,c) in enumerate(cuts):
            cs=slice(c*128,(c+1)*128)
            gs_ref[h,r,cs]=(p_ref[h,r,cs].astype(f32)*(dp_ref[h,r,cs]-ds[i])).astype(bf)
        return 0
    lax.fori_loop(0,rows//16,pass2,0,unroll=9)
    @pl.when(tile==0)
    def _():
        dka[...]=jnp.zeros_like(dka); dva[...]=jnp.zeros_like(dva)
    for hp in range(H//2):
        hs=slice(hp*128,(hp+1)*128)
        kt=k_ref[:,hs].T
        o=[jnp.dot(kt[h*64:(h+1)*64],gs_ref[2*hp+h],preferred_element_type=f32) for h in range(2)]
        dq=(jnp.concatenate(o,0)*scale).T.astype(bf)
        @pl.when(tile<last)
        def _():
            out_ref[pl.ds(pl.multiple_of(tile*PT,PT),PT),hs]=dq
        @pl.when(tile==last)
        def _():
            left=rows-rows//PT*PT if rows%PT else PT
            out_ref[rows-left:,hs]=dq[:left]
        qm=split(keep_rows(q_ref[:,hs],tile*PT,rows))
        dm=split(keep_rows(do_ref[:,hs],tile*PT,rows))
        dka[:,hs]+=jnp.dot(gs_ref[2*hp],qm[0],preferred_element_type=f32)+jnp.dot(gs_ref[2*hp+1],qm[1],preferred_element_type=f32)
        dva[:,hs]+=jnp.dot(p_ref[2*hp],dm[0],preferred_element_type=f32)+jnp.dot(p_ref[2*hp+1],dm[1],preferred_element_type=f32)
    @pl.when(tile==last)
    def _():
        W=dka.shape[1]
        out_ref[:,W:2*W]=(dka[...]*scale).astype(bf)
        out_ref[:,2*W:]=dva[...].astype(bf)

def attn_bwd(q, k, v, W, do, p, after=()):
    rows = do.shape[0]
    H = W // HEAD_DIM
    lanes = p.shape[2]
    column = lambda at: pl.BlockSpec((rows, W), lambda i: (0, at))
    big = pl.BlockSpec((H, rows, PT), lambda i: (0, 0, i))
    return pl.pallas_call(
        partial(skip_refs, bwd_kernel, 5, len(after)),
        grid=(lanes // PT,),
        in_specs=[pl.BlockSpec((PT, W), lambda i: (i, q[1])), column(k[1]), column(v[1]), pl.BlockSpec((PT, W), lambda i: (i, 0)), big] + [ANY] * len(after),
        out_specs=(pl.BlockSpec((rows, 3 * W), lambda i: (0, 0)), big),
        out_shape=(jax.ShapeDtypeStruct((rows, 3 * W), bf), jax.ShapeDtypeStruct((H, rows, lanes), bf)),
        scratch_shapes=[pltpu.VMEM((H, rows, PT), f32), pltpu.VMEM((rows, W), f32), pltpu.VMEM((rows, W), f32)],
        compiler_params=pltpu.CompilerParams(vmem_limit_bytes=VM),
        name="attn_bwd",
        cost_estimate=BRIEF,
    )(q[0], k[0], v[0], do, p, *after)


def finish_kernel(info_ref, mine_ref, theirs_ref, *refs, block, widths, turned):
    rows = mine_ref.shape[0]
    count = rows // block
    n = len(widths)
    outs, wide, sems = refs[:n], refs[n:2 * n], refs[2 * n]
    copies = []
    for p, src in enumerate((mine_ref, theirs_ref)):
        for j in range(count):
            rs = slice(j * block, (j + 1) * block)
            place = pl.multiple_of((jnp.bitwise_xor(info_ref[0], p) * count + jnp.bitwise_xor(info_ref[1], j)) * block, block)
            at = 0
            for i in range(n):
                part = src[rs, at:at + widths[i]].astype(f32)
                at += widths[i]
                if turned[i]:
                    wide[i][p, :, rs] = part.T
                    copy = pltpu.make_async_copy(wide[i].at[p, :, rs], outs[i].at[:, pl.ds(place, block)], sems.at[p, j, i])
                else:
                    wide[i][p, rs, :] = part
                    copy = pltpu.make_async_copy(wide[i].at[p, rs, :], outs[i].at[pl.ds(place, block), :], sems.at[p, j, i])
                copy.start()
                copies.append(copy)
    for copy in copies:
        copy.wait()


def finish(mine, theirs, core, base, block, widths, turned):
    rows = mine.shape[0]
    return pl.pallas_call(
        partial(finish_kernel, block=block, widths=widths, turned=turned),
        in_specs=[SMEM, VMEM, VMEM],
        out_specs=[ANY] * len(widths),
        out_shape=[jax.ShapeDtypeStruct((w, 2 * rows) if t else (2 * rows, w), f32) for w, t in zip(widths, turned)],
        scratch_shapes=[pltpu.VMEM((2, w, rows) if t else (2, rows, w), f32) for w, t in zip(widths, turned)]
        + [pltpu.SemaphoreType.DMA((2, rows // block, len(widths)))],
        compiler_params=pltpu.CompilerParams(vmem_limit_bytes=VM),
        name="finish",
        cost_estimate=BRIEF,
    )(jnp.stack([core, base]).astype(jnp.int32), mine, theirs)


def hist_kernel(gs_ref, go_ref, idx_ref, out_ref, toep_ref, acc, accT, *, part):
    H, rows, lanes = gs_ref.shape
    SB = 16
    heads = 2 * H
    near = BUCKETS_2D // 2
    step = pl.program_id(0)

    @pl.when(step == 0)
    def _():
        acc[...] = jnp.zeros_like(acc)
        accT[...] = jnp.zeros_like(accT)

    iota = lax.broadcasted_iota(jnp.int32, (near, lanes), 0).astype(i16)
    one = jnp.ones((near, lanes), bf)
    zero = jnp.zeros((near, lanes), bf)

    def body(i, _):
        r = pl.ds(pl.multiple_of(i * SB, SB), SB)
        s0 = (part + step) * rows + i * SB
        sb = s0 // 128
        off = pl.multiple_of(s0 % 128, SB)
        idx = [idx_ref[ax, r, :] for ax in range(2)]
        positive = [(x >= near).astype(i16).astype(jnp.int32) > 0 for x in idx]
        cols = [[], []]
        for ref in (gs_ref, go_ref):
            for h in range(H):
                full = ref[h, r, :].astype(f32)
                k = len(cols[0])
                for c in range(lanes // 128):
                    at = pl.ds(pl.multiple_of((jnp.clip(sb - c, -2, 2) + 2) * 128 + off, SB), SB)
                    accT[k, at, :] += full[:, c * 128:(c + 1) * 128]
                for ax in range(2):
                    some = jnp.where(positive[ax], full, 0.0)
                    cols[ax].append([jnp.concatenate([full[t:t + 8], some[t:t + 8]], 0).astype(bf) for t in (0, 8)])
        for ax in range(2):
            ix = jnp.bitwise_and(idx[ax], jnp.asarray(near - 1, i16))
            left = []
            right = []
            for t in range(2):
                left.append(jnp.concatenate([jnp.where(iota == ix[t * 8 + p:t * 8 + p + 1, :], one, zero) for p in range(8)], 0))
                right.append(jnp.concatenate([x[t] for x in cols[ax]], 0))
            acc[ax] += lax.dot_general(jnp.concatenate(left, 1), jnp.concatenate(right, 1), NT, preferred_element_type=f32)
        return 0

    lax.fori_loop(0, rows // SB, body, 0, unroll=3)

    @pl.when(step == pl.num_programs(0) - 1)
    def _():
        lane = lax.broadcasted_iota(jnp.int32, (near, heads * SB), 1) % 8
        for ax in range(2):
            t = jnp.zeros((near, heads * SB), f32)
            for p in range(8):
                t = t + jnp.where(lane == p, acc[ax, p * near:(p + 1) * near, :], 0.0)
            out_ref[ax] = t
        m = lax.broadcasted_iota(jnp.int32, (128, 128), 1)
        turned = m + lax.broadcasted_iota(jnp.int32, (128, 128), 0)
        wraps = turned >= 128
        turned = jnp.where(wraps, turned - 128, turned)
        for h in range(heads):
            for j in (-1, 0, 1):
                x = lane_gather(accT[h, (j + 2) * 128:(j + 3) * 128, :], turned)
                at = 2 * (j + 1)
                toep_ref[h, at:at + 1, :] = jnp.sum(jnp.where(wraps, 0.0, x), axis=0, keepdims=True)
                toep_ref[h, at + 1:at + 2, :] = jnp.sum(jnp.where(wraps, x, 0.0), axis=0, keepdims=True)
            toep_ref[h, 6:7, :] = jnp.sum(accT[h, 0:128, :], axis=0, keepdims=True)
            toep_ref[h, 7:8, :] = jnp.sum(accT[h, 512:640, :], axis=0, keepdims=True)


def hist(gs, go, idx, part, steps, after=()):
    H, rows, lanes = gs.shape
    SB = 48
    near = BUCKETS_2D // 2
    big = pl.BlockSpec((H, SB, lanes), lambda i: (0, part + i, 0))
    return pl.pallas_call(
        partial(skip_refs, partial(hist_kernel, part=part), 3, len(after)),
        grid=(steps,),
        in_specs=[big, big, pl.BlockSpec((2, SB, lanes), lambda i: (0, part + i, 0))] + [ANY] * len(after),
        out_specs=(pl.BlockSpec((2, near, 2 * H * 16), lambda i: (0, 0, 0)), pl.BlockSpec((2 * H, 8, 128), lambda i: (0, 0, 0))),
        out_shape=(jax.ShapeDtypeStruct((2, near, 2 * H * 16), f32), jax.ShapeDtypeStruct((2 * H, 8, 128), f32)),
        scratch_shapes=[pltpu.VMEM((2, 8 * near, 2 * H * 16), f32), pltpu.VMEM((2 * H, 640, 128), f32)],
        compiler_params=pltpu.CompilerParams(vmem_limit_bytes=VM),
        name="table_sums",
        cost_estimate=BRIEF,
    )(gs, go, idx, *after)


def tables_kernel(*refs, parts):
    sums = refs[:2 * parts]
    dqkv, dqkv_o, up, up_o = refs[2 * parts:2 * parts + 4]
    shared = refs[2 * parts + 4:-1]
    out_ref = refs[-1]
    out = sums[0][...]
    toep = sums[1][...]
    for i in range(1, parts):
        out = out + sums[2 * i][...]
        toep = toep + sums[2 * i + 1][...]
    both, rows_out, lanes_out = out_ref.shape
    heads = toep.shape[0] // both
    near = out.shape[1]
    width = dqkv.shape[1] // 3
    out_ref[...] = jnp.zeros_like(out_ref)
    for o, (d, u) in enumerate(((dqkv, up), (dqkv_o, up_o))):
        out_ref[o, 0:1, 0:u.shape[0]] = u[...][None]
        for at in (0, 2 * width):
            out_ref[o, 1:2, at:at + width] = jnp.sum(d[:, at:at + width].astype(f32), axis=0, keepdims=True)
        for i, v in enumerate(shared):
            out_ref[o, 2 + i:3 + i, 384:384 + v.shape[0]] = v[...][None]
    exact = lax.Precision.HIGHEST
    groups = lax.broadcasted_iota(jnp.int32, (4 * heads, out.shape[2]), 1) // 8
    groups = jnp.where(groups == lax.broadcasted_iota(jnp.int32, groups.shape, 0), 1.0, 0.0)
    for ax in range(2):
        t = lax.dot_general(groups, out[ax], NT, precision=exact, preferred_element_type=f32)
        for h in range(2 * heads):
            line = jnp.concatenate([t[2 * h:2 * h + 1] - t[2 * h + 1:2 * h + 2], t[2 * h + 1:2 * h + 2]], 1)
            out_ref[h // heads, 2 + h % heads:3 + h % heads, 128 * (ax + 1):128 * (ax + 1) + 2 * near] = line
    seq = jnp.zeros((2 * heads, 128), f32)
    m = lax.broadcasted_iota(jnp.int32, (128, 128), 0)
    lane = lax.broadcasted_iota(jnp.int32, (128, 128), 1)
    for i, base in enumerate((-128, 0, 0, 128, 128, 256, -MAX_DIST - 128, MAX_DIST + 256)):
        d = base - m
        b = jnp.where(d > 0, BUCKETS // 2, 0)
        for e in bucket_edges(BUCKETS, MAX_DIST):
            b = b + jnp.where(jnp.abs(d) >= e, 1, 0)
        seq = seq + jnp.dot(toep[:, i, :], jnp.where(b == lane, 1.0, 0.0), precision=exact, preferred_element_type=f32)
    for h in range(2 * heads):
        out_ref[h // heads, 2 + h % heads:3 + h % heads, 0:128] = seq[h:h + 1]


def pack_sums(sums, dqkv, dqkv_o, up, up_o, shared, rows, lanes, after=()):
    flat = [x for s in sums for x in s]
    return pl.pallas_call(
        partial(skip_refs, partial(tables_kernel, parts=len(sums)), len(flat) + 4 + len(shared), len(after)),
        out_shape=jax.ShapeDtypeStruct((2, rows, lanes), f32),
        in_specs=[VMEM] * (len(flat) + 4 + len(shared)) + [ANY] * len(after),
        out_specs=VMEM,
        compiler_params=pltpu.CompilerParams(vmem_limit_bytes=VM),
        name="pack_sums",
        cost_estimate=BRIEF,
    )(*flat, dqkv, dqkv_o, up, up_o, *shared, *after)


def unpack_kernel(total_ref, *refs, width, heads):
    bq, bv, bu, ts, tx, ty = refs[:6]
    bq[...] = total_ref[1, 0:width]
    bv[...] = total_ref[1, 2 * width:3 * width]
    bu[...] = total_ref[0, 0:bu.shape[0]]
    for i, t in enumerate((ts, tx, ty)):
        t[...] = total_ref[2:2 + heads, 128 * i:128 * i + t.shape[1]]
    for i, v in enumerate(refs[6:]):
        v[...] = total_ref[2 + i, 384:384 + v.shape[0]]


def unpack_sums(total, width, heads, shapes):
    return pl.pallas_call(
        partial(unpack_kernel, width=width, heads=heads),
        out_shape=[jax.ShapeDtypeStruct(s, f32) for s in shapes],
        in_specs=[VMEM],
        out_specs=[VMEM] * len(shapes),
        name="unpack_sums",
        cost_estimate=BRIEF,
    )(total)


def tokens_kernel(first_ref, d_ref, do_ref, wq_ref, wk_ref, wv_ref, wo_ref, out_ref):
    W = wq_ref.shape[1]
    total = first_ref[...] + lax.dot_general(do_ref[...], wo_ref[...], NT, preferred_element_type=f32)
    for i, w in enumerate((wq_ref, wk_ref, wv_ref)):
        total = total + lax.dot_general(d_ref[:, i * W:(i + 1) * W], w[...], NT, preferred_element_type=f32)
    out_ref[...] = total


def grad_tokens_of(first, d, do, wq, wk, wv, wo, seq, after=()):
    rows, width = first.shape
    RB = 240
    block = lambda n: pl.BlockSpec((RB, n), lambda i: (i, 0))
    whole = lambda w: pl.BlockSpec(w.shape, lambda i: (0, 0))
    return pl.pallas_call(
        partial(skip_refs, tokens_kernel, 7, len(after)),
        grid=(rows // RB,),
        in_specs=[block(width), block(d.shape[1]), block(d.shape[1]), whole(wq), whole(wk), whole(wv), whole(wo)] + [ANY] * len(after),
        out_specs=block(width),
        out_shape=jax.ShapeDtypeStruct((seq, width), f32),
        compiler_params=pltpu.CompilerParams(vmem_limit_bytes=VM),
        name="grad_tokens",
        cost_estimate=BRIEF,
    )(first, d, do, wq, wk, wv, wo, *after)

def swap(value, axis, bit=1):
    count = lax.axis_size(axis)
    return lax.ppermute(value, axis, [(i, i ^ bit) for i in range(count)])


def half_of(value, axis, which):
    size = value.shape[axis] // 2
    return lax.dynamic_slice_in_dim(value, which * size, size, axis)


def join(mine, theirs, which, axis):
    low = jnp.where(which == 0, mine, theirs)
    high = jnp.where(which == 0, theirs, mine)
    return jnp.concatenate([low, high], axis)


def far_bits():
    count = lax.axis_size("far")
    bits = []
    bit = 1
    while bit < count:
        bits.append(bit)
        bit *= 2
    return bits


def add_low(a, b):
    return (a.astype(f32) + b.astype(f32)).astype(bf)


def far_side(bit):
    return (lax.axis_index("far") // bit) % 2


def arrive(moment, *values):
    return lax.optimization_barrier(values + (moment,))[:-1]


def halve(total, bit):
    at = far_side(bit)
    return half_of(total, 0, at), swap(half_of(total, 0, 1 - at), "far", bit)


def double(total, got, bit, base):
    if total.shape[0] % 16:
        return join(total, got, far_side(bit), 0), base
    return jnp.concatenate([total, got], 0), base + [far_side(bit)]


def spread(total, got, base, widths, turned):
    place = 0
    for side in base[::-1]:
        place = 2 * place + side
    block = total.shape[0] >> len(base)
    return finish(total, got, lax.axis_index("core"), jnp.asarray(place), block, widths, turned)


def reduce_small(total):
    for bit in far_bits():
        total = total + swap(total, "far", bit)
    return total


def norm_parts(values):
    center = values - jnp.mean(values, axis=1, keepdims=True)
    inverse = lax.rsqrt(jnp.mean(center * center, axis=1, keepdims=True) + layer_eps)
    return center * inverse, inverse


def norm_back(grad_scaled, scaled, inverse):
    return inverse * (
        grad_scaled
        - jnp.mean(grad_scaled, axis=1, keepdims=True)
        - scaled * jnp.mean(grad_scaled * scaled, axis=1, keepdims=True)
    )


def gelu_parts(v):
    cdf = 0.5 * (1.0 + lax.erf(v * (0.5 ** 0.5)))
    pdf = jnp.exp(-0.5 * v * v) * (1.0 / math.sqrt(2.0 * math.pi))
    return v * cdf, cdf + v * pdf


def mm(a, b):
    return jnp.dot(a, b, preferred_element_type=f32)


def mm_nt(a, b):
    return lax.dot_general(a, b, (((1,), (1,)), ((), ())), preferred_element_type=f32)


def mm_tn(a, b):
    return lax.dot_general(a, b, (((0,), (0,)), ((), ())), preferred_element_type=f32)


def per_device(
    tokens, text_len, box_coords, w_query, b_query, w_key, w_value, b_value, w_out, b_out,
    table_seq, table_x, table_y, gain_attn, shift_attn, w_up, b_up, w_down, b_down,
    gain_ffn, shift_ffn, cotangent,
):
    seq, width = tokens.shape[1:]
    rows = -(-seq // 240) * 240
    lanes = -(-rows // PT) * PT
    local = w_query.shape[1]
    heads = local // HEAD_DIM
    hidden = w_up.shape[1]
    core = lax.axis_index("core")
    small_rows = -(-(2 + max(heads, 6)) // 8) * 8

    small, wide = pack(
        [b_query, b_value, b_up, table_seq, table_x, table_y],
        [b_out, gain_attn, shift_attn, b_down, gain_ffn, shift_ffn], width, hidden,
    )
    small_o = swap(small, "tensor")
    halves, _ = lax.optimization_barrier((jnp.concatenate([half_of(w, 0, core) for w in (w_query, w_key, w_value)], 1), small))
    qkv_half = swap(halves, "tensor")
    b_out, gain_attn, shift_attn, b_down, gain_ffn, shift_ffn = [wide[i:i + 1] for i in range(6)]

    x = jnp.pad(tokens[0], ((0, rows - seq), (0, 0)))
    g = jnp.pad(cotangent[0], ((0, rows - seq), (0, 0)))
    bias = small[1:2].astype(f32)
    q = ((mm(x, w_query) + bias[:, :local]).astype(bf), 0)
    k = (mm(x, w_key).astype(bf), 0)
    v = ((mm(x, w_value) + bias[:, 2 * local:3 * local]).astype(bf), 0)
    idx, toep, toep_o = prep(text_len, box_coords[0], small, small_o, heads, rows, lanes)

    def fetched(got):
        return join(got, swap(got, "core"), core, 0)

    out_half = swap(half_of(w_out, 0, core), "tensor")
    up_half = swap(half_of(w_up, 0, core), "tensor")
    ctx, prob = attn_fwd(q, k, v, local, idx, toep, small)
    wqkv_o = fetched(qkv_half)
    down_half, ctx = lax.optimization_barrier((half_of(w_down, 0, core), ctx))
    down_half = swap(down_half, "tensor")
    both = (mm(x, wqkv_o) + small_o[1:2, :3 * local].astype(f32)).astype(bf)
    q_o, k_o, v_o = (both, 0), (both, 1), (both, 2)
    wo_o = fetched(out_half)
    ctx_o, prob_o = attn_fwd(q_o, k_o, v_o, local, idx, toep_o, small_o, (wo_o,))
    wu_o = fetched(up_half)
    down_half, ctx_o = lax.optimization_barrier((down_half, ctx_o))
    wd_o = fetched(down_half)

    attn = mm(ctx, w_out) + mm(ctx_o, wo_o) + b_out
    n1, inv1 = norm_parts(x.astype(f32) + attn)
    normed = n1 * gain_attn + shift_attn
    low = normed.astype(bf)
    act, slope = gelu_parts(mm(low, w_up) + small[0:1].astype(f32))
    act_o, slope_o = gelu_parts(mm(low, wu_o) + small_o[0:1].astype(f32))
    act, act_o = act.astype(bf), act_o.astype(bf)
    slope, slope_o = slope.astype(bf), slope_o.astype(bf)
    branch = mm(act, w_down) + mm(act_o, wd_o) + b_down
    n2, inv2 = norm_parts(normed + branch)
    output = (n2 * gain_ffn + shift_ffn).astype(bf)[:seq][None]

    gf = g.astype(f32)
    grad_gain_ffn = jnp.sum(gf * n2, axis=0)
    grad_shift_ffn = jnp.sum(gf, axis=0)
    grad_mid = norm_back(gf * gain_ffn, n2, inv2)
    gb = grad_mid.astype(bf)
    grad_b_down = jnp.sum(gb.astype(f32), axis=0)

    def terms(left, right):
        sent = swap(mm_tn(half_of(left, 1, 1 - core), right).astype(bf), "core")
        return mm_tn(half_of(left, 1, core), right).astype(bf), sent

    def add_three(a, b, c):
        return (a.astype(f32) + b.astype(f32) + c.astype(f32)).astype(bf)

    bits = far_bits()
    down_o = add_low(*terms(act_o, gb))
    down_x = swap(down_o, "tensor")
    gh_o = (mm_nt(gb, wd_o) * slope_o.astype(f32)).astype(bf)
    gb, down_o = lax.optimization_barrier((gb, down_o))
    down = terms(act, gb)
    gh = (mm_nt(gb, w_down) * slope.astype(f32)).astype(bf)
    grad_b_up = jnp.sum(gh.astype(f32), axis=0)
    grad_b_up_o = jnp.sum(gh_o.astype(f32), axis=0)
    up_o = terms(low, gh_o)
    up = terms(low, gh)
    grad_normed = mm_nt(gh, w_up) + mm_nt(gh_o, wu_o) + grad_mid
    grad_gain_attn = jnp.sum(grad_normed * n1, axis=0)
    grad_shift_attn = jnp.sum(grad_normed, axis=0)
    grad_first = norm_back(grad_normed * gain_attn, n1, inv1)
    ga = grad_first.astype(bf)
    grad_b_out = jnp.sum(ga.astype(f32), axis=0)
    out_o = terms(ga, ctx_o)
    out = terms(ga, ctx)
    gc_o = mm_nt(ga, wo_o).astype(bf)
    gc = mm_nt(ga, w_out).astype(bf)
    up_o = add_low(jnp.concatenate([up_o[0], out_o[0]], 1), jnp.concatenate([up_o[1], out_o[1]], 1))
    up_x = swap(up_o, "tensor")
    up = [jnp.concatenate([u, o], 1) for u, o in zip(up, out)]
    dqkv_o, gs_o = attn_bwd(q_o, k_o, v_o, local, gc_o, prob_o, (up_o, output))
    down_x, = arrive(gs_o, down_x)
    down = add_three(*down, down_x)
    down, down_in = halve(down, bits[0])
    qkv_o = add_low(*terms(x, dqkv_o))
    qkv_x = swap(qkv_o, "tensor")
    dqkv, gs = attn_bwd(q, k, v, local, gc, prob, (down, qkv_o))

    up_x, down_in = arrive(gs, up_x, down_in)
    down, down_in = halve(add_low(down, down_in), bits[1])
    up, up_in = halve(add_three(*up, up_x), bits[0])
    qkv, qkv_core = terms(x, dqkv)
    sums = [hist(gs, gs_o, idx, 0, 6, (up, down, qkv))]

    down_in, up_in, qkv_core, qkv_x = arrive(sums[-1][0], down_in, up_in, qkv_core, qkv_x)
    down = add_low(down, down_in)
    up, up_in = halve(add_low(up, up_in), bits[1])
    qkv, qkv_in = halve(add_three(qkv, qkv_core, qkv_x), bits[0])
    for bit in bits[3:]:
        keep, got = halve(down, bit)
        down = add_low(keep, got)
    down, down_in = halve(down, bits[2])
    sums.append(hist(gs, gs_o, idx, 6, 3, (qkv, up, down)))

    down_in, up_in, qkv_in = arrive(sums[-1][0], down_in, up_in, qkv_in)
    down = add_low(down, down_in)
    up = add_low(up, up_in)
    qkv, qkv_in = halve(add_low(qkv, qkv_in), bits[1])
    for bit in bits[3:]:
        keep, got = halve(up, bit)
        up = add_low(keep, got)
    up, up_in = halve(up, bits[2])
    down_base, up_base, base = [], [], []
    for bit in bits[:2:-1]:
        down, down_base = double(down, swap(down, "far", bit), bit, down_base)
    down_in = swap(down, "far", bits[2])
    sums.append(hist(gs, gs_o, idx, 9, 3, (up, qkv, down)))

    down_in, up_in, qkv_in = arrive(sums[-1][0], down_in, up_in, qkv_in)
    down, down_base = double(down, down_in, bits[2], down_base)
    down_in = swap(down, "far", bits[1])
    up = add_low(up, up_in)
    for bit in bits[:2:-1]:
        up, up_base = double(up, swap(up, "far", bit), bit, up_base)
    up_in = swap(up, "far", bits[2])
    qkv = add_low(qkv, qkv_in)
    for bit in bits[3:]:
        keep, got = halve(qkv, bit)
        qkv = add_low(keep, got)
    qkv, qkv_in = halve(qkv, bits[2])
    sums.append(hist(gs, gs_o, idx, 12, 3, (up, qkv, down)))

    down_in, up_in, qkv_in = arrive(sums[-1][0], down_in, up_in, qkv_in)
    qkv = add_low(qkv, qkv_in)
    for bit in bits[:2:-1]:
        qkv, base = double(qkv, swap(qkv, "far", bit), bit, base)
    qkv_in = swap(qkv, "far", bits[2])
    up, up_base = double(up, up_in, bits[2], up_base)
    up_in = swap(up, "far", bits[1])
    down, down_base = double(down, down_in, bits[1], down_base)
    down_in = swap(down, "far", bits[0])
    shared = [grad_b_out, grad_gain_attn, grad_shift_attn, grad_b_down, grad_gain_ffn, grad_shift_ffn]
    payload = pack_sums(sums, dqkv, dqkv_o, grad_b_up, grad_b_up_o, shared, small_rows, hidden, (up, qkv, down))

    up_in, qkv_in = arrive(payload, up_in, qkv_in)
    qkv, base = double(qkv, qkv_in, bits[2], base)
    qkv_in = swap(qkv, "far", bits[1])
    up, up_base = double(up, up_in, bits[1], up_base)
    up_in = swap(up, "far", bits[0])
    total, total_in = payload[0], swap(payload[1], "tensor")
    grad_tokens = grad_tokens_of(grad_first, dqkv, dqkv_o, w_query, w_key, w_value, wqkv_o, seq, (up, qkv))

    qkv_in, total_in, down_in = arrive(grad_tokens, qkv_in, total_in, down_in)
    qkv, base = double(qkv, qkv_in, bits[1], base)
    qkv_in = swap(qkv, "far", bits[0])
    total = total + total_in
    total_in = swap(total, "core")
    down, down_base = double(down, down_in, bits[0], down_base)
    down_in = swap(down, "core")
    grad_tokens, qkv, total, down = arrive(qkv, grad_tokens, qkv, total, down)
    grad_tokens = grad_tokens[None]

    total = total + total_in
    grad_w_down, = spread(down, down_in, down_base, (width,), (False,))
    up_in, qkv_in = arrive(grad_w_down, up_in, qkv_in)
    up, up_base = double(up, up_in, bits[0], up_base)
    up_in = swap(up, "core")
    qkv, base = double(qkv, qkv_in, bits[0], base)
    qkv_in = swap(qkv, "core")
    totals = reduce_small(total)
    grads_qkv = spread(qkv, qkv_in, base, (local,) * 3, (False,) * 3)
    up_block = up.shape[0] >> len(up_base)
    grad_w_up, grad_w_out = spread(up, up_in, up_base, (hidden, local), (False, up_block % 128 == 0))
    if up_block % 128:
        grad_w_out = grad_w_out.T
    shapes = [(local,), (local,), (hidden,), table_seq.shape, table_x.shape, table_y.shape] + [(width,)] * 6
    pieces = unpack_sums(totals, local, heads, shapes)
    g_bq, g_bv, g_bu, g_ts, g_tx, g_ty, g_bo, g_ga, g_sa, g_bd, g_gf, g_sf = pieces
    return (
        output, grad_tokens,
        grads_qkv[0], g_bq, grads_qkv[1], grads_qkv[2], g_bv,
        grad_w_out, g_bo, g_ts, g_tx, g_ty, g_ga, g_sa, grad_w_up, g_bu, grad_w_down, g_bd, g_gf, g_sf,
    )


def solution(mesh):
    grid = mesh.devices.shape
    mesh = jax.sharding.Mesh(mesh.devices.reshape(grid[0] // 2, 2, grid[1]), ("far", "core", "tensor"))
    every = ("far", "core", "tensor")
    item = P(every, None, None)
    column, row, split, copied = P(None, "tensor"), P("tensor", None), P("tensor"), P()
    return jax.shard_map(
        per_device,
        mesh=mesh,
        in_specs=(
            item, P(every), item, column, split, column, column, split, row, copied,
            row, row, row, copied, copied, column, split, row, copied, copied, copied, item,
        ),
        out_specs=(
            item, item, column, split, column, column, split, row, copied, row, row, row,
            copied, copied, column, split, row, copied, copied, copied,
        ),
        check_vma=False,
    )
```

```python
from functools import partial
import math

import jax
import jax.numpy as jnp
from jax import lax
from jax.experimental import pallas as pl
from jax.experimental.pallas import tpu as pltpu
from jax.sharding import PartitionSpec as P

HEAD_DIM = 64
BUCKETS = 32
MAX_DIST = 128
BUCKETS_2D = 64
MAX_DIST_2D = 256
TEXT = 512
layer_eps = 1e-05

f32 = jnp.float32
bf = jnp.bfloat16
i16 = jnp.int16
PT = 256
NT = (((1,), (1,)), ((), ()))
VM = 56 << 20

BRIEF = pl.CostEstimate(flops=10_000_000_000, bytes_accessed=1, transcendentals=0)


def bucket_edges(buckets, farthest):
    exact=buckets//4
    r=list(range(1,exact+1))
    for k in range(1,exact):
        r.append(int(math.ceil(exact*(farthest/exact)**(k/exact)-1e-09)))
    return r
def lane_gather(table, index):
    dn=lax.GatherDimensionNumbers(offset_dims=(),collapsed_slice_dims=(1,),start_index_map=(1,),operand_batching_dims=(0,),start_indices_batching_dims=(0,))
    return lax.gather(table,index[...,None],dn,(1,1),mode=lax.GatherScatterMode.PROMISE_IN_BOUNDS)

def prep_kernel(len_ref, box_ref, own_ref, oth_ref, idx_ref, toep_ref, toep_o_ref, up_ref, bias_ref, line_ref, col_ref, *, seq):
    up_ref[...] = oth_ref[0:1, :].astype(f32)
    bias_ref[...] = oth_ref[1:2, 0:bias_ref.shape[1]].astype(f32)
    rows, lanes = idx_ref.shape[1:]
    heads = toep_ref.shape[0]
    edges = bucket_edges(BUCKETS_2D, MAX_DIST_2D)
    near = [e for e in edges if e < 128]
    far = [e for e in edges if e >= 128]
    n = len_ref[0]
    rb = 16
    line_ref[...] = jnp.zeros_like(line_ref)
    line_ref[0:2, 0:seq] = box_ref[...].astype(f32)
    col_ref[...] = line_ref[...].T
    lane = lax.broadcasted_iota(jnp.int32, (rb, 128), 1)
    tab = jnp.zeros((rb, 128), jnp.int32)
    for e in near:
        tab = tab + jnp.where(lane >= e, 1, 0)
    tab = tab.astype(i16)

    def body(i, _):
        r = pl.ds(pl.multiple_of(i * rb, rb), rb)
        place = lax.broadcasted_iota(jnp.int32, (rb, 128), 0) + i * rb
        ok = ((place < n) | (place >= TEXT)) & (place < seq)
        for ax in range(2):
            col = jnp.broadcast_to(col_ref[r, ax:ax + 1], (rb, 128))
            for c in range(lanes // 128):
                cs = slice(c * 128, (c + 1) * 128)
                d = col - line_ref[ax:ax + 1, cs]
                a = jnp.abs(d)
                b = jnp.where(d > 0, float(BUCKETS_2D // 2), 0.0)
                for e in far:
                    b = b + jnp.where(a >= e, 1.0, 0.0)
                b = b.astype(jnp.int32).astype(i16) + lane_gather(tab, jnp.minimum(a, 127.0).astype(jnp.int32).astype(i16))
                if ax == 1:
                    b = jnp.where(ok, b.astype(jnp.int32), BUCKETS_2D).astype(i16)
                idx_ref[ax, r, cs] = b
        return 0

    lax.fori_loop(0, rows // rb, body, 0, unroll=5)
    for j in range(5):
        d = lax.broadcasted_iota(jnp.int32, (128, 128), 0) - lax.broadcasted_iota(jnp.int32, (128, 128), 1) + 128 * (j - 2)
        a = jnp.abs(d)
        b = jnp.zeros_like(d)
        for e in bucket_edges(BUCKETS, MAX_DIST):
            b = b + jnp.where(a >= e, 1, 0)
        b = (b + jnp.where(d > 0, BUCKETS // 2, 0)).astype(i16)
        for src, dst in ((own_ref, toep_ref), (oth_ref, toep_o_ref)):
            for h in range(heads):
                dst[h, j * 128:(j + 1) * 128, :] = lane_gather(jnp.broadcast_to(src[2 + h:3 + h, 0:128], (128, 128)), b)


VMEM = pl.BlockSpec(memory_space=pltpu.VMEM)
SMEM = pl.BlockSpec(memory_space=pltpu.SMEM)
ANY = pl.BlockSpec(memory_space=pl.ANY)


def prep(length, box, own, oth, heads, rows, lanes):
    seq = box.shape[1]
    toep = jax.ShapeDtypeStruct((heads, 640, 128), bf)
    return pl.pallas_call(
        partial(prep_kernel, seq=seq),
        out_shape=(
            jax.ShapeDtypeStruct((2, rows, lanes), i16), toep, toep,
            jax.ShapeDtypeStruct((1, own.shape[1]), f32), jax.ShapeDtypeStruct((1, 3 * heads * HEAD_DIM), f32),
        ),
        in_specs=[SMEM, VMEM, VMEM, VMEM],
        out_specs=(VMEM,) * 5,
        scratch_shapes=[pltpu.VMEM((8, lanes), f32), pltpu.VMEM((lanes, 8), f32)],
        compiler_params=pltpu.CompilerParams(vmem_limit_bytes=VM),
        name="buckets",
        cost_estimate=BRIEF,
    )(length, box, own, oth)


def pack_kernel(bq, bv, bu, ts, tx, ty, *refs):
    vectors, small_ref, up_ref, bias_ref, rows = refs[:6], refs[6], refs[7], refs[8], refs[9:]
    local = bq.shape[0]
    heads = ts.shape[0]
    hidden = bu.shape[0]
    small_ref[...] = jnp.zeros_like(small_ref)
    small_ref[0:1, 0:hidden] = bu[...][None]
    small_ref[1:2, 0:local] = bq[...][None]
    small_ref[1:2, 2 * local:3 * local] = bv[...][None]
    small_ref[2:2 + heads, 0:ts.shape[1]] = ts[...]
    small_ref[2:2 + heads, 128:128 + tx.shape[1]] = tx[...]
    small_ref[2:2 + heads, 256:384] = jnp.full((heads, 128), -1e9, bf)
    small_ref[2:2 + heads, 256:256 + ty.shape[1]] = ty[...]
    up_ref[...] = bu[...].astype(f32)[None]
    bias_ref[...] = jnp.zeros_like(bias_ref)
    bias_ref[0:1, 0:local] = bq[...].astype(f32)[None]
    bias_ref[0:1, 2 * local:3 * local] = bv[...].astype(f32)[None]
    for v, row in zip(vectors, rows):
        row[...] = v[...].astype(f32)[None]


def pack(split, copied, width, hidden):
    row = lambda n: jax.ShapeDtypeStruct((1, n), f32)
    out = pl.pallas_call(
        pack_kernel,
        out_shape=[jax.ShapeDtypeStruct((16, hidden), bf), row(hidden), row(3 * split[0].shape[0])] + [row(width)] * 6,
        in_specs=[VMEM] * 12,
        out_specs=[VMEM] * 9,
        name="pack",
        cost_estimate=BRIEF,
    )(*split, *copied)
    return out[0], out[1], out[2], out[3:]


def project_kernel(core_ref, x_ref, *refs):
    weights, bias_ref, out_ref = refs[:-2], refs[-2], refs[-1]
    if len(weights) == 3:
        at = 0
        for w in weights:
            n = w.shape[1]
            part = jnp.dot(x_ref[...], w[...], preferred_element_type=f32) + bias_ref[:, at:at + n]
            out_ref[:, at:at + n] = part.astype(bf)
            at += n
        return
    n = weights[0].shape[0]
    total = bias_ref[...]
    for i, w in enumerate(weights):
        at = pl.multiple_of(jnp.bitwise_xor(core_ref[0], i) * n, n)
        total = total + jnp.dot(x_ref[:, pl.ds(at, n)], w[...], preferred_element_type=f32)
    out_ref[...] = total.astype(bf)


def project(core, x, weights, bias):
    rows, width = x.shape
    RB = rows // 3
    whole = lambda w: pl.BlockSpec(w.shape, lambda i: (0, 0))
    return pl.pallas_call(
        project_kernel,
        grid=(rows // RB,),
        in_specs=[SMEM, pl.BlockSpec((RB, width), lambda i: (i, 0))] + [whole(w) for w in weights] + [whole(bias)],
        out_specs=pl.BlockSpec((RB, bias.shape[1]), lambda i: (i, 0)),
        out_shape=jax.ShapeDtypeStruct((rows, bias.shape[1]), bf),
        compiler_params=pltpu.CompilerParams(vmem_limit_bytes=VM),
        name="project",
        cost_estimate=BRIEF,
    )(core, x, *weights, bias)


def keep_rows(x,first_row,limit):
    rr=lax.broadcasted_iota(jnp.int32,(x.shape[0],1),0)+first_row
    return jnp.where(rr<limit,x,jnp.zeros_like(x))

def fwd_kernel(q_ref, k_ref, v_ref, idx_ref, toep_ref, small_ref, ctx_ref, p_ref, s_ref, qm_ref):
    H,rows,PT=p_ref.shape
    nch=PT//128
    tile=pl.program_id(0)
    lane=lax.broadcasted_iota(jnp.int32,(1,128),1)
    first=lane<HEAD_DIM
    for hp in range(H//2):
        hs=slice(hp*128,(hp+1)*128)
        q=keep_rows(q_ref[:,hs],tile*PT,rows)*jnp.asarray(HEAD_DIM**-0.5,bf)
        for h in range(2):
            qm=jnp.where(first if h==0 else ~first,q,jnp.zeros_like(q))
            qm_ref[2*hp+h]=qm
    tabs=[(jnp.broadcast_to(small_ref[2+h:3+h,128:256],(16,128)),jnp.broadcast_to(small_ref[2+h:3+h,256:384],(16,128))) for h in range(H)]
    cuts=[(h,c) for c in range(nch) for h in range(H)]
    BR=144
    def block1(i,ms):
        r=pl.ds(pl.multiple_of(i*BR,16),BR)
        for h in range(H):
            s_ref[h,r,:]=lax.dot_general(k_ref[r,h//2*128:(h//2+1)*128],qm_ref[h],NT,preferred_element_type=f32)
        for g in range(BR//16):
            ms=pass1(i*(BR//16)+g,ms)
        return ms
    def pass1(g,ms):
        r0=pl.multiple_of(g*16,16); r=pl.ds(r0,16)
        sb=r0//128; off=r0%128
        out=[]
        for c in range(nch):
            cs=slice(c*128,(c+1)*128)
            ix=idx_ref[0,r,cs]; iy=idx_ref[1,r,cs]
            tr=pl.ds(pl.multiple_of((jnp.clip(sb-(tile*nch+c),-2,2)+2)*128+off,16),16)
            gx=[lane_gather(tabs[h][0],ix) for h in range(H)]
            gy=[lane_gather(tabs[h][1],iy) for h in range(H)]
            for h in range(H):
                s=s_ref[h,r,cs]+gx[h].astype(f32)+gy[h].astype(f32)+toep_ref[h,tr,:].astype(f32)
                s_ref[h,r,cs]=s
                out.append(jnp.maximum(ms[c*H+h],jnp.maximum(s[:8],s[8:])))
        return tuple(out)
    ms=lax.fori_loop(0,rows//BR,block1,tuple(jnp.full((8,128),-jnp.inf,f32) for _ in cuts))
    ms=[jnp.max(m,axis=0,keepdims=True) for m in ms]
    def pass2(g,ls):
        r=pl.ds(pl.multiple_of(g*16,16),16)
        out=[]
        for i,(h,c) in enumerate(cuts):
            cs=slice(c*128,(c+1)*128)
            e=jnp.exp(s_ref[h,r,cs]-ms[i])
            s_ref[h,r,cs]=e
            out.append(ls[i]+(e[:8]+e[8:]))
        return tuple(out)
    ls=lax.fori_loop(0,rows//16,pass2,tuple(jnp.zeros((8,128),f32) for _ in cuts),unroll=5)
    inv=[1.0/jnp.sum(l,axis=0,keepdims=True) for l in ls]
    def pass3(g,_):
        r=pl.ds(pl.multiple_of(g*16,16),16)
        for i,(h,c) in enumerate(cuts):
            cs=slice(c*128,(c+1)*128)
            p_ref[h,r,cs]=(s_ref[h,r,cs]*inv[i]).astype(bf)
        return 0
    lax.fori_loop(0,rows//16,pass3,0,unroll=5)
    for hp in range(H//2):
        hs=slice(hp*128,(hp+1)*128)
        vt=v_ref[:,hs].T
        o=[jnp.dot(vt[h*64:(h+1)*64],p_ref[2*hp+h],preferred_element_type=f32) for h in range(2)]
        ctx_ref[:,hs]=jnp.concatenate(o,0).T.astype(bf)

def attn_fwd(q, k, v, W, idx, toep, small, after=()):
    rows = q[0].shape[0]
    H = W // HEAD_DIM
    lanes = idx.shape[2]
    whole = lambda shape: pl.BlockSpec(shape, lambda i: (0,) * len(shape))
    column = lambda at: pl.BlockSpec((rows, W), lambda i: (0, at))
    return pl.pallas_call(
        partial(skip_refs, fwd_kernel, 6, len(after)),
        grid=(lanes // PT,),
        in_specs=[pl.BlockSpec((PT, W), lambda i: (i, q[1])), column(k[1]), column(v[1]), pl.BlockSpec((2, rows, PT), lambda i: (0, 0, i)), whole(toep.shape), whole(small.shape)] + [ANY] * len(after),
        out_specs=(pl.BlockSpec((PT, W), lambda i: (i, 0)), pl.BlockSpec((H, rows, PT), lambda i: (0, 0, i))),
        out_shape=(jax.ShapeDtypeStruct((rows, W), bf), jax.ShapeDtypeStruct((H, rows, lanes), bf)),
        scratch_shapes=[pltpu.VMEM((H, rows, PT), f32), pltpu.VMEM((H, PT, 128), bf)],
        compiler_params=pltpu.CompilerParams(vmem_limit_bytes=VM),
        name="attn_fwd",
        cost_estimate=BRIEF,
    )(q[0], k[0], v[0], idx, toep, small, *after)


def skip_refs(kernel, first, count, *refs):
    kernel(*refs[:first], *refs[first + count:])


def bwd_kernel(q_ref, k_ref, v_ref, do_ref, p_ref, out_ref, gs_ref, dp_ref, dka, dva, dqa):
    H,rows,PT=p_ref.shape
    nch=PT//128
    tile=pl.program_id(0); last=pl.num_programs(0)-1
    lane=lax.broadcasted_iota(jnp.int32,(1,128),1)
    first=lane<HEAD_DIM
    scale=HEAD_DIM**-0.5
    cuts=[(h,c) for c in range(nch) for h in range(H)]
    split=lambda x: (jnp.where(first,x,jnp.zeros_like(x)),jnp.where(first,jnp.zeros_like(x),x))
    for hp in range(H//2):
        hs=slice(hp*128,(hp+1)*128)
        dm=split(keep_rows(do_ref[:,hs],tile*PT,rows))
        for h in range(2):
            dp_ref[2*hp+h]=lax.dot_general(v_ref[:,hs],dm[h],NT,preferred_element_type=f32)
    def pass1(g,ds):
        r=pl.ds(pl.multiple_of(g*16,16),16)
        out=[]
        for i,(h,c) in enumerate(cuts):
            cs=slice(c*128,(c+1)*128)
            t=p_ref[h,r,cs].astype(f32)*dp_ref[h,r,cs]
            out.append(ds[i]+(t[:8]+t[8:]))
        return tuple(out)
    ds=lax.fori_loop(0,rows//16,pass1,tuple(jnp.zeros((8,128),f32) for _ in cuts),unroll=9)
    ds=[jnp.sum(d,axis=0,keepdims=True) for d in ds]
    def pass2(g,_):
        r=pl.ds(pl.multiple_of(g*16,16),16)
        for i,(h,c) in enumerate(cuts):
            cs=slice(c*128,(c+1)*128)
            gs_ref[h,r,cs]=(p_ref[h,r,cs].astype(f32)*(dp_ref[h,r,cs]-ds[i])).astype(bf)
        return 0
    lax.fori_loop(0,rows//16,pass2,0,unroll=9)
    @pl.when(tile==0)
    def _():
        dka[...]=jnp.zeros_like(dka); dva[...]=jnp.zeros_like(dva)
    for hp in range(H//2):
        hs=slice(hp*128,(hp+1)*128)
        kt=k_ref[:,hs].T
        o=[jnp.dot(kt[h*64:(h+1)*64],gs_ref[2*hp+h],preferred_element_type=f32) for h in range(2)]
        dq=(jnp.concatenate(o,0)*scale).T.astype(bf)
        dqa[pl.ds(pl.multiple_of(tile*PT,PT),PT),hs]=dq
        qm=split(keep_rows(q_ref[:,hs],tile*PT,rows))
        dm=split(keep_rows(do_ref[:,hs],tile*PT,rows))
        dka[:,hs]+=jnp.dot(gs_ref[2*hp],qm[0],preferred_element_type=f32)+jnp.dot(gs_ref[2*hp+1],qm[1],preferred_element_type=f32)
        dva[:,hs]+=jnp.dot(p_ref[2*hp],dm[0],preferred_element_type=f32)+jnp.dot(p_ref[2*hp+1],dm[1],preferred_element_type=f32)
    @pl.when(tile==last)
    def _():
        W=dka.shape[1]
        out_ref[:,0:W]=dqa[0:rows,:]
        out_ref[:,W:2*W]=(dka[...]*scale).astype(bf)
        out_ref[:,2*W:]=dva[...].astype(bf)

def attn_bwd(q, k, v, W, do, p, after=()):
    rows = do.shape[0]
    H = W // HEAD_DIM
    lanes = p.shape[2]
    column = lambda at: pl.BlockSpec((rows, W), lambda i: (0, at))
    big = pl.BlockSpec((H, rows, PT), lambda i: (0, 0, i))
    return pl.pallas_call(
        partial(skip_refs, bwd_kernel, 5, len(after)),
        grid=(lanes // PT,),
        in_specs=[pl.BlockSpec((PT, W), lambda i: (i, q[1])), column(k[1]), column(v[1]), pl.BlockSpec((PT, W), lambda i: (i, 0)), big] + [ANY] * len(after),
        out_specs=(pl.BlockSpec((rows, 3 * W), lambda i: (0, 0)), big),
        out_shape=(jax.ShapeDtypeStruct((rows, 3 * W), bf), jax.ShapeDtypeStruct((H, rows, lanes), bf)),
        scratch_shapes=[pltpu.VMEM((H, rows, PT), f32), pltpu.VMEM((rows, W), f32), pltpu.VMEM((rows, W), f32), pltpu.VMEM((lanes, W), bf)],
        compiler_params=pltpu.CompilerParams(vmem_limit_bytes=VM),
        name="attn_bwd",
        cost_estimate=BRIEF,
    )(q[0], k[0], v[0], do, p, *after)


def finish_kernel(info_ref, mine_ref, theirs_ref, *refs, block, widths, turned):
    rows = mine_ref.shape[0]
    count = rows // block
    n = len(widths)
    outs, wide, sems = refs[:n], refs[n:2 * n], refs[2 * n]
    copies = []
    for p, src in enumerate((mine_ref, theirs_ref)):
        for j in range(count):
            rs = slice(j * block, (j + 1) * block)
            place = pl.multiple_of((jnp.bitwise_xor(info_ref[0], p) * count + jnp.bitwise_xor(info_ref[1], j)) * block, block)
            at = 0
            for i in range(n):
                part = src[rs, at:at + widths[i]].astype(f32)
                at += widths[i]
                if turned[i]:
                    wide[i][pl.ds(place, block), :] = part
                else:
                    wide[i][p, rs, :] = part
                    copy = pltpu.make_async_copy(wide[i].at[p, rs, :], outs[i].at[pl.ds(place, block), :], sems.at[p, j, i])
                    copy.start()
                    copies.append(copy)
    for i in range(n):
        if turned[i]:
            refs[2 * n + 1][...] = wide[i][...].T
            copy = pltpu.make_async_copy(refs[2 * n + 1], outs[i], sems.at[0, 0, i])
            copy.start()
            copies.append(copy)
    for copy in copies:
        copy.wait()


def finish(mine, theirs, core, base, block, widths, turned):
    rows = mine.shape[0]
    return pl.pallas_call(
        partial(finish_kernel, block=block, widths=widths, turned=turned),
        in_specs=[SMEM, VMEM, VMEM],
        out_specs=[ANY] * len(widths),
        out_shape=[jax.ShapeDtypeStruct((w, 2 * rows) if t else (2 * rows, w), f32) for w, t in zip(widths, turned)],
        scratch_shapes=[pltpu.VMEM((2 * rows, w) if t else (2, rows, w), f32) for w, t in zip(widths, turned)]
        + [pltpu.SemaphoreType.DMA((2, rows // block, len(widths)))]
        + [pltpu.VMEM((w, 2 * rows), f32) for w, t in zip(widths, turned) if t],
        compiler_params=pltpu.CompilerParams(vmem_limit_bytes=VM),
        name="finish",
        cost_estimate=BRIEF,
    )(jnp.stack([core, base]).astype(jnp.int32), mine, theirs)


def hist_kernel(gs_ref, go_ref, idx_ref, out_ref, toep_ref, acc, accT, *, part):
    H, rows, lanes = gs_ref.shape
    SB = 16
    heads = 2 * H
    near = BUCKETS_2D // 2
    step = pl.program_id(0)

    @pl.when(step == 0)
    def _():
        acc[...] = jnp.zeros_like(acc)
        accT[...] = jnp.zeros_like(accT)

    iota = lax.broadcasted_iota(jnp.int32, (near, lanes), 0).astype(i16)
    one = jnp.ones((near, lanes), bf)
    zero = jnp.zeros((near, lanes), bf)

    def body(i, _):
        r = pl.ds(pl.multiple_of(i * SB, SB), SB)
        s0 = (part + step) * rows + i * SB
        sb = s0 // 128
        off = pl.multiple_of(s0 % 128, SB)
        idx = [idx_ref[ax, r, :] for ax in range(2)]
        positive = [(x >= near).astype(i16).astype(jnp.int32) > 0 for x in idx]
        cols = [[], []]
        for ref in (gs_ref, go_ref):
            for h in range(H):
                full = ref[h, r, :].astype(f32)
                k = len(cols[0])
                for c in range(lanes // 128):
                    at = pl.ds(pl.multiple_of((jnp.clip(sb - c, -2, 2) + 2) * 128 + off, SB), SB)
                    accT[k, at, :] += full[:, c * 128:(c + 1) * 128]
                for ax in range(2):
                    some = jnp.where(positive[ax], full, 0.0)
                    cols[ax].append([jnp.concatenate([full[t:t + 8], some[t:t + 8]], 0).astype(bf) for t in (0, 8)])
        for ax in range(2):
            ix = jnp.bitwise_and(idx[ax], jnp.asarray(near - 1, i16))
            left = []
            right = []
            for t in range(2):
                left.append(jnp.concatenate([jnp.where(iota == ix[t * 8 + p:t * 8 + p + 1, :], one, zero) for p in range(8)], 0))
                right.append(jnp.concatenate([x[t] for x in cols[ax]], 0))
            acc[ax] += lax.dot_general(jnp.concatenate(left, 1), jnp.concatenate(right, 1), NT, preferred_element_type=f32)
        return 0

    lax.fori_loop(0, rows // SB, body, 0, unroll=3)

    @pl.when(step == pl.num_programs(0) - 1)
    def _():
        lane = lax.broadcasted_iota(jnp.int32, (near, heads * SB), 1) % 8
        for ax in range(2):
            t = jnp.zeros((near, heads * SB), f32)
            for p in range(8):
                t = t + jnp.where(lane == p, acc[ax, p * near:(p + 1) * near, :], 0.0)
            out_ref[ax] = t
        lane8 = lax.broadcasted_iota(jnp.int32, (8, 128), 1)
        row8 = lax.broadcasted_iota(jnp.int32, (8, 128), 0)
        kept = {}
        for g in range(16):
            turned = lane8 + row8 + 8 * g
            wraps = turned >= 128
            turned = jnp.where(wraps, turned - 128, turned)
            for h in range(heads):
                for j in (-1, 0, 1):
                    at = (j + 2) * 128 + 8 * g
                    x = lane_gather(accT[h, at:at + 8, :], turned)
                    for k, part_sum in enumerate((jnp.where(wraps, 0.0, x), jnp.where(wraps, x, 0.0))):
                        key = (h, 2 * (j + 1) + k)
                        kept[key] = part_sum if g == 0 else kept[key] + part_sum
        for h in range(heads):
            for k in range(6):
                toep_ref[h, k:k + 1, :] = jnp.sum(kept[h, k], axis=0, keepdims=True)
            toep_ref[h, 6:7, :] = jnp.sum(accT[h, 0:128, :], axis=0, keepdims=True)
            toep_ref[h, 7:8, :] = jnp.sum(accT[h, 512:640, :], axis=0, keepdims=True)


def hist(gs, go, idx, part, steps, after=()):
    H, rows, lanes = gs.shape
    SB = 48
    near = BUCKETS_2D // 2
    big = pl.BlockSpec((H, SB, lanes), lambda i: (0, part + i, 0))
    return pl.pallas_call(
        partial(skip_refs, partial(hist_kernel, part=part), 3, len(after)),
        grid=(steps,),
        in_specs=[big, big, pl.BlockSpec((2, SB, lanes), lambda i: (0, part + i, 0))] + [ANY] * len(after),
        out_specs=(pl.BlockSpec((2, near, 2 * H * 16), lambda i: (0, 0, 0)), pl.BlockSpec((2 * H, 8, 128), lambda i: (0, 0, 0))),
        out_shape=(jax.ShapeDtypeStruct((2, near, 2 * H * 16), f32), jax.ShapeDtypeStruct((2 * H, 8, 128), f32)),
        scratch_shapes=[pltpu.VMEM((2, 8 * near, 2 * H * 16), f32), pltpu.VMEM((2 * H, 640, 128), f32)],
        compiler_params=pltpu.CompilerParams(vmem_limit_bytes=VM),
        name="table_sums",
        cost_estimate=BRIEF,
    )(gs, go, idx, *after)


def tables_kernel(*refs, parts):
    sums = refs[:2 * parts]
    dqkv, dqkv_o, up, up_o = refs[2 * parts:2 * parts + 4]
    shared = refs[2 * parts + 4:-1]
    out_ref = refs[-1]
    out = sums[0][...]
    toep = sums[1][...]
    for i in range(1, parts):
        out = out + sums[2 * i][...]
        toep = toep + sums[2 * i + 1][...]
    both, rows_out, lanes_out = out_ref.shape
    heads = toep.shape[0] // both
    near = out.shape[1]
    width = dqkv.shape[1] // 3
    out_ref[...] = jnp.zeros_like(out_ref)
    for o, (d, u) in enumerate(((dqkv, up), (dqkv_o, up_o))):
        out_ref[o, 0:1, 0:u.shape[0]] = u[...][None]
        for at in (0, 2 * width):
            out_ref[o, 1:2, at:at + width] = jnp.sum(d[:, at:at + width].astype(f32), axis=0, keepdims=True)
        for i, v in enumerate(shared):
            out_ref[o, 2 + i:3 + i, 384:384 + v.shape[0]] = v[...][None]
    exact = lax.Precision.HIGHEST
    groups = lax.broadcasted_iota(jnp.int32, (4 * heads, out.shape[2]), 1) // 8
    groups = jnp.where(groups == lax.broadcasted_iota(jnp.int32, groups.shape, 0), 1.0, 0.0)
    for ax in range(2):
        t = lax.dot_general(groups, out[ax], NT, precision=exact, preferred_element_type=f32)
        for h in range(2 * heads):
            line = jnp.concatenate([t[2 * h:2 * h + 1] - t[2 * h + 1:2 * h + 2], t[2 * h + 1:2 * h + 2]], 1)
            out_ref[h // heads, 2 + h % heads:3 + h % heads, 128 * (ax + 1):128 * (ax + 1) + 2 * near] = line
    seq = jnp.zeros((2 * heads, 128), f32)
    m = lax.broadcasted_iota(jnp.int32, (128, 128), 0)
    lane = lax.broadcasted_iota(jnp.int32, (128, 128), 1)
    for i, base in enumerate((-128, 0, 0, 128, 128, 256, -MAX_DIST - 128, MAX_DIST + 256)):
        d = base - m
        b = jnp.where(d > 0, BUCKETS // 2, 0)
        for e in bucket_edges(BUCKETS, MAX_DIST):
            b = b + jnp.where(jnp.abs(d) >= e, 1, 0)
        seq = seq + jnp.dot(toep[:, i, :], jnp.where(b == lane, 1.0, 0.0), precision=exact, preferred_element_type=f32)
    for h in range(2 * heads):
        out_ref[h // heads, 2 + h % heads:3 + h % heads, 0:128] = seq[h:h + 1]


def pack_sums(sums, dqkv, dqkv_o, up, up_o, shared, rows, lanes, after=()):
    flat = [x for s in sums for x in s]
    return pl.pallas_call(
        partial(skip_refs, partial(tables_kernel, parts=len(sums)), len(flat) + 4 + len(shared), len(after)),
        out_shape=jax.ShapeDtypeStruct((2, rows, lanes), f32),
        in_specs=[VMEM] * (len(flat) + 4 + len(shared)) + [ANY] * len(after),
        out_specs=VMEM,
        compiler_params=pltpu.CompilerParams(vmem_limit_bytes=VM),
        name="pack_sums",
        cost_estimate=BRIEF,
    )(*flat, dqkv, dqkv_o, up, up_o, *shared, *after)


def unpack_kernel(total_ref, *refs, width, heads):
    bq, bv, bu, ts, tx, ty = refs[:6]
    bq[...] = total_ref[1, 0:width]
    bv[...] = total_ref[1, 2 * width:3 * width]
    bu[...] = total_ref[0, 0:bu.shape[0]]
    for i, t in enumerate((ts, tx, ty)):
        t[...] = total_ref[2:2 + heads, 128 * i:128 * i + t.shape[1]]
    for i, v in enumerate(refs[6:]):
        v[...] = total_ref[2 + i, 384:384 + v.shape[0]]


def unpack_sums(total, width, heads, shapes):
    return pl.pallas_call(
        partial(unpack_kernel, width=width, heads=heads),
        out_shape=[jax.ShapeDtypeStruct(s, f32) for s in shapes],
        in_specs=[VMEM],
        out_specs=[VMEM] * len(shapes),
        name="unpack_sums",
        cost_estimate=BRIEF,
    )(total)


def tokens_kernel(core_ref, first_ref, d_ref, do_ref, wq_ref, wk_ref, wv_ref, got_ref, peer_ref, out_ref):
    W = wq_ref.shape[1]
    total = first_ref[...]
    for i, w in enumerate((wq_ref, wk_ref, wv_ref)):
        total = total + lax.dot_general(d_ref[:, i * W:(i + 1) * W], w[...], NT, preferred_element_type=f32)
    out_ref[...] = total
    n = got_ref.shape[0]
    for i, w in enumerate((got_ref, peer_ref)):
        at = pl.ds(pl.multiple_of(jnp.bitwise_xor(core_ref[0], i) * n, n), n)
        out_ref[:, at] += lax.dot_general(do_ref[...], w[...], NT, preferred_element_type=f32)


def grad_tokens_of(core, first, d, do, weights, seq, after=()):
    rows, width = first.shape
    RB = 240
    block = lambda n: pl.BlockSpec((RB, n), lambda i: (i, 0))
    whole = lambda w: pl.BlockSpec(w.shape, lambda i: (0, 0))
    return pl.pallas_call(
        partial(skip_refs, tokens_kernel, 9, len(after)),
        grid=(rows // RB,),
        in_specs=[SMEM, block(width), block(d.shape[1]), block(d.shape[1])] + [whole(w) for w in weights] + [ANY] * len(after),
        out_specs=block(width),
        out_shape=jax.ShapeDtypeStruct((seq, width), f32),
        compiler_params=pltpu.CompilerParams(vmem_limit_bytes=VM),
        name="grad_tokens",
        cost_estimate=BRIEF,
    )(core, first, d, do, *weights, *after)

def swap(value, axis, bit=1):
    count = lax.axis_size(axis)
    return lax.ppermute(value, axis, [(i, i ^ bit) for i in range(count)])


def half_of(value, axis, which):
    size = value.shape[axis] // 2
    return lax.dynamic_slice_in_dim(value, which * size, size, axis)


def join(mine, theirs, which, axis=0):
    place = jnp.arange(2).reshape(2, 1, 1)
    return jnp.where(place == which, mine[None], theirs[None]).reshape(-1, mine.shape[1])


def far_bits():
    count = lax.axis_size("far")
    bits = []
    bit = 1
    while bit < count:
        bits.append(bit)
        bit *= 2
    return bits


def add_low(a, b):
    return (a.astype(f32) + b.astype(f32)).astype(bf)


def far_side(bit):
    return (lax.axis_index("far") // bit) % 2


def arrive(moment, *values):
    return lax.optimization_barrier(values + (moment,))[:-1]


def halve(parts, bit):
    at = far_side(bit)
    add = lambda which: sum(half_of(p, 0, which).astype(f32) for p in parts).astype(bf)
    return add(at), swap(add(1 - at), "far", bit)


def double(total, got, bit, base):
    if total.shape[0] % 16:
        return join(total, got, far_side(bit), 0), base
    return jnp.concatenate([total, got], 0), base + [far_side(bit)]


def spread(total, got, base, widths, turned):
    place = 0
    for side in base[::-1]:
        place = 2 * place + side
    block = total.shape[0] >> len(base)
    return finish(total, got, lax.axis_index("core"), jnp.asarray(place), block, widths, turned)


def norm_parts(values):
    center = values - jnp.mean(values, axis=1, keepdims=True)
    inverse = lax.rsqrt(jnp.mean(center * center, axis=1, keepdims=True) + layer_eps)
    return center * inverse, inverse


def norm_back(grad_scaled, scaled, inverse):
    return inverse * (
        grad_scaled
        - jnp.mean(grad_scaled, axis=1, keepdims=True)
        - scaled * jnp.mean(grad_scaled * scaled, axis=1, keepdims=True)
    )


def gelu_parts(v):
    cdf = 0.5 * (1.0 + lax.erf(v * (0.5 ** 0.5)))
    pdf = jnp.exp(-0.5 * v * v) * (1.0 / math.sqrt(2.0 * math.pi))
    return v * cdf, cdf + v * pdf


def mm(a, b):
    return jnp.dot(a, b, preferred_element_type=f32)


def mm_nt(a, b):
    return lax.dot_general(a, b, (((1,), (1,)), ((), ())), preferred_element_type=f32)


def mm_tn(a, b):
    return lax.dot_general(a, b, (((0,), (0,)), ((), ())), preferred_element_type=f32)


def per_device(
    tokens, text_len, box_coords, w_query, b_query, w_key, w_value, b_value, w_out, b_out,
    table_seq, table_x, table_y, gain_attn, shift_attn, w_up, b_up, w_down, b_down,
    gain_ffn, shift_ffn, cotangent,
):
    seq, width = tokens.shape[1:]
    rows = -(-seq // 240) * 240
    lanes = -(-rows // PT) * PT
    local = w_query.shape[1]
    heads = local // HEAD_DIM
    hidden = w_up.shape[1]
    core = lax.axis_index("core")
    small_rows = -(-(2 + max(heads, 6)) // 8) * 8

    small, up_bias, bias, vectors = pack(
        [b_query, b_value, b_up, table_seq, table_x, table_y],
        [b_out, gain_attn, shift_attn, b_down, gain_ffn, shift_ffn], width, hidden,
    )
    small_o = swap(small, "tensor")
    halves, _ = lax.optimization_barrier((jnp.concatenate([half_of(w, 0, core) for w in (w_query, w_key, w_value)], 1), small))
    qkv_half = swap(halves, "tensor")
    b_out, gain_attn, shift_attn, b_down, gain_ffn, shift_ffn = vectors
    which = core.reshape(1).astype(jnp.int32)

    x = jnp.pad(tokens[0], ((0, rows - seq), (0, 0)))
    g = jnp.pad(cotangent[0], ((0, rows - seq), (0, 0)))
    both = project(which, x, [w_query, w_key, w_value], bias)
    q, k, v = (both, 0), (both, 1), (both, 2)
    idx, toep, toep_o, up_bias_o, bias_o = prep(text_len, box_coords[0], small, small_o, heads, rows, lanes)

    def fetched(got):
        return join(got, swap(got, "core"), core)

    qkv_half, out_half, up_half, idx, both = lax.optimization_barrier(
        (qkv_half, half_of(w_out, 0, core), half_of(w_up, 0, core), idx, both)
    )
    q, k, v = (both, 0), (both, 1), (both, 2)
    qkv_peer = swap(qkv_half, "core")
    out_half = swap(out_half, "tensor")
    up_half = swap(up_half, "tensor")
    ctx, prob = attn_fwd(q, k, v, local, idx, toep, small, (qkv_half,))
    qkv_peer, down_half, ctx = arrive(ctx, qkv_peer, half_of(w_down, 0, core), ctx)
    down_half = swap(down_half, "tensor")
    both_o = project(which, x, [qkv_half, qkv_peer], bias_o)
    q_o, k_o, v_o = (both_o, 0), (both_o, 1), (both_o, 2)
    wo_o = fetched(out_half)
    ctx_o, prob_o = attn_fwd(q_o, k_o, v_o, local, idx, toep_o, small_o, (wo_o,))
    wu_o = fetched(up_half)
    down_half, ctx_o = lax.optimization_barrier((down_half, ctx_o))
    wd_o = fetched(down_half)

    attn = mm(ctx, w_out) + mm(ctx_o, wo_o) + b_out
    n1, inv1 = norm_parts(x.astype(f32) + attn)
    normed = n1 * gain_attn + shift_attn
    low = normed.astype(bf)
    act, slope = gelu_parts(mm(low, w_up) + up_bias)
    act_o, slope_o = gelu_parts(mm(low, wu_o) + up_bias_o)
    act, act_o = act.astype(bf), act_o.astype(bf)
    slope, slope_o = slope.astype(bf), slope_o.astype(bf)
    branch = mm(act, w_down) + mm(act_o, wd_o) + b_down
    n2, inv2 = norm_parts(normed + branch)
    output = (n2 * gain_ffn + shift_ffn).astype(bf)[:seq][None]

    gf = g.astype(f32)
    grad_gain_ffn = jnp.sum(gf * n2, axis=0)
    grad_shift_ffn = jnp.sum(gf, axis=0)
    grad_mid = norm_back(gf * gain_ffn, n2, inv2)
    gb = grad_mid.astype(bf)
    grad_b_down = jnp.sum(gb.astype(f32), axis=0)

    def terms(left, right):
        sent = swap(mm_tn(half_of(left, 1, 1 - core), right).astype(bf), "core")
        return mm_tn(half_of(left, 1, core), right).astype(bf), sent

    def add_three(a, b, c):
        return (a.astype(f32) + b.astype(f32) + c.astype(f32)).astype(bf)

    bits = far_bits()
    down_o = add_low(*terms(act_o, gb))
    down_x = swap(down_o, "tensor")
    gh_o = (mm_nt(gb, wd_o) * slope_o.astype(f32)).astype(bf)
    gb, down_o = lax.optimization_barrier((gb, down_o))
    down = terms(act, gb)
    gh = (mm_nt(gb, w_down) * slope.astype(f32)).astype(bf)
    grad_b_up = jnp.sum(gh.astype(f32), axis=0)
    grad_b_up_o = jnp.sum(gh_o.astype(f32), axis=0)
    up_o = terms(low, gh_o)
    up = terms(low, gh)
    grad_normed = mm_nt(gh, w_up) + mm_nt(gh_o, wu_o) + grad_mid
    grad_gain_attn = jnp.sum(grad_normed * n1, axis=0)
    grad_shift_attn = jnp.sum(grad_normed, axis=0)
    grad_first = norm_back(grad_normed * gain_attn, n1, inv1)
    ga = grad_first.astype(bf)
    grad_b_out = jnp.sum(ga.astype(f32), axis=0)
    out_o = terms(ga, ctx_o)
    out = terms(ga, ctx)
    gc_o = mm_nt(ga, wo_o).astype(bf)
    gc = mm_nt(ga, w_out).astype(bf)
    up_o = add_low(jnp.concatenate([up_o[0], out_o[0]], 1), jnp.concatenate([up_o[1], out_o[1]], 1))
    up_x = swap(up_o, "tensor")
    up = [jnp.concatenate([u, o], 1) for u, o in zip(up, out)]
    dqkv_o, gs_o = attn_bwd(q_o, k_o, v_o, local, gc_o, prob_o, (up_o, output))
    down_x, = arrive(gs_o, down_x)
    down = halve([*down, down_x], bits[0])
    qkv_o = add_low(*terms(x, dqkv_o))
    qkv_x = swap(qkv_o, "tensor")
    dqkv, gs = attn_bwd(q, k, v, local, gc, prob, (down[0], qkv_o))

    up_x, down_in = arrive(gs, up_x, down[1])
    down = halve([down[0], down_in], bits[1])
    up = halve([*up, up_x], bits[0])
    qkv = terms(x, dqkv)
    sums = [hist(gs, gs_o, idx, 0, 6, (up[0], down[0], qkv[0]))]

    down_in, up_in, qkv_core, qkv_x = arrive(sums[-1][0], down[1], up[1], qkv[1], qkv_x)
    down = [down[0], down_in]
    for bit in bits[3:]:
        down = halve(down, bit)
    down = halve(down, bits[2])
    up = halve([up[0], up_in], bits[1])
    qkv = halve([qkv[0], qkv_core, qkv_x], bits[0])
    sums.append(hist(gs, gs_o, idx, 6, 3, (qkv[0], up[0], down[0])))

    down_in, up_in, qkv_in = arrive(sums[-1][0], down[1], up[1], qkv[1])
    down_base, up_base, base = [], [], []
    down = add_low(down[0], down_in)
    for bit in bits[:2:-1]:
        down, down_base = double(down, swap(down, "far", bit), bit, down_base)
    down_in = swap(down, "far", bits[2])
    up = [up[0], up_in]
    for bit in bits[3:]:
        up = halve(up, bit)
    up = halve(up, bits[2])
    qkv = halve([qkv[0], qkv_in], bits[1])
    sums.append(hist(gs, gs_o, idx, 9, 3, (up[0], qkv[0], down)))

    down_in, up_in, qkv_in = arrive(sums[-1][0], down_in, up[1], qkv[1])
    down, down_base = double(down, down_in, bits[2], down_base)
    down_in = swap(down, "far", bits[1])
    up = add_low(up[0], up_in)
    for bit in bits[:2:-1]:
        up, up_base = double(up, swap(up, "far", bit), bit, up_base)
    up_in = swap(up, "far", bits[2])
    qkv = [qkv[0], qkv_in]
    for bit in bits[3:]:
        qkv = halve(qkv, bit)
    qkv = halve(qkv, bits[2])
    sums.append(hist(gs, gs_o, idx, 12, 3, (up, qkv[0], down)))

    down_in, up_in, qkv_in = arrive(sums[-1][0], down_in, up_in, qkv[1])
    qkv = add_low(qkv[0], qkv_in)
    for bit in bits[:2:-1]:
        qkv, base = double(qkv, swap(qkv, "far", bit), bit, base)
    qkv_in = swap(qkv, "far", bits[2])
    up, up_base = double(up, up_in, bits[2], up_base)
    up_in = swap(up, "far", bits[1])
    down, down_base = double(down, down_in, bits[1], down_base)
    down_in = swap(down, "far", bits[0])
    shared = [grad_b_out, grad_gain_attn, grad_shift_attn, grad_b_down, grad_gain_ffn, grad_shift_ffn]
    payload = pack_sums(sums, dqkv, dqkv_o, grad_b_up, grad_b_up_o, shared, small_rows, hidden, (up, qkv, down))

    total, total_in = payload[0], swap(payload[1], "tensor")
    up_in, qkv_in = arrive(payload, up_in, qkv_in)
    qkv, base = double(qkv, qkv_in, bits[2], base)
    qkv_in = swap(qkv, "far", bits[1])
    up, up_base = double(up, up_in, bits[1], up_base)
    up_in = swap(up, "far", bits[0])
    total_in, up = arrive(up, total_in, up)
    total = total + total_in
    total_in = swap(total, "core")
    grad_tokens = grad_tokens_of(which, grad_first, dqkv, dqkv_o, [w_query, w_key, w_value, qkv_half, qkv_peer], seq, (up, qkv, total))

    qkv_in, total_in, down_in = arrive(grad_tokens, qkv_in, total_in, down_in)
    qkv, base = double(qkv, qkv_in, bits[1], base)
    qkv_in = swap(qkv, "far", bits[0])
    total = total + total_in
    total_in = swap(total, "far", bits[0])
    down, down_base = double(down, down_in, bits[0], down_base)
    down_in = swap(down, "core")
    up_in, qkv, down, total = arrive(qkv, up_in, qkv, down, total)
    up, up_base = double(up, up_in, bits[0], up_base)
    up_in = swap(up, "core")
    down_in, total_in, up = arrive(up, down_in, total_in, up)
    total = total + total_in
    total_in = swap(total, "far", bits[1])
    grad_w_down, = spread(down, down_in, down_base, (width,), (False,))
    total_in, up_in = arrive(grad_w_down, total_in, up_in)
    total = total + total_in
    total_in = swap(total, "far", bits[2])
    grad_w_up, grad_w_out = spread(up, up_in, up_base, (hidden, local), (False, True))
    total_in, qkv_in = arrive(grad_w_up, total_in, qkv_in)
    qkv, base = double(qkv, qkv_in, bits[0], base)
    qkv_in = swap(qkv, "core")
    total = total + total_in
    for bit in bits[3:]:
        total = total + swap(total, "far", bit)
    grads_qkv = spread(qkv, qkv_in, base, (local,) * 3, (False,) * 3)
    totals = total
    grads_qkv = spread(qkv, qkv_in, base, (local,) * 3, (False,) * 3)
    grad_tokens = grad_tokens[None]
    shapes = [(local,), (local,), (hidden,), table_seq.shape, table_x.shape, table_y.shape] + [(width,)] * 6
    pieces = unpack_sums(totals, local, heads, shapes)
    g_bq, g_bv, g_bu, g_ts, g_tx, g_ty, g_bo, g_ga, g_sa, g_bd, g_gf, g_sf = pieces
    return (
        output, grad_tokens,
        grads_qkv[0], g_bq, grads_qkv[1], grads_qkv[2], g_bv,
        grad_w_out, g_bo, g_ts, g_tx, g_ty, g_ga, g_sa, grad_w_up, g_bu, grad_w_down, g_bd, g_gf, g_sf,
    )


def solution(mesh):
    grid = mesh.devices.shape
    mesh = jax.sharding.Mesh(mesh.devices.reshape(grid[0] // 2, 2, grid[1]), ("far", "core", "tensor"))
    every = ("far", "core", "tensor")
    item = P(every, None, None)
    column, row, split, copied = P(None, "tensor"), P("tensor", None), P("tensor"), P()
    return jax.shard_map(
        per_device,
        mesh=mesh,
        in_specs=(
            item, P(every), item, column, split, column, column, split, row, copied,
            row, row, row, copied, copied, column, split, row, copied, copied, copied, item,
        ),
        out_specs=(
            item, item, column, split, column, column, split, row, copied, row, row, row,
            copied, copied, column, split, row, copied, copied, copied,
        ),
        check_vma=False,
    )
```

```python
from functools import partial
import math

import jax
import jax.numpy as jnp
from jax import lax
from jax.experimental import pallas as pl
from jax.experimental.pallas import tpu as pltpu
from jax.sharding import PartitionSpec as P

HEAD_DIM = 64
BUCKETS = 32
MAX_DIST = 128
BUCKETS_2D = 64
MAX_DIST_2D = 256
TEXT = 512
layer_eps = 1e-05

f32 = jnp.float32
bf = jnp.bfloat16
i16 = jnp.int16
PT = 256
NT = (((1,), (1,)), ((), ()))
VM = 56 << 20

BRIEF = pl.CostEstimate(flops=10_000_000_000, bytes_accessed=1, transcendentals=0)


def bucket_edges(buckets, farthest):
    exact=buckets//4
    r=list(range(1,exact+1))
    for k in range(1,exact):
        r.append(int(math.ceil(exact*(farthest/exact)**(k/exact)-1e-09)))
    return r
def lane_gather(table, index):
    dn=lax.GatherDimensionNumbers(offset_dims=(),collapsed_slice_dims=(1,),start_index_map=(1,),operand_batching_dims=(0,),start_indices_batching_dims=(0,))
    return lax.gather(table,index[...,None],dn,(1,1),mode=lax.GatherScatterMode.PROMISE_IN_BOUNDS)

def prep_kernel(len_ref, box_ref, own_ref, oth_ref, idx_ref, toep_ref, toep_o_ref, up_ref, bias_ref, line_ref, col_ref, *, seq):
    up_ref[...] = oth_ref[0:1, :].astype(f32)
    bias_ref[...] = oth_ref[1:2, 0:bias_ref.shape[1]].astype(f32)
    rows, lanes = idx_ref.shape[1:]
    heads = toep_ref.shape[0]
    edges = bucket_edges(BUCKETS_2D, MAX_DIST_2D)
    near = [e for e in edges if e < 128]
    far = [e for e in edges if e >= 128]
    n = len_ref[0]
    rb = 16
    line_ref[...] = jnp.zeros_like(line_ref)
    line_ref[0:2, 0:seq] = box_ref[...].astype(f32)
    col_ref[...] = line_ref[...].T
    lane = lax.broadcasted_iota(jnp.int32, (rb, 128), 1)
    tab = jnp.zeros((rb, 128), jnp.int32)
    for e in near:
        tab = tab + jnp.where(lane >= e, 1, 0)
    tab = tab.astype(i16)

    def body(i, _):
        r = pl.ds(pl.multiple_of(i * rb, rb), rb)
        place = lax.broadcasted_iota(jnp.int32, (rb, 128), 0) + i * rb
        ok = ((place < n) | (place >= TEXT)) & (place < seq)
        for ax in range(2):
            col = jnp.broadcast_to(col_ref[r, ax:ax + 1], (rb, 128))
            for c in range(lanes // 128):
                cs = slice(c * 128, (c + 1) * 128)
                d = col - line_ref[ax:ax + 1, cs]
                a = jnp.abs(d)
                b = jnp.where(d > 0, float(BUCKETS_2D // 2), 0.0)
                for e in far:
                    b = b + jnp.where(a >= e, 1.0, 0.0)
                b = b.astype(jnp.int32).astype(i16) + lane_gather(tab, jnp.minimum(a, 127.0).astype(jnp.int32).astype(i16))
                if ax == 1:
                    b = jnp.where(ok, b.astype(jnp.int32), BUCKETS_2D).astype(i16)
                idx_ref[ax, r, cs] = b
        return 0

    lax.fori_loop(0, rows // rb, body, 0, unroll=5)
    for j in range(5):
        d = lax.broadcasted_iota(jnp.int32, (128, 128), 0) - lax.broadcasted_iota(jnp.int32, (128, 128), 1) + 128 * (j - 2)
        a = jnp.abs(d)
        b = jnp.zeros_like(d)
        for e in bucket_edges(BUCKETS, MAX_DIST):
            b = b + jnp.where(a >= e, 1, 0)
        b = (b + jnp.where(d > 0, BUCKETS // 2, 0)).astype(i16)
        for src, dst in ((own_ref, toep_ref), (oth_ref, toep_o_ref)):
            for h in range(heads):
                dst[h, j * 128:(j + 1) * 128, :] = lane_gather(jnp.broadcast_to(src[2 + h:3 + h, 0:128], (128, 128)), b)


VMEM = pl.BlockSpec(memory_space=pltpu.VMEM)
SMEM = pl.BlockSpec(memory_space=pltpu.SMEM)
ANY = pl.BlockSpec(memory_space=pl.ANY)


def prep(length, box, own, oth, heads, rows, lanes):
    seq = box.shape[1]
    toep = jax.ShapeDtypeStruct((heads, 640, 128), bf)
    return pl.pallas_call(
        partial(prep_kernel, seq=seq),
        out_shape=(
            jax.ShapeDtypeStruct((2, rows, lanes), i16), toep, toep,
            jax.ShapeDtypeStruct((1, own.shape[1]), f32), jax.ShapeDtypeStruct((1, 3 * heads * HEAD_DIM), f32),
        ),
        in_specs=[SMEM, VMEM, VMEM, VMEM],
        out_specs=(VMEM,) * 5,
        scratch_shapes=[pltpu.VMEM((8, lanes), f32), pltpu.VMEM((lanes, 8), f32)],
        compiler_params=pltpu.CompilerParams(vmem_limit_bytes=VM),
        name="buckets",
        cost_estimate=BRIEF,
    )(length, box, own, oth)


def pack_kernel(bq, bv, bu, ts, tx, ty, *refs):
    vectors, small_ref, up_ref, bias_ref, rows = refs[:6], refs[6], refs[7], refs[8], refs[9:]
    local = bq.shape[0]
    heads = ts.shape[0]
    hidden = bu.shape[0]
    small_ref[...] = jnp.zeros_like(small_ref)
    small_ref[0:1, 0:hidden] = bu[...][None]
    small_ref[1:2, 0:local] = bq[...][None]
    small_ref[1:2, 2 * local:3 * local] = bv[...][None]
    small_ref[2:2 + heads, 0:ts.shape[1]] = ts[...]
    small_ref[2:2 + heads, 128:128 + tx.shape[1]] = tx[...]
    small_ref[2:2 + heads, 256:384] = jnp.full((heads, 128), -1e9, bf)
    small_ref[2:2 + heads, 256:256 + ty.shape[1]] = ty[...]
    up_ref[...] = bu[...].astype(f32)[None]
    bias_ref[...] = jnp.zeros_like(bias_ref)
    bias_ref[0:1, 0:local] = bq[...].astype(f32)[None]
    bias_ref[0:1, 2 * local:3 * local] = bv[...].astype(f32)[None]
    for v, row in zip(vectors, rows):
        row[...] = v[...].astype(f32)[None]


def pack(split, copied, width, hidden):
    row = lambda n: jax.ShapeDtypeStruct((1, n), f32)
    out = pl.pallas_call(
        pack_kernel,
        out_shape=[jax.ShapeDtypeStruct((16, hidden), bf), row(hidden), row(3 * split[0].shape[0])] + [row(width)] * 6,
        in_specs=[VMEM] * 12,
        out_specs=[VMEM] * 9,
        name="pack",
        cost_estimate=BRIEF,
    )(*split, *copied)
    return out[0], out[1], out[2], out[3:]


def project_kernel(core_ref, x_ref, *refs):
    weights, bias_ref, out_ref = refs[:-2], refs[-2], refs[-1]
    if len(weights) == 3:
        at = 0
        for w in weights:
            n = w.shape[1]
            part = jnp.dot(x_ref[...], w[...], preferred_element_type=f32) + bias_ref[:, at:at + n]
            out_ref[:, at:at + n] = part.astype(bf)
            at += n
        return
    n = weights[0].shape[0]
    total = bias_ref[...]
    for i, w in enumerate(weights):
        at = pl.multiple_of(jnp.bitwise_xor(core_ref[0], i) * n, n)
        total = total + jnp.dot(x_ref[:, pl.ds(at, n)], w[...], preferred_element_type=f32)
    out_ref[...] = total.astype(bf)


def project(core, x, weights, bias):
    rows, width = x.shape
    RB = rows // 3
    whole = lambda w: pl.BlockSpec(w.shape, lambda i: (0, 0))
    return pl.pallas_call(
        project_kernel,
        grid=(rows // RB,),
        in_specs=[SMEM, pl.BlockSpec((RB, width), lambda i: (i, 0))] + [whole(w) for w in weights] + [whole(bias)],
        out_specs=pl.BlockSpec((RB, bias.shape[1]), lambda i: (i, 0)),
        out_shape=jax.ShapeDtypeStruct((rows, bias.shape[1]), bf),
        compiler_params=pltpu.CompilerParams(vmem_limit_bytes=VM),
        name="project",
        cost_estimate=BRIEF,
    )(core, x, *weights, bias)


def keep_rows(x,first_row,limit):
    rr=lax.broadcasted_iota(jnp.int32,(x.shape[0],1),0)+first_row
    return jnp.where(rr<limit,x,jnp.zeros_like(x))

def fwd_kernel(q_ref, k_ref, v_ref, idx_ref, toep_ref, small_ref, ctx_ref, p_ref, s_ref, qm_ref):
    H,rows,PT=p_ref.shape
    nch=PT//128
    tile=pl.program_id(0)
    lane=lax.broadcasted_iota(jnp.int32,(1,128),1)
    first=lane<HEAD_DIM
    for hp in range(H//2):
        hs=slice(hp*128,(hp+1)*128)
        q=keep_rows(q_ref[:,hs],tile*PT,rows)*jnp.asarray(HEAD_DIM**-0.5,bf)
        for h in range(2):
            qm=jnp.where(first if h==0 else ~first,q,jnp.zeros_like(q))
            qm_ref[2*hp+h]=qm
    tabs=[(jnp.broadcast_to(small_ref[2+h:3+h,128:256],(16,128)),jnp.broadcast_to(small_ref[2+h:3+h,256:384],(16,128))) for h in range(H)]
    cuts=[(h,c) for c in range(nch) for h in range(H)]
    BR=144
    def block1(i,ms):
        r=pl.ds(pl.multiple_of(i*BR,16),BR)
        for h in range(H):
            s_ref[h,r,:]=lax.dot_general(k_ref[r,h//2*128:(h//2+1)*128],qm_ref[h],NT,preferred_element_type=f32)
        for g in range(BR//16):
            ms=pass1(i*(BR//16)+g,ms)
        return ms
    def pass1(g,ms):
        r0=pl.multiple_of(g*16,16); r=pl.ds(r0,16)
        sb=r0//128; off=r0%128
        out=[]
        for c in range(nch):
            cs=slice(c*128,(c+1)*128)
            ix=idx_ref[0,r,cs]; iy=idx_ref[1,r,cs]
            tr=pl.ds(pl.multiple_of((jnp.clip(sb-(tile*nch+c),-2,2)+2)*128+off,16),16)
            gx=[lane_gather(tabs[h][0],ix) for h in range(H)]
            gy=[lane_gather(tabs[h][1],iy) for h in range(H)]
            for h in range(H):
                s=s_ref[h,r,cs]+gx[h].astype(f32)+gy[h].astype(f32)+toep_ref[h,tr,:].astype(f32)
                s_ref[h,r,cs]=s
                out.append(jnp.maximum(ms[c*H+h],jnp.maximum(s[:8],s[8:])))
        return tuple(out)
    ms=lax.fori_loop(0,rows//BR,block1,tuple(jnp.full((8,128),-jnp.inf,f32) for _ in cuts))
    ms=[jnp.max(m,axis=0,keepdims=True) for m in ms]
    def pass2(g,ls):
        r=pl.ds(pl.multiple_of(g*16,16),16)
        out=[]
        for i,(h,c) in enumerate(cuts):
            cs=slice(c*128,(c+1)*128)
            e=jnp.exp(s_ref[h,r,cs]-ms[i])
            s_ref[h,r,cs]=e
            out.append(ls[i]+(e[:8]+e[8:]))
        return tuple(out)
    ls=lax.fori_loop(0,rows//16,pass2,tuple(jnp.zeros((8,128),f32) for _ in cuts),unroll=5)
    inv=[1.0/jnp.sum(l,axis=0,keepdims=True) for l in ls]
    def pass3(g,_):
        r=pl.ds(pl.multiple_of(g*16,16),16)
        for i,(h,c) in enumerate(cuts):
            cs=slice(c*128,(c+1)*128)
            p_ref[h,r,cs]=(s_ref[h,r,cs]*inv[i]).astype(bf)
        return 0
    lax.fori_loop(0,rows//16,pass3,0,unroll=5)
    for hp in range(H//2):
        hs=slice(hp*128,(hp+1)*128)
        vt=v_ref[:,hs].T
        o=[jnp.dot(vt[h*64:(h+1)*64],p_ref[2*hp+h],preferred_element_type=f32) for h in range(2)]
        ctx_ref[:,hs]=jnp.concatenate(o,0).T.astype(bf)

def attn_fwd(q, k, v, W, idx, toep, small, after=()):
    rows = q[0].shape[0]
    H = W // HEAD_DIM
    lanes = idx.shape[2]
    whole = lambda shape: pl.BlockSpec(shape, lambda i: (0,) * len(shape))
    column = lambda at: pl.BlockSpec((rows, W), lambda i: (0, at))
    return pl.pallas_call(
        partial(skip_refs, fwd_kernel, 6, len(after)),
        grid=(lanes // PT,),
        in_specs=[pl.BlockSpec((PT, W), lambda i: (i, q[1])), column(k[1]), column(v[1]), pl.BlockSpec((2, rows, PT), lambda i: (0, 0, i)), whole(toep.shape), whole(small.shape)] + [ANY] * len(after),
        out_specs=(pl.BlockSpec((PT, W), lambda i: (i, 0)), pl.BlockSpec((H, rows, PT), lambda i: (0, 0, i))),
        out_shape=(jax.ShapeDtypeStruct((rows, W), bf), jax.ShapeDtypeStruct((H, rows, lanes), bf)),
        scratch_shapes=[pltpu.VMEM((H, rows, PT), f32), pltpu.VMEM((H, PT, 128), bf)],
        compiler_params=pltpu.CompilerParams(vmem_limit_bytes=VM),
        name="attn_fwd",
        cost_estimate=BRIEF,
    )(q[0], k[0], v[0], idx, toep, small, *after)


def skip_refs(kernel, first, count, *refs):
    kernel(*refs[:first], *refs[first + count:])


def bwd_kernel(q_ref, k_ref, v_ref, do_ref, p_ref, out_ref, gs_ref, dp_ref, dka, dva, dqa):
    H,rows,PT=p_ref.shape
    nch=PT//128
    tile=pl.program_id(0); last=pl.num_programs(0)-1
    lane=lax.broadcasted_iota(jnp.int32,(1,128),1)
    first=lane<HEAD_DIM
    scale=HEAD_DIM**-0.5
    cuts=[(h,c) for c in range(nch) for h in range(H)]
    split=lambda x: (jnp.where(first,x,jnp.zeros_like(x)),jnp.where(first,jnp.zeros_like(x),x))
    for hp in range(H//2):
        hs=slice(hp*128,(hp+1)*128)
        dm=split(keep_rows(do_ref[:,hs],tile*PT,rows))
        for h in range(2):
            dp_ref[2*hp+h]=lax.dot_general(v_ref[:,hs],dm[h],NT,preferred_element_type=f32)
    def pass1(g,ds):
        r=pl.ds(pl.multiple_of(g*16,16),16)
        out=[]
        for i,(h,c) in enumerate(cuts):
            cs=slice(c*128,(c+1)*128)
            t=p_ref[h,r,cs].astype(f32)*dp_ref[h,r,cs]
            out.append(ds[i]+(t[:8]+t[8:]))
        return tuple(out)
    ds=lax.fori_loop(0,rows//16,pass1,tuple(jnp.zeros((8,128),f32) for _ in cuts),unroll=9)
    ds=[jnp.sum(d,axis=0,keepdims=True) for d in ds]
    def pass2(g,_):
        r=pl.ds(pl.multiple_of(g*16,16),16)
        for i,(h,c) in enumerate(cuts):
            cs=slice(c*128,(c+1)*128)
            gs_ref[h,r,cs]=(p_ref[h,r,cs].astype(f32)*(dp_ref[h,r,cs]-ds[i])).astype(bf)
        return 0
    lax.fori_loop(0,rows//16,pass2,0,unroll=9)
    @pl.when(tile==0)
    def _():
        dka[...]=jnp.zeros_like(dka); dva[...]=jnp.zeros_like(dva)
    for hp in range(H//2):
        hs=slice(hp*128,(hp+1)*128)
        kt=k_ref[:,hs].T
        o=[jnp.dot(kt[h*64:(h+1)*64],gs_ref[2*hp+h],preferred_element_type=f32) for h in range(2)]
        dq=(jnp.concatenate(o,0)*scale).T.astype(bf)
        dqa[pl.ds(pl.multiple_of(tile*PT,PT),PT),hs]=dq
        qm=split(keep_rows(q_ref[:,hs],tile*PT,rows))
        dm=split(keep_rows(do_ref[:,hs],tile*PT,rows))
        dka[:,hs]+=jnp.dot(gs_ref[2*hp],qm[0],preferred_element_type=f32)+jnp.dot(gs_ref[2*hp+1],qm[1],preferred_element_type=f32)
        dva[:,hs]+=jnp.dot(p_ref[2*hp],dm[0],preferred_element_type=f32)+jnp.dot(p_ref[2*hp+1],dm[1],preferred_element_type=f32)
    @pl.when(tile==last)
    def _():
        W=dka.shape[1]
        out_ref[:,0:W]=dqa[0:rows,:]
        out_ref[:,W:2*W]=(dka[...]*scale).astype(bf)
        out_ref[:,2*W:]=dva[...].astype(bf)

def attn_bwd(q, k, v, W, do, p, after=()):
    rows = do.shape[0]
    H = W // HEAD_DIM
    lanes = p.shape[2]
    column = lambda at: pl.BlockSpec((rows, W), lambda i: (0, at))
    big = pl.BlockSpec((H, rows, PT), lambda i: (0, 0, i))
    return pl.pallas_call(
        partial(skip_refs, bwd_kernel, 5, len(after)),
        grid=(lanes // PT,),
        in_specs=[pl.BlockSpec((PT, W), lambda i: (i, q[1])), column(k[1]), column(v[1]), pl.BlockSpec((PT, W), lambda i: (i, 0)), big] + [ANY] * len(after),
        out_specs=(pl.BlockSpec((rows, 3 * W), lambda i: (0, 0)), big),
        out_shape=(jax.ShapeDtypeStruct((rows, 3 * W), bf), jax.ShapeDtypeStruct((H, rows, lanes), bf)),
        scratch_shapes=[pltpu.VMEM((H, rows, PT), f32), pltpu.VMEM((rows, W), f32), pltpu.VMEM((rows, W), f32), pltpu.VMEM((lanes, W), bf)],
        compiler_params=pltpu.CompilerParams(vmem_limit_bytes=VM),
        name="attn_bwd",
        cost_estimate=BRIEF,
    )(q[0], k[0], v[0], do, p, *after)


def finish_kernel(info_ref, mine_ref, theirs_ref, *refs, block, widths, turned):
    rows = mine_ref.shape[0]
    count = rows // block
    n = len(widths)
    outs, wide, sems = refs[:n], refs[n:2 * n], refs[2 * n]
    copies = []
    for p, src in enumerate((mine_ref, theirs_ref)):
        for j in range(count):
            rs = slice(j * block, (j + 1) * block)
            place = pl.multiple_of((jnp.bitwise_xor(info_ref[0], p) * count + jnp.bitwise_xor(info_ref[1], j)) * block, block)
            at = 0
            for i in range(n):
                part = src[rs, at:at + widths[i]].astype(f32)
                at += widths[i]
                if turned[i]:
                    wide[i][pl.ds(place, block), :] = part
                else:
                    wide[i][p, rs, :] = part
                    copy = pltpu.make_async_copy(wide[i].at[p, rs, :], outs[i].at[pl.ds(place, block), :], sems.at[p, j, i])
                    copy.start()
                    copies.append(copy)
    for i in range(n):
        if turned[i]:
            refs[2 * n + 1][...] = wide[i][...].T
            copy = pltpu.make_async_copy(refs[2 * n + 1], outs[i], sems.at[0, 0, i])
            copy.start()
            copies.append(copy)
    for copy in copies:
        copy.wait()


def finish(mine, theirs, core, base, block, widths, turned):
    rows = mine.shape[0]
    return pl.pallas_call(
        partial(finish_kernel, block=block, widths=widths, turned=turned),
        in_specs=[SMEM, VMEM, VMEM],
        out_specs=[ANY] * len(widths),
        out_shape=[jax.ShapeDtypeStruct((w, 2 * rows) if t else (2 * rows, w), f32) for w, t in zip(widths, turned)],
        scratch_shapes=[pltpu.VMEM((2 * rows, w) if t else (2, rows, w), f32) for w, t in zip(widths, turned)]
        + [pltpu.SemaphoreType.DMA((2, rows // block, len(widths)))]
        + [pltpu.VMEM((w, 2 * rows), f32) for w, t in zip(widths, turned) if t],
        compiler_params=pltpu.CompilerParams(vmem_limit_bytes=VM),
        name="finish",
        cost_estimate=BRIEF,
    )(jnp.stack([core, base]).astype(jnp.int32), mine, theirs)


def hist_kernel(gs_ref, go_ref, idx_ref, out_ref, toep_ref, acc, accT, *, part):
    H, rows, lanes = gs_ref.shape
    SB = 16
    heads = 2 * H
    near = BUCKETS_2D // 2
    step = pl.program_id(0)

    @pl.when(step == 0)
    def _():
        acc[...] = jnp.zeros_like(acc)
        accT[...] = jnp.zeros_like(accT)

    iota = lax.broadcasted_iota(jnp.int32, (near, lanes), 0).astype(i16)
    one = jnp.ones((near, lanes), bf)
    zero = jnp.zeros((near, lanes), bf)

    def body(i, _):
        r = pl.ds(pl.multiple_of(i * SB, SB), SB)
        s0 = (part + step) * rows + i * SB
        sb = s0 // 128
        off = pl.multiple_of(s0 % 128, SB)
        idx = [idx_ref[ax, r, :] for ax in range(2)]
        positive = [(x >= near).astype(i16).astype(jnp.int32) > 0 for x in idx]
        cols = [[], []]
        for ref in (gs_ref, go_ref):
            for h in range(H):
                full = ref[h, r, :].astype(f32)
                k = len(cols[0])
                for c in range(lanes // 128):
                    at = pl.ds(pl.multiple_of((jnp.clip(sb - c, -2, 2) + 2) * 128 + off, SB), SB)
                    accT[k, at, :] += full[:, c * 128:(c + 1) * 128]
                for ax in range(2):
                    some = jnp.where(positive[ax], full, 0.0)
                    cols[ax].append([jnp.concatenate([full[t:t + 8], some[t:t + 8]], 0).astype(bf) for t in (0, 8)])
        for ax in range(2):
            ix = jnp.bitwise_and(idx[ax], jnp.asarray(near - 1, i16))
            left = []
            right = []
            for t in range(2):
                left.append(jnp.concatenate([jnp.where(iota == ix[t * 8 + p:t * 8 + p + 1, :], one, zero) for p in range(8)], 0))
                right.append(jnp.concatenate([x[t] for x in cols[ax]], 0))
            acc[ax] += lax.dot_general(jnp.concatenate(left, 1), jnp.concatenate(right, 1), NT, preferred_element_type=f32)
        return 0

    lax.fori_loop(0, rows // SB, body, 0, unroll=3)

    @pl.when(step == pl.num_programs(0) - 1)
    def _():
        lane = lax.broadcasted_iota(jnp.int32, (near, heads * SB), 1) % 8
        for ax in range(2):
            t = jnp.zeros((near, heads * SB), f32)
            for p in range(8):
                t = t + jnp.where(lane == p, acc[ax, p * near:(p + 1) * near, :], 0.0)
            out_ref[ax] = t
        lane8 = lax.broadcasted_iota(jnp.int32, (8, 128), 1)
        row8 = lax.broadcasted_iota(jnp.int32, (8, 128), 0)
        kept = {}
        for g in range(16):
            turned = lane8 + row8 + 8 * g
            wraps = turned >= 128
            turned = jnp.where(wraps, turned - 128, turned)
            for h in range(heads):
                for j in (-1, 0, 1):
                    at = (j + 2) * 128 + 8 * g
                    x = lane_gather(accT[h, at:at + 8, :], turned)
                    for k, part_sum in enumerate((jnp.where(wraps, 0.0, x), jnp.where(wraps, x, 0.0))):
                        key = (h, 2 * (j + 1) + k)
                        kept[key] = part_sum if g == 0 else kept[key] + part_sum
        for h in range(heads):
            for k in range(6):
                toep_ref[h, k:k + 1, :] = jnp.sum(kept[h, k], axis=0, keepdims=True)
            toep_ref[h, 6:7, :] = jnp.sum(accT[h, 0:128, :], axis=0, keepdims=True)
            toep_ref[h, 7:8, :] = jnp.sum(accT[h, 512:640, :], axis=0, keepdims=True)


def hist(gs, go, idx, part, steps, after=()):
    H, rows, lanes = gs.shape
    SB = 48
    near = BUCKETS_2D // 2
    big = pl.BlockSpec((H, SB, lanes), lambda i: (0, part + i, 0))
    return pl.pallas_call(
        partial(skip_refs, partial(hist_kernel, part=part), 3, len(after)),
        grid=(steps,),
        in_specs=[big, big, pl.BlockSpec((2, SB, lanes), lambda i: (0, part + i, 0))] + [ANY] * len(after),
        out_specs=(pl.BlockSpec((2, near, 2 * H * 16), lambda i: (0, 0, 0)), pl.BlockSpec((2 * H, 8, 128), lambda i: (0, 0, 0))),
        out_shape=(jax.ShapeDtypeStruct((2, near, 2 * H * 16), f32), jax.ShapeDtypeStruct((2 * H, 8, 128), f32)),
        scratch_shapes=[pltpu.VMEM((2, 8 * near, 2 * H * 16), f32), pltpu.VMEM((2 * H, 640, 128), f32)],
        compiler_params=pltpu.CompilerParams(vmem_limit_bytes=VM),
        name="table_sums",
        cost_estimate=BRIEF,
    )(gs, go, idx, *after)


def tables_kernel(*refs, parts):
    sums = refs[:2 * parts]
    dqkv, dqkv_o, up, up_o = refs[2 * parts:2 * parts + 4]
    shared = refs[2 * parts + 4:-2]
    outs = refs[-2:]
    out = sums[0][...]
    toep = sums[1][...]
    for i in range(1, parts):
        out = out + sums[2 * i][...]
        toep = toep + sums[2 * i + 1][...]
    heads = toep.shape[0] // 2
    near = out.shape[1]
    width = dqkv.shape[1] // 3
    for out_ref, d, u in zip(outs, (dqkv, dqkv_o), (up, up_o)):
        out_ref[...] = jnp.zeros_like(out_ref)
        out_ref[0:1, 0:u.shape[0]] = u[...][None]
        for at in (0, 2 * width):
            out_ref[1:2, at:at + width] = jnp.sum(d[:, at:at + width].astype(f32), axis=0, keepdims=True)
        for i, v in enumerate(shared):
            out_ref[2 + i:3 + i, 384:384 + v.shape[0]] = v[...][None]
    exact = lax.Precision.HIGHEST
    groups = lax.broadcasted_iota(jnp.int32, (4 * heads, out.shape[2]), 1) // 8
    groups = jnp.where(groups == lax.broadcasted_iota(jnp.int32, groups.shape, 0), 1.0, 0.0)
    for ax in range(2):
        t = lax.dot_general(groups, out[ax], NT, precision=exact, preferred_element_type=f32)
        for h in range(2 * heads):
            line = jnp.concatenate([t[2 * h:2 * h + 1] - t[2 * h + 1:2 * h + 2], t[2 * h + 1:2 * h + 2]], 1)
            outs[h // heads][2 + h % heads:3 + h % heads, 128 * (ax + 1):128 * (ax + 1) + 2 * near] = line
    seq = jnp.zeros((2 * heads, 128), f32)
    m = lax.broadcasted_iota(jnp.int32, (128, 128), 0)
    lane = lax.broadcasted_iota(jnp.int32, (128, 128), 1)
    for i, base in enumerate((-128, 0, 0, 128, 128, 256, -MAX_DIST - 128, MAX_DIST + 256)):
        d = base - m
        b = jnp.where(d > 0, BUCKETS // 2, 0)
        for e in bucket_edges(BUCKETS, MAX_DIST):
            b = b + jnp.where(jnp.abs(d) >= e, 1, 0)
        seq = seq + jnp.dot(toep[:, i, :], jnp.where(b == lane, 1.0, 0.0), precision=exact, preferred_element_type=f32)
    for h in range(2 * heads):
        outs[h // heads][2 + h % heads:3 + h % heads, 0:128] = seq[h:h + 1]


def pack_sums(sums, dqkv, dqkv_o, up, up_o, shared, rows, lanes, after=()):
    flat = [x for s in sums for x in s]
    return pl.pallas_call(
        partial(skip_refs, partial(tables_kernel, parts=len(sums)), len(flat) + 4 + len(shared), len(after)),
        out_shape=(jax.ShapeDtypeStruct((rows, lanes), f32),) * 2,
        in_specs=[VMEM] * (len(flat) + 4 + len(shared)) + [ANY] * len(after),
        out_specs=(VMEM, VMEM),
        compiler_params=pltpu.CompilerParams(vmem_limit_bytes=VM),
        name="pack_sums",
        cost_estimate=BRIEF,
    )(*flat, dqkv, dqkv_o, up, up_o, *shared, *after)


def unpack_kernel(total_ref, *refs, width, heads):
    bq, bv, bu, ts, tx, ty = refs[:6]
    bq[...] = total_ref[1, 0:width]
    bv[...] = total_ref[1, 2 * width:3 * width]
    bu[...] = total_ref[0, 0:bu.shape[0]]
    for i, t in enumerate((ts, tx, ty)):
        t[...] = total_ref[2:2 + heads, 128 * i:128 * i + t.shape[1]]
    for i, v in enumerate(refs[6:]):
        v[...] = total_ref[2 + i, 384:384 + v.shape[0]]


def unpack_sums(total, width, heads, shapes):
    return pl.pallas_call(
        partial(unpack_kernel, width=width, heads=heads),
        out_shape=[jax.ShapeDtypeStruct(s, f32) for s in shapes],
        in_specs=[VMEM],
        out_specs=[VMEM] * len(shapes),
        name="unpack_sums",
        cost_estimate=BRIEF,
    )(total)


def tokens_kernel(core_ref, first_ref, d_ref, do_ref, wq_ref, wk_ref, wv_ref, got_ref, peer_ref, out_ref, total_ref):
    W = wq_ref.shape[1]
    total = first_ref[...]
    for i, w in enumerate((wq_ref, wk_ref, wv_ref)):
        total = total + lax.dot_general(d_ref[:, i * W:(i + 1) * W], w[...], NT, preferred_element_type=f32)
    total_ref[...] = total
    n = got_ref.shape[0]
    for i, w in enumerate((got_ref, peer_ref)):
        at = pl.ds(pl.multiple_of(jnp.bitwise_xor(core_ref[0], i) * n, n), n)
        total_ref[:, at] += lax.dot_general(do_ref[...], w[...], NT, preferred_element_type=f32)
    out_ref[...] = total_ref[...].reshape(out_ref.shape)


def grad_tokens_of(core, first, d, do, weights, seq, after=()):
    rows, width = first.shape
    RB = 240
    block = lambda n: pl.BlockSpec((RB, n), lambda i: (i, 0))
    whole = lambda w: pl.BlockSpec(w.shape, lambda i: (0, 0))
    return pl.pallas_call(
        partial(skip_refs, tokens_kernel, 9, len(after)),
        grid=(rows // RB,),
        in_specs=[SMEM, block(width), block(d.shape[1]), block(d.shape[1])] + [whole(w) for w in weights] + [ANY] * len(after),
        out_specs=pl.BlockSpec((RB, 1, width), lambda i: (i, 0, 0)),
        out_shape=jax.ShapeDtypeStruct((seq, 1, width), f32),
        scratch_shapes=[pltpu.VMEM((RB, width), f32)],
        compiler_params=pltpu.CompilerParams(vmem_limit_bytes=VM),
        name="grad_tokens",
        cost_estimate=BRIEF,
    )(core, first, d, do, *weights, *after)

def swap(value, axis, bit=1):
    count = lax.axis_size(axis)
    return lax.ppermute(value, axis, [(i, i ^ bit) for i in range(count)])


def half_of(value, axis, which):
    size = value.shape[axis] // 2
    return lax.dynamic_slice_in_dim(value, which * size, size, axis)


def join(mine, theirs, which, axis=0):
    place = jnp.arange(2).reshape(2, 1, 1)
    return jnp.where(place == which, mine[None], theirs[None]).reshape(-1, mine.shape[1])


def far_bits():
    count = lax.axis_size("far")
    bits = []
    bit = 1
    while bit < count:
        bits.append(bit)
        bit *= 2
    return bits


def add_low(a, b):
    return (a.astype(f32) + b.astype(f32)).astype(bf)


def far_side(bit):
    return (lax.axis_index("far") // bit) % 2


def arrive(moment, *values):
    return lax.optimization_barrier(values + (moment,))[:-1]


def halve(parts, bit):
    at = far_side(bit)

    def pick(part, which):
        if isinstance(part, tuple):
            return jnp.concatenate([half_of(p, 0, which) for p in part], 1)
        return half_of(part, 0, which)

    add = lambda which: sum(pick(p, which).astype(f32) for p in parts).astype(bf)
    return add(at), swap(add(1 - at), "far", bit)


def double(total, got, bit, base):
    if total.shape[0] % 16:
        return join(total, got, far_side(bit), 0), base
    return jnp.concatenate([total, got], 0), base + [far_side(bit)]


def spread(total, got, base, widths, turned):
    place = 0
    for side in base[::-1]:
        place = 2 * place + side
    block = total.shape[0] >> len(base)
    return finish(total, got, lax.axis_index("core"), jnp.asarray(place), block, widths, turned)


def norm_parts(values):
    center = values - jnp.mean(values, axis=1, keepdims=True)
    inverse = lax.rsqrt(jnp.mean(center * center, axis=1, keepdims=True) + layer_eps)
    return center * inverse, inverse


def norm_back(grad_scaled, scaled, inverse):
    return inverse * (
        grad_scaled
        - jnp.mean(grad_scaled, axis=1, keepdims=True)
        - scaled * jnp.mean(grad_scaled * scaled, axis=1, keepdims=True)
    )


def gelu_parts(v):
    cdf = 0.5 * (1.0 + lax.erf(v * (0.5 ** 0.5)))
    pdf = jnp.exp(-0.5 * v * v) * (1.0 / math.sqrt(2.0 * math.pi))
    return v * cdf, cdf + v * pdf


def mm(a, b):
    return jnp.dot(a, b, preferred_element_type=f32)


def mm_nt(a, b):
    return lax.dot_general(a, b, (((1,), (1,)), ((), ())), preferred_element_type=f32)


def mm_tn(a, b):
    return lax.dot_general(a, b, (((0,), (0,)), ((), ())), preferred_element_type=f32)


def per_device(
    tokens, text_len, box_coords, w_query, b_query, w_key, w_value, b_value, w_out, b_out,
    table_seq, table_x, table_y, gain_attn, shift_attn, w_up, b_up, w_down, b_down,
    gain_ffn, shift_ffn, cotangent,
):
    seq, width = tokens.shape[1:]
    rows = -(-seq // 240) * 240
    lanes = -(-rows // PT) * PT
    local = w_query.shape[1]
    heads = local // HEAD_DIM
    hidden = w_up.shape[1]
    core = lax.axis_index("core")
    small_rows = -(-(2 + max(heads, 6)) // 8) * 8

    small, up_bias, bias, vectors = pack(
        [b_query, b_value, b_up, table_seq, table_x, table_y],
        [b_out, gain_attn, shift_attn, b_down, gain_ffn, shift_ffn], width, hidden,
    )
    small_o = swap(small, "tensor")
    halves, _ = lax.optimization_barrier((jnp.concatenate([half_of(w, 0, core) for w in (w_query, w_key, w_value)], 1), small))
    qkv_half = swap(halves, "tensor")
    b_out, gain_attn, shift_attn, b_down, gain_ffn, shift_ffn = vectors
    which = core.reshape(1).astype(jnp.int32)

    x = jnp.pad(tokens[0], ((0, rows - seq), (0, 0)))
    g = jnp.pad(cotangent[0], ((0, rows - seq), (0, 0)))
    both = project(which, x, [w_query, w_key, w_value], bias)
    q, k, v = (both, 0), (both, 1), (both, 2)
    idx, toep, toep_o, up_bias_o, bias_o = prep(text_len, box_coords[0], small, small_o, heads, rows, lanes)

    def fetched(got):
        return join(got, swap(got, "core"), core)

    qkv_half, out_half, up_half, idx, both = lax.optimization_barrier(
        (qkv_half, half_of(w_out, 0, core), half_of(w_up, 0, core), idx, both)
    )
    q, k, v = (both, 0), (both, 1), (both, 2)
    qkv_peer = swap(qkv_half, "core")
    out_half = swap(out_half, "tensor")
    up_half = swap(up_half, "tensor")
    ctx, prob = attn_fwd(q, k, v, local, idx, toep, small, (qkv_half,))
    qkv_peer, out_half, down_half, ctx = arrive(ctx, qkv_peer, out_half, half_of(w_down, 0, core), ctx)
    down_half = swap(down_half, "tensor")
    both_o = project(which, x, [qkv_half, qkv_peer], bias_o)
    q_o, k_o, v_o = (both_o, 0), (both_o, 1), (both_o, 2)
    wo_o = fetched(out_half)
    ctx_o, prob_o = attn_fwd(q_o, k_o, v_o, local, idx, toep_o, small_o, (wo_o,))
    wu_o = fetched(up_half)

    attn = mm(ctx, w_out) + mm(ctx_o, wo_o) + b_out
    n1, inv1 = norm_parts(x.astype(f32) + attn)
    normed = n1 * gain_attn + shift_attn
    low = normed.astype(bf)
    act, slope = gelu_parts(mm(low, w_up) + up_bias)
    act_o, slope_o = gelu_parts(mm(low, wu_o) + up_bias_o)
    act, act_o = act.astype(bf), act_o.astype(bf)
    down_half, act, act_o = lax.optimization_barrier((down_half, act, act_o))
    wd_o = fetched(down_half)
    slope, slope_o = slope.astype(bf), slope_o.astype(bf)
    branch = mm(act, w_down) + mm(act_o, wd_o) + b_down
    n2, inv2 = norm_parts(normed + branch)
    output = (n2 * gain_ffn + shift_ffn).astype(bf)[:seq][None]

    gf = g.astype(f32)
    grad_gain_ffn = jnp.sum(gf * n2, axis=0)
    grad_shift_ffn = jnp.sum(gf, axis=0)
    grad_mid = norm_back(gf * gain_ffn, n2, inv2)
    gb = grad_mid.astype(bf)
    grad_b_down = jnp.sum(gb.astype(f32), axis=0)

    def terms(left, right):
        sent = swap(mm_tn(half_of(left, 1, 1 - core), right).astype(bf), "core")
        return mm_tn(half_of(left, 1, core), right).astype(bf), sent

    def add_three(a, b, c):
        return (a.astype(f32) + b.astype(f32) + c.astype(f32)).astype(bf)

    bits = far_bits()
    down_o = add_low(*terms(act_o, gb))
    down_x = swap(down_o, "tensor")
    gh_o = (mm_nt(gb, wd_o) * slope_o.astype(f32)).astype(bf)
    gb, down_o = lax.optimization_barrier((gb, down_o))
    down = terms(act, gb)
    gh = (mm_nt(gb, w_down) * slope.astype(f32)).astype(bf)
    grad_b_up = jnp.sum(gh.astype(f32), axis=0)
    grad_b_up_o = jnp.sum(gh_o.astype(f32), axis=0)
    up_o = terms(low, gh_o)
    up = terms(low, gh)
    grad_normed = mm_nt(gh, w_up) + mm_nt(gh_o, wu_o) + grad_mid
    grad_gain_attn = jnp.sum(grad_normed * n1, axis=0)
    grad_shift_attn = jnp.sum(grad_normed, axis=0)
    grad_first = norm_back(grad_normed * gain_attn, n1, inv1)
    ga = grad_first.astype(bf)
    grad_b_out = jnp.sum(ga.astype(f32), axis=0)
    out_o = terms(ga, ctx_o)
    out = terms(ga, ctx)
    gc_o = mm_nt(ga, wo_o).astype(bf)
    gc = mm_nt(ga, w_out).astype(bf)
    up_o = add_low(jnp.concatenate([up_o[0], out_o[0]], 1), jnp.concatenate([up_o[1], out_o[1]], 1))
    up_x = swap(up_o, "tensor")
    up = list(zip(up, out))
    dqkv_o, gs_o = attn_bwd(q_o, k_o, v_o, local, gc_o, prob_o, (up_o, output))
    down_x, = arrive(gs_o, down_x)
    down = halve([*down, down_x], bits[0])
    qkv_o = add_low(*terms(x, dqkv_o))
    qkv_x = swap(qkv_o, "tensor")
    dqkv, gs = attn_bwd(q, k, v, local, gc, prob, (down[0], qkv_o))

    up_x, down_in = arrive(gs, up_x, down[1])
    down = halve([down[0], down_in], bits[1])
    up = halve([*up, up_x], bits[0])
    qkv = terms(x, dqkv)
    sums = [hist(gs, gs_o, idx, 0, 6, (up[0], down[0], qkv[0]))]

    down_in, up_in, qkv_core, qkv_x = arrive(sums[-1][0], down[1], up[1], qkv[1], qkv_x)
    down = [down[0], down_in]
    for bit in bits[3:]:
        down = halve(down, bit)
    down = halve(down, bits[2])
    up = halve([up[0], up_in], bits[1])
    qkv = halve([qkv[0], qkv_core, qkv_x], bits[0])
    sums.append(hist(gs, gs_o, idx, 6, 3, (qkv[0], up[0], down[0])))

    down_in, up_in, qkv_in = arrive(sums[-1][0], down[1], up[1], qkv[1])
    down_base, up_base, base = [], [], []
    down = add_low(down[0], down_in)
    for bit in bits[:2:-1]:
        down, down_base = double(down, swap(down, "far", bit), bit, down_base)
    down_in = swap(down, "far", bits[2])
    up = [up[0], up_in]
    for bit in bits[3:]:
        up = halve(up, bit)
    up = halve(up, bits[2])
    qkv = halve([qkv[0], qkv_in], bits[1])
    sums.append(hist(gs, gs_o, idx, 9, 3, (up[0], qkv[0], down)))

    down_in, up_in, qkv_in = arrive(sums[-1][0], down_in, up[1], qkv[1])
    down, down_base = double(down, down_in, bits[2], down_base)
    down_in = swap(down, "far", bits[1])
    up = add_low(up[0], up_in)
    for bit in bits[:2:-1]:
        up, up_base = double(up, swap(up, "far", bit), bit, up_base)
    up_in = swap(up, "far", bits[2])
    qkv = [qkv[0], qkv_in]
    for bit in bits[3:]:
        qkv = halve(qkv, bit)
    qkv = halve(qkv, bits[2])
    sums.append(hist(gs, gs_o, idx, 12, 3, (up, qkv[0], down)))

    down_in, up_in, qkv_in = arrive(sums[-1][0], down_in, up_in, qkv[1])
    qkv = add_low(qkv[0], qkv_in)
    for bit in bits[:2:-1]:
        qkv, base = double(qkv, swap(qkv, "far", bit), bit, base)
    qkv_in = swap(qkv, "far", bits[2])
    up, up_base = double(up, up_in, bits[2], up_base)
    up_in = swap(up, "far", bits[1])
    down, down_base = double(down, down_in, bits[1], down_base)
    down_in = swap(down, "far", bits[0])
    shared = [grad_b_out, grad_gain_attn, grad_shift_attn, grad_b_down, grad_gain_ffn, grad_shift_ffn]
    payload, payload_o = pack_sums(sums, dqkv, dqkv_o, grad_b_up, grad_b_up_o, shared, small_rows, hidden, (up, qkv, down))

    total, total_in = payload, swap(payload_o, "tensor")
    up_in, qkv_in = arrive(payload, up_in, qkv_in)
    qkv, base = double(qkv, qkv_in, bits[2], base)
    qkv_in = swap(qkv, "far", bits[1])
    up, up_base = double(up, up_in, bits[1], up_base)
    up_in = swap(up, "far", bits[0])
    total_in, up = arrive(up, total_in, up)
    total = total + total_in
    total_in = swap(total, "core")
    grad_tokens = grad_tokens_of(which, grad_first, dqkv, dqkv_o, [w_query, w_key, w_value, qkv_half, qkv_peer], seq, (up, qkv, total))

    qkv_in, total_in, down_in = arrive(grad_tokens, qkv_in, total_in, down_in)
    qkv, base = double(qkv, qkv_in, bits[1], base)
    qkv_in = swap(qkv, "far", bits[0])
    total = total + total_in
    total_in = swap(total, "far", bits[0])
    down, down_base = double(down, down_in, bits[0], down_base)
    down_in = swap(down, "core")
    up_in, qkv, down, total = arrive(qkv, up_in, qkv, down, total)
    up, up_base = double(up, up_in, bits[0], up_base)
    up_in = swap(up, "core")
    down_in, total_in, up = arrive(up, down_in, total_in, up)
    total = total + total_in
    total_in = swap(total, "far", bits[1])
    grad_w_down, = spread(down, down_in, down_base, (width,), (False,))
    total_in, up_in = arrive(grad_w_down, total_in, up_in)
    total = total + total_in
    total_in = swap(total, "far", bits[2])
    grad_w_up, grad_w_out = spread(up, up_in, up_base, (hidden, local), (False, True))
    total_in, qkv_in = arrive(grad_w_up, total_in, qkv_in)
    qkv, base = double(qkv, qkv_in, bits[0], base)
    qkv_in = swap(qkv, "core")
    total = total + total_in
    for bit in bits[3:]:
        total = total + swap(total, "far", bit)
    grads_qkv = spread(qkv, qkv_in, base, (local,) * 3, (False,) * 3)
    totals = total
    grads_qkv = spread(qkv, qkv_in, base, (local,) * 3, (False,) * 3)
    grad_tokens = grad_tokens.reshape(1, seq, width)
    shapes = [(local,), (local,), (hidden,), table_seq.shape, table_x.shape, table_y.shape] + [(width,)] * 6
    pieces = unpack_sums(totals, local, heads, shapes)
    g_bq, g_bv, g_bu, g_ts, g_tx, g_ty, g_bo, g_ga, g_sa, g_bd, g_gf, g_sf = pieces
    return (
        output, grad_tokens,
        grads_qkv[0], g_bq, grads_qkv[1], grads_qkv[2], g_bv,
        grad_w_out, g_bo, g_ts, g_tx, g_ty, g_ga, g_sa, grad_w_up, g_bu, grad_w_down, g_bd, g_gf, g_sf,
    )


def solution(mesh):
    grid = mesh.devices.shape
    mesh = jax.sharding.Mesh(mesh.devices.reshape(grid[0] // 2, 2, grid[1]), ("far", "core", "tensor"))
    every = ("far", "core", "tensor")
    item = P(every, None, None)
    column, row, split, copied = P(None, "tensor"), P("tensor", None), P("tensor"), P()
    return jax.shard_map(
        per_device,
        mesh=mesh,
        in_specs=(
            item, P(every), item, column, split, column, column, split, row, copied,
            row, row, row, copied, copied, column, split, row, copied, copied, copied, item,
        ),
        out_specs=(
            item, item, column, split, column, column, split, row, copied, row, row, row,
            copied, copied, column, split, row, copied, copied, copied,
        ),
        check_vma=False,
    )
```

```python
from functools import partial
import math

import jax
import jax.numpy as jnp
from jax import lax
from jax.experimental import pallas as pl
from jax.experimental.pallas import tpu as pltpu
from jax.sharding import PartitionSpec as P

HEAD_DIM = 64
BUCKETS = 32
MAX_DIST = 128
BUCKETS_2D = 64
MAX_DIST_2D = 256
TEXT = 512
layer_eps = 1e-05

f32 = jnp.float32
bf = jnp.bfloat16
i16 = jnp.int16
PT = 256
NT = (((1,), (1,)), ((), ()))
VM = 56 << 20

USUAL = pl.CostEstimate(flops=10_000_000_000, bytes_accessed=1, transcendentals=0)


SHORT = pl.CostEstimate(flops=1, bytes_accessed=1, transcendentals=0)


def bucket_edges(buckets, farthest):
    exact=buckets//4
    r=list(range(1,exact+1))
    for k in range(1,exact):
        r.append(int(math.ceil(exact*(farthest/exact)**(k/exact)-1e-09)))
    return r
def lane_gather(table, index):
    dn=lax.GatherDimensionNumbers(offset_dims=(),collapsed_slice_dims=(1,),start_index_map=(1,),operand_batching_dims=(0,),start_indices_batching_dims=(0,))
    return lax.gather(table,index[...,None],dn,(1,1),mode=lax.GatherScatterMode.PROMISE_IN_BOUNDS)

def prep_kernel(len_ref, box_ref, own_ref, oth_ref, idx_ref, toep_ref, toep_o_ref, up_ref, bias_ref, line_ref, col_ref, *, seq):
    up_ref[...] = oth_ref[0:1, :].astype(f32)
    bias_ref[...] = oth_ref[1:2, 0:bias_ref.shape[1]].astype(f32)
    rows, lanes = idx_ref.shape[1:]
    heads = toep_ref.shape[0]
    edges = bucket_edges(BUCKETS_2D, MAX_DIST_2D)
    near = [e for e in edges if e < 128]
    far = [e for e in edges if e >= 128]
    n = len_ref[0]
    rb = 16
    line_ref[...] = jnp.zeros_like(line_ref)
    line_ref[0:2, 0:seq] = box_ref[...].astype(f32)
    col_ref[...] = line_ref[...].T
    lane = lax.broadcasted_iota(jnp.int32, (rb, 128), 1)
    tab = jnp.zeros((rb, 128), jnp.int32)
    for e in near:
        tab = tab + jnp.where(lane >= e, 1, 0)
    tab = tab.astype(i16)

    def body(i, _):
        r = pl.ds(pl.multiple_of(i * rb, rb), rb)
        place = lax.broadcasted_iota(jnp.int32, (rb, 128), 0) + i * rb
        ok = ((place < n) | (place >= TEXT)) & (place < seq)
        for ax in range(2):
            col = jnp.broadcast_to(col_ref[r, ax:ax + 1], (rb, 128))
            for c in range(lanes // 128):
                cs = slice(c * 128, (c + 1) * 128)
                d = col - line_ref[ax:ax + 1, cs]
                a = jnp.abs(d)
                b = jnp.where(d > 0, float(BUCKETS_2D // 2), 0.0)
                for e in far:
                    b = b + jnp.where(a >= e, 1.0, 0.0)
                b = b.astype(jnp.int32).astype(i16) + lane_gather(tab, jnp.minimum(a, 127.0).astype(jnp.int32).astype(i16))
                if ax == 1:
                    b = jnp.where(ok, b.astype(jnp.int32), BUCKETS_2D).astype(i16)
                idx_ref[ax, r, cs] = b
        return 0

    lax.fori_loop(0, rows // rb, body, 0, unroll=5)
    for j in range(5):
        d = lax.broadcasted_iota(jnp.int32, (128, 128), 0) - lax.broadcasted_iota(jnp.int32, (128, 128), 1) + 128 * (j - 2)
        a = jnp.abs(d)
        b = jnp.zeros_like(d)
        for e in bucket_edges(BUCKETS, MAX_DIST):
            b = b + jnp.where(a >= e, 1, 0)
        b = (b + jnp.where(d > 0, BUCKETS // 2, 0)).astype(i16)
        for src, dst in ((own_ref, toep_ref), (oth_ref, toep_o_ref)):
            for h in range(heads):
                dst[h, j * 128:(j + 1) * 128, :] = lane_gather(jnp.broadcast_to(src[2 + h:3 + h, 0:128], (128, 128)), b)


VMEM = pl.BlockSpec(memory_space=pltpu.VMEM)
SMEM = pl.BlockSpec(memory_space=pltpu.SMEM)
ANY = pl.BlockSpec(memory_space=pl.ANY)


def prep(length, box, own, oth, heads, rows, lanes):
    seq = box.shape[1]
    toep = jax.ShapeDtypeStruct((heads, 640, 128), bf)
    return pl.pallas_call(
        partial(prep_kernel, seq=seq),
        out_shape=(
            jax.ShapeDtypeStruct((2, rows, lanes), i16), toep, toep,
            jax.ShapeDtypeStruct((1, own.shape[1]), f32), jax.ShapeDtypeStruct((1, 3 * heads * HEAD_DIM), f32),
        ),
        in_specs=[SMEM, VMEM, VMEM, VMEM],
        out_specs=(VMEM,) * 5,
        scratch_shapes=[pltpu.VMEM((8, lanes), f32), pltpu.VMEM((lanes, 8), f32)],
        compiler_params=pltpu.CompilerParams(vmem_limit_bytes=VM),
        name="buckets",
        cost_estimate=USUAL,
    )(length, box, own, oth)


def pack_kernel(bq, bv, bu, ts, tx, ty, *refs):
    vectors, small_ref, up_ref, bias_ref, rows = refs[:6], refs[6], refs[7], refs[8], refs[9:]
    local = bq.shape[0]
    heads = ts.shape[0]
    hidden = bu.shape[0]
    small_ref[...] = jnp.zeros_like(small_ref)
    small_ref[0:1, 0:hidden] = bu[...][None]
    small_ref[1:2, 0:local] = bq[...][None]
    small_ref[1:2, 2 * local:3 * local] = bv[...][None]
    small_ref[2:2 + heads, 0:ts.shape[1]] = ts[...]
    small_ref[2:2 + heads, 128:128 + tx.shape[1]] = tx[...]
    small_ref[2:2 + heads, 256:384] = jnp.full((heads, 128), -1e9, bf)
    small_ref[2:2 + heads, 256:256 + ty.shape[1]] = ty[...]
    up_ref[...] = bu[...].astype(f32)[None]
    bias_ref[...] = jnp.zeros_like(bias_ref)
    bias_ref[0:1, 0:local] = bq[...].astype(f32)[None]
    bias_ref[0:1, 2 * local:3 * local] = bv[...].astype(f32)[None]
    for v, row in zip(vectors, rows):
        row[...] = v[...].astype(f32)[None]


def pack(split, copied, width, hidden):
    row = lambda n: jax.ShapeDtypeStruct((1, n), f32)
    out = pl.pallas_call(
        pack_kernel,
        out_shape=[jax.ShapeDtypeStruct((16, hidden), bf), row(hidden), row(3 * split[0].shape[0])] + [row(width)] * 6,
        in_specs=[VMEM] * 12,
        out_specs=[VMEM] * 9,
        name="pack",
        cost_estimate=USUAL,
    )(*split, *copied)
    return out[0], out[1], out[2], out[3:]


def project_kernel(core_ref, x_ref, *refs):
    weights, bias_ref, out_ref = refs[:-2], refs[-2], refs[-1]
    if len(weights) == 3:
        at = 0
        for w in weights:
            n = w.shape[1]
            part = jnp.dot(x_ref[...], w[...], preferred_element_type=f32) + bias_ref[:, at:at + n]
            out_ref[:, at:at + n] = part.astype(bf)
            at += n
        return
    n = weights[0].shape[0]
    total = bias_ref[...]
    for i, w in enumerate(weights):
        at = pl.multiple_of(jnp.bitwise_xor(core_ref[0], i) * n, n)
        total = total + jnp.dot(x_ref[:, pl.ds(at, n)], w[...], preferred_element_type=f32)
    out_ref[...] = total.astype(bf)


def project(core, x, weights, bias):
    rows, width = x.shape
    RB = rows // 3
    whole = lambda w: pl.BlockSpec(w.shape, lambda i: (0, 0))
    return pl.pallas_call(
        project_kernel,
        grid=(rows // RB,),
        in_specs=[SMEM, pl.BlockSpec((RB, width), lambda i: (i, 0))] + [whole(w) for w in weights] + [whole(bias)],
        out_specs=pl.BlockSpec((RB, bias.shape[1]), lambda i: (i, 0)),
        out_shape=jax.ShapeDtypeStruct((rows, bias.shape[1]), bf),
        compiler_params=pltpu.CompilerParams(vmem_limit_bytes=VM),
        name="project",
        cost_estimate=USUAL,
    )(core, x, *weights, bias)


def keep_rows(x,first_row,limit):
    rr=lax.broadcasted_iota(jnp.int32,(x.shape[0],1),0)+first_row
    return jnp.where(rr<limit,x,jnp.zeros_like(x))

def fwd_kernel(q_ref, k_ref, v_ref, idx_ref, toep_ref, small_ref, ctx_ref, p_ref, inv_ref, s_ref, qm_ref):
    H,rows,PT=p_ref.shape
    nch=PT//128
    tile=pl.program_id(0)
    lane=lax.broadcasted_iota(jnp.int32,(1,128),1)
    first=lane<HEAD_DIM
    for hp in range(H//2):
        hs=slice(hp*128,(hp+1)*128)
        q=keep_rows(q_ref[:,hs],tile*PT,rows)*jnp.asarray(HEAD_DIM**-0.5,bf)
        for h in range(2):
            qm=jnp.where(first if h==0 else ~first,q,jnp.zeros_like(q))
            qm_ref[2*hp+h]=qm
    tabs=[(jnp.broadcast_to(small_ref[2+h:3+h,128:256],(16,128)),jnp.broadcast_to(small_ref[2+h:3+h,256:384],(16,128))) for h in range(H)]
    cuts=[(h,c) for c in range(nch) for h in range(H)]
    BR=144
    def block1(i,ms):
        r=pl.ds(pl.multiple_of(i*BR,16),BR)
        for h in range(H):
            s_ref[h,r,:]=lax.dot_general(k_ref[r,h//2*128:(h//2+1)*128],qm_ref[h],NT,preferred_element_type=f32)
        for g in range(BR//16):
            ms=pass1(i*(BR//16)+g,ms)
        return ms
    def pass1(g,ms):
        r0=pl.multiple_of(g*16,16); r=pl.ds(r0,16)
        sb=r0//128; off=r0%128
        out=[]
        for c in range(nch):
            cs=slice(c*128,(c+1)*128)
            ix=idx_ref[0,r,cs]; iy=idx_ref[1,r,cs]
            tr=pl.ds(pl.multiple_of((jnp.clip(sb-(tile*nch+c),-2,2)+2)*128+off,16),16)
            gx=[lane_gather(tabs[h][0],ix) for h in range(H)]
            gy=[lane_gather(tabs[h][1],iy) for h in range(H)]
            for h in range(H):
                s=s_ref[h,r,cs]+gx[h].astype(f32)+gy[h].astype(f32)+toep_ref[h,tr,:].astype(f32)
                s_ref[h,r,cs]=s
                out.append(jnp.maximum(ms[c*H+h],jnp.maximum(s[:8],s[8:])))
        return tuple(out)
    ms=lax.fori_loop(0,rows//BR,block1,tuple(jnp.full((8,128),-jnp.inf,f32) for _ in cuts))
    ms=[jnp.max(m,axis=0,keepdims=True) for m in ms]
    def pass2(g,ls):
        r=pl.ds(pl.multiple_of(g*16,16),16)
        out=[]
        for i,(h,c) in enumerate(cuts):
            cs=slice(c*128,(c+1)*128)
            e=jnp.exp(s_ref[h,r,cs]-ms[i])
            p_ref[h,r,cs]=e.astype(bf)
            out.append(ls[i]+(e[:8]+e[8:]))
        return tuple(out)
    ls=lax.fori_loop(0,rows//16,pass2,tuple(jnp.zeros((8,128),f32) for _ in cuts),unroll=5)
    inv=[1.0/jnp.sum(l,axis=0,keepdims=True) for l in ls]
    for i,(h,c) in enumerate(cuts):
        inv_ref[h:h+1,c*128:(c+1)*128]=inv[i]
    for hp in range(H//2):
        hs=slice(hp*128,(hp+1)*128)
        vt=v_ref[:,hs].T
        o=[jnp.dot(vt[h*64:(h+1)*64],p_ref[2*hp+h],preferred_element_type=f32)*inv_ref[2*hp+h:2*hp+h+1,:] for h in range(2)]
        ctx_ref[:,hs]=jnp.concatenate(o,0).T.astype(bf)

def attn_fwd(q, k, v, W, idx, toep, small, after=()):
    rows = q[0].shape[0]
    H = W // HEAD_DIM
    lanes = idx.shape[2]
    whole = lambda shape: pl.BlockSpec(shape, lambda i: (0,) * len(shape))
    column = lambda at: pl.BlockSpec((rows, W), lambda i: (0, at))
    return pl.pallas_call(
        partial(skip_refs, fwd_kernel, 6, len(after)),
        grid=(lanes // PT,),
        in_specs=[pl.BlockSpec((PT, W), lambda i: (i, q[1])), column(k[1]), column(v[1]), pl.BlockSpec((2, rows, PT), lambda i: (0, 0, i)), whole(toep.shape), whole(small.shape)] + [ANY] * len(after),
        out_specs=(pl.BlockSpec((PT, W), lambda i: (i, 0)), pl.BlockSpec((H, rows, PT), lambda i: (0, 0, i)), pl.BlockSpec((H, PT), lambda i: (0, i))),
        out_shape=(jax.ShapeDtypeStruct((rows, W), bf), jax.ShapeDtypeStruct((H, rows, lanes), bf), jax.ShapeDtypeStruct((H, lanes), f32)),
        scratch_shapes=[pltpu.VMEM((H, rows, PT), f32), pltpu.VMEM((H, PT, 128), bf)],
        compiler_params=pltpu.CompilerParams(vmem_limit_bytes=VM),
        name="attn_fwd",
        cost_estimate=USUAL,
    )(q[0], k[0], v[0], idx, toep, small, *after)


def skip_refs(kernel, first, count, *refs):
    kernel(*refs[:first], *refs[first + count:])


def bwd_kernel(q_ref, k_ref, v_ref, do_ref, p_ref, inv_ref, out_ref, gs_ref, dp_ref, dka, dva, dqa):
    H,rows,PT=p_ref.shape
    nch=PT//128
    tile=pl.program_id(0); last=pl.num_programs(0)-1
    lane=lax.broadcasted_iota(jnp.int32,(1,128),1)
    first=lane<HEAD_DIM
    scale=HEAD_DIM**-0.5
    cuts=[(h,c) for c in range(nch) for h in range(H)]
    split=lambda x: (jnp.where(first,x,jnp.zeros_like(x)),jnp.where(first,jnp.zeros_like(x),x))
    for hp in range(H//2):
        hs=slice(hp*128,(hp+1)*128)
        dm=split(keep_rows(do_ref[:,hs],tile*PT,rows))
        for h in range(2):
            dp_ref[2*hp+h]=lax.dot_general(v_ref[:,hs],dm[h],NT,preferred_element_type=f32)
    def pass1(g,ds):
        r=pl.ds(pl.multiple_of(g*16,16),16)
        out=[]
        for i,(h,c) in enumerate(cuts):
            cs=slice(c*128,(c+1)*128)
            t=p_ref[h,r,cs].astype(f32)*dp_ref[h,r,cs]
            out.append(ds[i]+(t[:8]+t[8:]))
        return tuple(out)
    ds=lax.fori_loop(0,rows//16,pass1,tuple(jnp.zeros((8,128),f32) for _ in cuts),unroll=9)
    iv=[inv_ref[h:h+1,c*128:(c+1)*128] for h,c in cuts]
    ds=[jnp.sum(d,axis=0,keepdims=True)*v*v for d,v in zip(ds,iv)]
    def pass2(g,_):
        r=pl.ds(pl.multiple_of(g*16,16),16)
        for i,(h,c) in enumerate(cuts):
            cs=slice(c*128,(c+1)*128)
            gs_ref[h,r,cs]=(p_ref[h,r,cs].astype(f32)*(dp_ref[h,r,cs]*iv[i]-ds[i])).astype(bf)
        return 0
    lax.fori_loop(0,rows//16,pass2,0,unroll=9)
    @pl.when(tile==0)
    def _():
        dka[...]=jnp.zeros_like(dka); dva[...]=jnp.zeros_like(dva)
    pad=jnp.zeros((-H%8,PT),f32)
    col=jnp.concatenate([inv_ref[...],pad],0).T
    for hp in range(H//2):
        hs=slice(hp*128,(hp+1)*128)
        kt=k_ref[:,hs].T
        o=[jnp.dot(kt[h*64:(h+1)*64],gs_ref[2*hp+h],preferred_element_type=f32) for h in range(2)]
        dq=(jnp.concatenate(o,0)*scale).T.astype(bf)
        dqa[pl.ds(pl.multiple_of(tile*PT,PT),PT),hs]=dq
        qm=split(keep_rows(q_ref[:,hs],tile*PT,rows))
        dm=split(keep_rows(do_ref[:,hs],tile*PT,rows).astype(f32))
        dm=[(dm[h]*col[:,2*hp+h:2*hp+h+1]).astype(bf) for h in range(2)]
        dka[:,hs]+=jnp.dot(gs_ref[2*hp],qm[0],preferred_element_type=f32)+jnp.dot(gs_ref[2*hp+1],qm[1],preferred_element_type=f32)
        dva[:,hs]+=jnp.dot(p_ref[2*hp],dm[0],preferred_element_type=f32)+jnp.dot(p_ref[2*hp+1],dm[1],preferred_element_type=f32)
    @pl.when(tile==last)
    def _():
        W=dka.shape[1]
        out_ref[:,0:W]=dqa[0:rows,:]
        out_ref[:,W:2*W]=(dka[...]*scale).astype(bf)
        out_ref[:,2*W:]=dva[...].astype(bf)

def attn_bwd(q, k, v, W, do, p, inv, after=()):
    rows = do.shape[0]
    H = W // HEAD_DIM
    lanes = p.shape[2]
    column = lambda at: pl.BlockSpec((rows, W), lambda i: (0, at))
    big = pl.BlockSpec((H, rows, PT), lambda i: (0, 0, i))
    return pl.pallas_call(
        partial(skip_refs, bwd_kernel, 6, len(after)),
        grid=(lanes // PT,),
        in_specs=[pl.BlockSpec((PT, W), lambda i: (i, q[1])), column(k[1]), column(v[1]), pl.BlockSpec((PT, W), lambda i: (i, 0)), big, pl.BlockSpec((H, PT), lambda i: (0, i))] + [ANY] * len(after),
        out_specs=(pl.BlockSpec((rows, 3 * W), lambda i: (0, 0)), big),
        out_shape=(jax.ShapeDtypeStruct((rows, 3 * W), bf), jax.ShapeDtypeStruct((H, rows, lanes), bf)),
        scratch_shapes=[pltpu.VMEM((H, rows, PT), f32), pltpu.VMEM((rows, W), f32), pltpu.VMEM((rows, W), f32), pltpu.VMEM((lanes, W), bf)],
        compiler_params=pltpu.CompilerParams(vmem_limit_bytes=VM),
        name="attn_bwd",
        cost_estimate=SHORT,
    )(q[0], k[0], v[0], do, p, inv, *after)


def finish_kernel(info_ref, mine_ref, theirs_ref, *refs, block, widths, turned):
    rows = mine_ref.shape[0]
    count = rows // block
    n = len(widths)
    outs, wide, sems = refs[:n], refs[n:2 * n], refs[2 * n]
    copies = []
    for p, src in enumerate((mine_ref, theirs_ref)):
        for j in range(count):
            rs = slice(j * block, (j + 1) * block)
            place = pl.multiple_of((jnp.bitwise_xor(info_ref[0], p) * count + jnp.bitwise_xor(info_ref[1], j)) * block, block)
            at = 0
            for i in range(n):
                part = src[rs, at:at + widths[i]].astype(f32)
                at += widths[i]
                if turned[i]:
                    wide[i][pl.ds(place, block), :] = part
                else:
                    wide[i][p, rs, :] = part
                    copy = pltpu.make_async_copy(wide[i].at[p, rs, :], outs[i].at[pl.ds(place, block), :], sems.at[p, j, i])
                    copy.start()
                    copies.append(copy)
    for i in range(n):
        if turned[i]:
            refs[2 * n + 1][...] = wide[i][...].T
            copy = pltpu.make_async_copy(refs[2 * n + 1], outs[i], sems.at[0, 0, i])
            copy.start()
            copies.append(copy)
    for copy in copies:
        copy.wait()


def finish(mine, theirs, info, block, widths, turned):
    rows = mine.shape[0]
    return pl.pallas_call(
        partial(finish_kernel, block=block, widths=widths, turned=turned),
        in_specs=[SMEM, VMEM, VMEM],
        out_specs=[ANY] * len(widths),
        out_shape=[jax.ShapeDtypeStruct((w, 2 * rows) if t else (2 * rows, w), f32) for w, t in zip(widths, turned)],
        scratch_shapes=[pltpu.VMEM((2 * rows, w) if t else (2, rows, w), f32) for w, t in zip(widths, turned)]
        + [pltpu.SemaphoreType.DMA((2, rows // block, len(widths)))]
        + [pltpu.VMEM((w, 2 * rows), f32) for w, t in zip(widths, turned) if t],
        compiler_params=pltpu.CompilerParams(vmem_limit_bytes=VM),
        name="finish",
        cost_estimate=USUAL,
    )(info, mine, theirs)


def hist_kernel(gs_ref, go_ref, idx_ref, out_ref, toep_ref, acc, accT, *, part):
    H, rows, lanes = gs_ref.shape
    SB = 16
    heads = 2 * H
    near = BUCKETS_2D // 2
    step = pl.program_id(0)

    @pl.when(step == 0)
    def _():
        acc[...] = jnp.zeros_like(acc)
        accT[...] = jnp.zeros_like(accT)

    iota = lax.broadcasted_iota(jnp.int32, (near, lanes), 0).astype(i16)
    one = jnp.ones((near, lanes), bf)
    zero = jnp.zeros((near, lanes), bf)

    def body(i, _):
        r = pl.ds(pl.multiple_of(i * SB, SB), SB)
        s0 = (part + step) * rows + i * SB
        sb = s0 // 128
        off = pl.multiple_of(s0 % 128, SB)
        idx = [idx_ref[ax, r, :] for ax in range(2)]
        positive = [(x >= near).astype(i16).astype(jnp.int32) > 0 for x in idx]
        cols = [[], []]
        for ref in (gs_ref, go_ref):
            for h in range(H):
                full = ref[h, r, :].astype(f32)
                k = len(cols[0])
                for c in range(lanes // 128):
                    at = pl.ds(pl.multiple_of((jnp.clip(sb - c, -2, 2) + 2) * 128 + off, SB), SB)
                    accT[k, at, :] += full[:, c * 128:(c + 1) * 128]
                for ax in range(2):
                    some = jnp.where(positive[ax], full, 0.0)
                    cols[ax].append([jnp.concatenate([full[t:t + 8], some[t:t + 8]], 0).astype(bf) for t in (0, 8)])
        for ax in range(2):
            ix = jnp.bitwise_and(idx[ax], jnp.asarray(near - 1, i16))
            left = []
            right = []
            for t in range(2):
                left.append(jnp.concatenate([jnp.where(iota == ix[t * 8 + p:t * 8 + p + 1, :], one, zero) for p in range(8)], 0))
                right.append(jnp.concatenate([x[t] for x in cols[ax]], 0))
            acc[ax] += lax.dot_general(jnp.concatenate(left, 1), jnp.concatenate(right, 1), NT, preferred_element_type=f32)
        return 0

    lax.fori_loop(0, rows // SB, body, 0, unroll=3)

    @pl.when(step == pl.num_programs(0) - 1)
    def _():
        lane = lax.broadcasted_iota(jnp.int32, (near, heads * SB), 1) % 8
        for ax in range(2):
            t = jnp.zeros((near, heads * SB), f32)
            for p in range(8):
                t = t + jnp.where(lane == p, acc[ax, p * near:(p + 1) * near, :], 0.0)
            out_ref[ax] = t
        lane8 = lax.broadcasted_iota(jnp.int32, (8, 128), 1)
        row8 = lax.broadcasted_iota(jnp.int32, (8, 128), 0)
        kept = {}
        for g in range(16):
            turned = lane8 + row8 + 8 * g
            wraps = turned >= 128
            turned = jnp.where(wraps, turned - 128, turned)
            for h in range(heads):
                for j in (-1, 0, 1):
                    at = (j + 2) * 128 + 8 * g
                    x = lane_gather(accT[h, at:at + 8, :], turned)
                    for k, part_sum in enumerate((jnp.where(wraps, 0.0, x), jnp.where(wraps, x, 0.0))):
                        key = (h, 2 * (j + 1) + k)
                        kept[key] = part_sum if g == 0 else kept[key] + part_sum
        for h in range(heads):
            for k in range(6):
                toep_ref[h, k:k + 1, :] = jnp.sum(kept[h, k], axis=0, keepdims=True)
            toep_ref[h, 6:7, :] = jnp.sum(accT[h, 0:128, :], axis=0, keepdims=True)
            toep_ref[h, 7:8, :] = jnp.sum(accT[h, 512:640, :], axis=0, keepdims=True)


def hist(gs, go, idx, part, steps, after=()):
    H, rows, lanes = gs.shape
    SB = 48
    near = BUCKETS_2D // 2
    big = pl.BlockSpec((H, SB, lanes), lambda i: (0, part + i, 0))
    return pl.pallas_call(
        partial(skip_refs, partial(hist_kernel, part=part), 3, len(after)),
        grid=(steps,),
        in_specs=[big, big, pl.BlockSpec((2, SB, lanes), lambda i: (0, part + i, 0))] + [ANY] * len(after),
        out_specs=(pl.BlockSpec((2, near, 2 * H * 16), lambda i: (0, 0, 0)), pl.BlockSpec((2 * H, 8, 128), lambda i: (0, 0, 0))),
        out_shape=(jax.ShapeDtypeStruct((2, near, 2 * H * 16), f32), jax.ShapeDtypeStruct((2 * H, 8, 128), f32)),
        scratch_shapes=[pltpu.VMEM((2, 8 * near, 2 * H * 16), f32), pltpu.VMEM((2 * H, 640, 128), f32)],
        compiler_params=pltpu.CompilerParams(vmem_limit_bytes=VM),
        name="table_sums",
        cost_estimate=USUAL,
    )(gs, go, idx, *after)


def tables_kernel(*refs, parts):
    sums = refs[:2 * parts]
    dqkv, dqkv_o, up, up_o = refs[2 * parts:2 * parts + 4]
    shared = refs[2 * parts + 4:-2]
    outs = refs[-2:]
    out = sums[0][...]
    toep = sums[1][...]
    for i in range(1, parts):
        out = out + sums[2 * i][...]
        toep = toep + sums[2 * i + 1][...]
    heads = toep.shape[0] // 2
    near = out.shape[1]
    width = dqkv.shape[1] // 3
    for out_ref, d, u in zip(outs, (dqkv, dqkv_o), (up, up_o)):
        out_ref[...] = jnp.zeros_like(out_ref)
        out_ref[0:1, 0:u.shape[0]] = u[...][None]
        for at in (0, 2 * width):
            out_ref[1:2, at:at + width] = jnp.sum(d[:, at:at + width].astype(f32), axis=0, keepdims=True)
        for i, v in enumerate(shared):
            out_ref[2 + i:3 + i, 384:384 + v.shape[0]] = v[...][None]
    exact = lax.Precision.HIGHEST
    groups = lax.broadcasted_iota(jnp.int32, (4 * heads, out.shape[2]), 1) // 8
    groups = jnp.where(groups == lax.broadcasted_iota(jnp.int32, groups.shape, 0), 1.0, 0.0)
    for ax in range(2):
        t = lax.dot_general(groups, out[ax], NT, precision=exact, preferred_element_type=f32)
        for h in range(2 * heads):
            line = jnp.concatenate([t[2 * h:2 * h + 1] - t[2 * h + 1:2 * h + 2], t[2 * h + 1:2 * h + 2]], 1)
            outs[h // heads][2 + h % heads:3 + h % heads, 128 * (ax + 1):128 * (ax + 1) + 2 * near] = line
    seq = jnp.zeros((2 * heads, 128), f32)
    m = lax.broadcasted_iota(jnp.int32, (128, 128), 0)
    lane = lax.broadcasted_iota(jnp.int32, (128, 128), 1)
    for i, base in enumerate((-128, 0, 0, 128, 128, 256, -MAX_DIST - 128, MAX_DIST + 256)):
        d = base - m
        b = jnp.where(d > 0, BUCKETS // 2, 0)
        for e in bucket_edges(BUCKETS, MAX_DIST):
            b = b + jnp.where(jnp.abs(d) >= e, 1, 0)
        seq = seq + jnp.dot(toep[:, i, :], jnp.where(b == lane, 1.0, 0.0), precision=exact, preferred_element_type=f32)
    for h in range(2 * heads):
        outs[h // heads][2 + h % heads:3 + h % heads, 0:128] = seq[h:h + 1]


def pack_sums(sums, dqkv, dqkv_o, up, up_o, shared, rows, lanes, after=()):
    flat = [x for s in sums for x in s]
    return pl.pallas_call(
        partial(skip_refs, partial(tables_kernel, parts=len(sums)), len(flat) + 4 + len(shared), len(after)),
        out_shape=(jax.ShapeDtypeStruct((rows, lanes), f32),) * 2,
        in_specs=[VMEM] * (len(flat) + 4 + len(shared)) + [ANY] * len(after),
        out_specs=(VMEM, VMEM),
        compiler_params=pltpu.CompilerParams(vmem_limit_bytes=VM),
        name="pack_sums",
        cost_estimate=USUAL,
    )(*flat, dqkv, dqkv_o, up, up_o, *shared, *after)


def unpack_kernel(mine_ref, theirs_ref, *refs, width, heads):
    refs, total_ref = refs[:-1], refs[-1]
    total_ref[...] = mine_ref[...] + theirs_ref[...]
    bq, bv, bu, ts, tx, ty = refs[:6]
    bq[...] = total_ref[1, 0:width]
    bv[...] = total_ref[1, 2 * width:3 * width]
    bu[...] = total_ref[0, 0:bu.shape[0]]
    for i, t in enumerate((ts, tx, ty)):
        t[...] = total_ref[2:2 + heads, 128 * i:128 * i + t.shape[1]]
    for i, v in enumerate(refs[6:]):
        v[...] = total_ref[2 + i, 384:384 + v.shape[0]]


def unpack_sums(mine, theirs, width, heads, shapes):
    return pl.pallas_call(
        partial(unpack_kernel, width=width, heads=heads),
        out_shape=[jax.ShapeDtypeStruct(s, f32) for s in shapes],
        in_specs=[VMEM, VMEM],
        out_specs=[VMEM] * len(shapes),
        scratch_shapes=[pltpu.VMEM(mine.shape, f32)],
        name="unpack_sums",
        cost_estimate=USUAL,
    )(mine, theirs)


def tokens_kernel(core_ref, first_ref, d_ref, do_ref, wq_ref, wk_ref, wv_ref, got_ref, peer_ref, out_ref, total_ref):
    W = wq_ref.shape[1]
    total = first_ref[...]
    for i, w in enumerate((wq_ref, wk_ref, wv_ref)):
        total = total + lax.dot_general(d_ref[:, i * W:(i + 1) * W], w[...], NT, preferred_element_type=f32)
    total_ref[...] = total
    n = got_ref.shape[0]
    for i, w in enumerate((got_ref, peer_ref)):
        at = pl.ds(pl.multiple_of(jnp.bitwise_xor(core_ref[0], i) * n, n), n)
        total_ref[:, at] += lax.dot_general(do_ref[...], w[...], NT, preferred_element_type=f32)
    out_ref[...] = total_ref[...].reshape(out_ref.shape)


def grad_tokens_of(core, first, d, do, weights, seq, after=()):
    rows, width = first.shape
    RB = 240
    block = lambda n: pl.BlockSpec((RB, n), lambda i: (i, 0))
    whole = lambda w: pl.BlockSpec(w.shape, lambda i: (0, 0))
    return pl.pallas_call(
        partial(skip_refs, tokens_kernel, 9, len(after)),
        grid=(rows // RB,),
        in_specs=[SMEM, block(width), block(d.shape[1]), block(d.shape[1])] + [whole(w) for w in weights] + [ANY] * len(after),
        out_specs=pl.BlockSpec((RB, 1, width), lambda i: (i, 0, 0)),
        out_shape=jax.ShapeDtypeStruct((seq, 1, width), f32),
        scratch_shapes=[pltpu.VMEM((RB, width), f32)],
        compiler_params=pltpu.CompilerParams(vmem_limit_bytes=VM),
        name="grad_tokens",
        cost_estimate=USUAL,
    )(core, first, d, do, *weights, *after)

def swap(value, axis, bit=1):
    count = lax.axis_size(axis)
    return lax.ppermute(value, axis, [(i, i ^ bit) for i in range(count)])


def half_of(value, axis, which):
    size = value.shape[axis] // 2
    return lax.dynamic_slice_in_dim(value, which * size, size, axis)


def join(mine, theirs, which, axis=0):
    place = jnp.arange(2).reshape(2, 1, 1)
    return jnp.where(place == which, mine[None], theirs[None]).reshape(-1, mine.shape[1])


def far_bits():
    count = lax.axis_size("far")
    bits = []
    bit = 1
    while bit < count:
        bits.append(bit)
        bit *= 2
    return bits


def add_low(a, b):
    return (a.astype(f32) + b.astype(f32)).astype(bf)


def far_side(bit):
    return (lax.axis_index("far") // bit) % 2


def arrive(moment, *values):
    return lax.optimization_barrier(values + (moment,))[:-1]


def halve(parts, bit):
    at = far_side(bit)

    def pick(part, which):
        if isinstance(part, tuple):
            return jnp.concatenate([half_of(p, 0, which) for p in part], 1)
        return half_of(part, 0, which)

    add = lambda which: sum(pick(p, which).astype(f32) for p in parts).astype(bf)
    return add(at), swap(add(1 - at), "far", bit)


def double(total, got, bit, base):
    if total.shape[0] % 16:
        return join(total, got, far_side(bit), 0), base
    return jnp.concatenate([total, got], 0), base + [far_side(bit)]


def spread(total, got, base, widths, turned):
    place = 0
    for side in base[::-1]:
        place = 2 * place + side
    block = total.shape[0] >> len(base)
    info = jnp.stack([lax.axis_index("core"), place]).astype(jnp.int32)
    return finish(total, got, info, block, widths, turned)


def norm_parts(values):
    center = values - jnp.mean(values, axis=1, keepdims=True)
    inverse = lax.rsqrt(jnp.mean(center * center, axis=1, keepdims=True) + layer_eps)
    return center * inverse, inverse


def norm_back(grad_scaled, scaled, inverse):
    return inverse * (
        grad_scaled
        - jnp.mean(grad_scaled, axis=1, keepdims=True)
        - scaled * jnp.mean(grad_scaled * scaled, axis=1, keepdims=True)
    )


def gelu_parts(v):
    cdf = 0.5 * (1.0 + lax.erf(v * (0.5 ** 0.5)))
    pdf = jnp.exp(-0.5 * v * v) * (1.0 / math.sqrt(2.0 * math.pi))
    return v * cdf, cdf + v * pdf


def mm(a, b):
    return jnp.dot(a, b, preferred_element_type=f32)


def mm_nt(a, b):
    return lax.dot_general(a, b, (((1,), (1,)), ((), ())), preferred_element_type=f32)


def mm_tn(a, b):
    return lax.dot_general(a, b, (((0,), (0,)), ((), ())), preferred_element_type=f32)


def per_device(
    tokens, text_len, box_coords, w_query, b_query, w_key, w_value, b_value, w_out, b_out,
    table_seq, table_x, table_y, gain_attn, shift_attn, w_up, b_up, w_down, b_down,
    gain_ffn, shift_ffn, cotangent,
):
    seq, width = tokens.shape[1:]
    rows = -(-seq // 240) * 240
    lanes = -(-rows // PT) * PT
    local = w_query.shape[1]
    heads = local // HEAD_DIM
    hidden = w_up.shape[1]
    core = lax.axis_index("core")
    small_rows = -(-(2 + max(heads, 6)) // 8) * 8

    small, up_bias, bias, vectors = pack(
        [b_query, b_value, b_up, table_seq, table_x, table_y],
        [b_out, gain_attn, shift_attn, b_down, gain_ffn, shift_ffn], width, hidden,
    )
    small_o = swap(small, "tensor")
    halves, _ = lax.optimization_barrier((jnp.concatenate([half_of(w, 0, core) for w in (w_query, w_key, w_value)], 1), small))
    qkv_half = swap(halves, "tensor")
    b_out, gain_attn, shift_attn, b_down, gain_ffn, shift_ffn = vectors
    which = core.reshape(1).astype(jnp.int32)

    x = jnp.pad(tokens[0], ((0, rows - seq), (0, 0)))
    g = jnp.pad(cotangent[0], ((0, rows - seq), (0, 0)))
    both = project(which, x, [w_query, w_key, w_value], bias)
    q, k, v = (both, 0), (both, 1), (both, 2)
    idx, toep, toep_o, up_bias_o, bias_o = prep(text_len, box_coords[0], small, small_o, heads, rows, lanes)

    def fetched(got):
        return join(got, swap(got, "core"), core)

    qkv_half, out_half, up_half, idx, both = lax.optimization_barrier(
        (qkv_half, half_of(w_out, 0, core), half_of(w_up, 0, core), idx, both)
    )
    q, k, v = (both, 0), (both, 1), (both, 2)
    qkv_peer = swap(qkv_half, "core")
    out_half = swap(out_half, "tensor")
    up_half = swap(up_half, "tensor")
    ctx, *prob = attn_fwd(q, k, v, local, idx, toep, small, (qkv_half,))
    qkv_peer, out_half, down_half, ctx = arrive(ctx, qkv_peer, out_half, half_of(w_down, 0, core), ctx)
    down_half = swap(down_half, "tensor")
    both_o = project(which, x, [qkv_half, qkv_peer], bias_o)
    q_o, k_o, v_o = (both_o, 0), (both_o, 1), (both_o, 2)
    wo_o = fetched(out_half)
    ctx_o, *prob_o = attn_fwd(q_o, k_o, v_o, local, idx, toep_o, small_o, (wo_o,))
    wu_o = fetched(up_half)

    attn = mm(ctx, w_out) + mm(ctx_o, wo_o) + b_out
    n1, inv1 = norm_parts(x.astype(f32) + attn)
    normed = n1 * gain_attn + shift_attn
    low = normed.astype(bf)
    act, slope = gelu_parts(mm(low, w_up) + up_bias)
    act_o, slope_o = gelu_parts(mm(low, wu_o) + up_bias_o)
    act, act_o = act.astype(bf), act_o.astype(bf)
    down_half, act, act_o = lax.optimization_barrier((down_half, act, act_o))
    wd_o = fetched(down_half)
    slope, slope_o = slope.astype(bf), slope_o.astype(bf)
    branch = mm(act, w_down) + mm(act_o, wd_o) + b_down
    n2, inv2 = norm_parts(normed + branch)
    output = (n2 * gain_ffn + shift_ffn).astype(bf)[:seq][None]

    gf = g.astype(f32)
    grad_gain_ffn = jnp.sum(gf * n2, axis=0)
    grad_shift_ffn = jnp.sum(gf, axis=0)
    grad_mid = norm_back(gf * gain_ffn, n2, inv2)
    gb = grad_mid.astype(bf)
    grad_b_down = jnp.sum(gb.astype(f32), axis=0)

    def terms(left, right):
        sent = swap(mm_tn(half_of(left, 1, 1 - core), right).astype(bf), "core")
        return mm_tn(half_of(left, 1, core), right).astype(bf), sent

    def add_three(a, b, c):
        return (a.astype(f32) + b.astype(f32) + c.astype(f32)).astype(bf)

    bits = far_bits()
    down_o = add_low(*terms(act_o, gb))
    down_x = swap(down_o, "tensor")
    gh_o = (mm_nt(gb, wd_o) * slope_o.astype(f32)).astype(bf)
    gb, down_o = lax.optimization_barrier((gb, down_o))
    down = terms(act, gb)
    gh = (mm_nt(gb, w_down) * slope.astype(f32)).astype(bf)
    grad_b_up = jnp.sum(gh.astype(f32), axis=0)
    grad_b_up_o = jnp.sum(gh_o.astype(f32), axis=0)
    up_o = terms(low, gh_o)
    up = terms(low, gh)
    grad_normed = mm_nt(gh, w_up) + mm_nt(gh_o, wu_o) + grad_mid
    grad_gain_attn = jnp.sum(grad_normed * n1, axis=0)
    grad_shift_attn = jnp.sum(grad_normed, axis=0)
    grad_first = norm_back(grad_normed * gain_attn, n1, inv1)
    ga = grad_first.astype(bf)
    grad_b_out = jnp.sum(ga.astype(f32), axis=0)
    out_o = terms(ga, ctx_o)
    out = terms(ga, ctx)
    gc_o = mm_nt(ga, wo_o).astype(bf)
    gc = mm_nt(ga, w_out).astype(bf)
    up_o = add_low(jnp.concatenate([up_o[0], out_o[0]], 1), jnp.concatenate([up_o[1], out_o[1]], 1))
    up_x = swap(up_o, "tensor")
    up = list(zip(up, out))
    dqkv_o, gs_o = attn_bwd(q_o, k_o, v_o, local, gc_o, *prob_o, (up_o, output))
    down_x, = arrive(gs_o, down_x)
    down = halve([*down, down_x], bits[0])
    qkv_o = add_low(*terms(x, dqkv_o))
    qkv_x = swap(qkv_o, "tensor")
    dqkv, gs = attn_bwd(q, k, v, local, gc, *prob, (down[0], qkv_o))

    up_x, down_in = arrive(gs, up_x, down[1])
    down = halve([down[0], down_in], bits[1])
    up = halve([*up, up_x], bits[0])
    qkv = terms(x, dqkv)
    sums = [hist(gs, gs_o, idx, 0, 6, (up[0], down[0], qkv[0]))]

    down_in, up_in, qkv_core, qkv_x = arrive(sums[-1][0], down[1], up[1], qkv[1], qkv_x)
    down = [down[0], down_in]
    for bit in bits[3:]:
        down = halve(down, bit)
    down = halve(down, bits[2])
    up = halve([up[0], up_in], bits[1])
    qkv = halve([qkv[0], qkv_core, qkv_x], bits[0])
    sums.append(hist(gs, gs_o, idx, 6, 3, (qkv[0], up[0], down[0])))

    down_in, up_in, qkv_in = arrive(sums[-1][0], down[1], up[1], qkv[1])
    down_base, up_base, base = [], [], []
    down = add_low(down[0], down_in)
    for bit in bits[:2:-1]:
        down, down_base = double(down, swap(down, "far", bit), bit, down_base)
    down_in = swap(down, "far", bits[2])
    up = [up[0], up_in]
    for bit in bits[3:]:
        up = halve(up, bit)
    up = halve(up, bits[2])
    qkv = halve([qkv[0], qkv_in], bits[1])
    sums.append(hist(gs, gs_o, idx, 9, 3, (up[0], qkv[0], down)))

    down_in, up_in, qkv_in = arrive(sums[-1][0], down_in, up[1], qkv[1])
    down, down_base = double(down, down_in, bits[2], down_base)
    down_in = swap(down, "far", bits[1])
    up = add_low(up[0], up_in)
    for bit in bits[:2:-1]:
        up, up_base = double(up, swap(up, "far", bit), bit, up_base)
    up_in = swap(up, "far", bits[2])
    qkv = [qkv[0], qkv_in]
    for bit in bits[3:]:
        qkv = halve(qkv, bit)
    qkv = halve(qkv, bits[2])
    sums.append(hist(gs, gs_o, idx, 12, 3, (up, qkv[0], down)))

    down_in, up_in, qkv_in = arrive(sums[-1][0], down_in, up_in, qkv[1])
    qkv = add_low(qkv[0], qkv_in)
    for bit in bits[:2:-1]:
        qkv, base = double(qkv, swap(qkv, "far", bit), bit, base)
    qkv_in = swap(qkv, "far", bits[2])
    up, up_base = double(up, up_in, bits[2], up_base)
    up_in = swap(up, "far", bits[1])
    down, down_base = double(down, down_in, bits[1], down_base)
    down_in = swap(down, "far", bits[0])
    shared = [grad_b_out, grad_gain_attn, grad_shift_attn, grad_b_down, grad_gain_ffn, grad_shift_ffn]
    payload, payload_o = pack_sums(sums, dqkv, dqkv_o, grad_b_up, grad_b_up_o, shared, small_rows, hidden, (up, qkv, down))

    total, total_in = payload, swap(payload_o, "tensor")
    up_in, qkv_in = arrive(payload, up_in, qkv_in)
    qkv, base = double(qkv, qkv_in, bits[2], base)
    qkv_in = swap(qkv, "far", bits[1])
    up, up_base = double(up, up_in, bits[1], up_base)
    up_in = swap(up, "far", bits[0])
    total_in, up = arrive(up, total_in, up)
    total = total + total_in
    total_in = swap(total, "core")
    grad_tokens = grad_tokens_of(which, grad_first, dqkv, dqkv_o, [w_query, w_key, w_value, qkv_half, qkv_peer], seq, (up, qkv, total))

    qkv_in, total_in, down_in = arrive(grad_tokens, qkv_in, total_in, down_in)
    qkv, base = double(qkv, qkv_in, bits[1], base)
    qkv_in = swap(qkv, "far", bits[0])
    total = total + total_in
    total_in = swap(total, "far", bits[0])
    down, down_base = double(down, down_in, bits[0], down_base)
    down_in = swap(down, "core")
    up_in, qkv, down, total = arrive(qkv, up_in, qkv, down, total)
    up, up_base = double(up, up_in, bits[0], up_base)
    up_in = swap(up, "core")
    down_in, total_in, up = arrive(up, down_in, total_in, up)
    total = total + total_in
    total_in = swap(total, "far", bits[1])
    grad_w_down, = spread(down, down_in, down_base, (width,), (False,))
    total_in, up_in = arrive(grad_w_down, total_in, up_in)
    total = total + total_in
    total_in = swap(total, "far", bits[2])
    grad_w_up, grad_w_out = spread(up, up_in, up_base, (hidden, local), (False, True))
    total_in, qkv_in = arrive(grad_w_up, total_in, qkv_in)
    qkv, base = double(qkv, qkv_in, bits[0], base)
    qkv_in = swap(qkv, "core")
    total_last = total_in
    for bit in bits[3:]:
        total = total + total_last
        total_last = swap(total, "far", bit)
    grads_qkv = spread(qkv, qkv_in, base, (local,) * 3, (False,) * 3)
    grads_qkv = spread(qkv, qkv_in, base, (local,) * 3, (False,) * 3)
    grad_tokens = grad_tokens.reshape(1, seq, width)
    shapes = [(local,), (local,), (hidden,), table_seq.shape, table_x.shape, table_y.shape] + [(width,)] * 6
    pieces = unpack_sums(total, total_last, local, heads, shapes)
    g_bq, g_bv, g_bu, g_ts, g_tx, g_ty, g_bo, g_ga, g_sa, g_bd, g_gf, g_sf = pieces
    return (
        output, grad_tokens,
        grads_qkv[0], g_bq, grads_qkv[1], grads_qkv[2], g_bv,
        grad_w_out, g_bo, g_ts, g_tx, g_ty, g_ga, g_sa, grad_w_up, g_bu, grad_w_down, g_bd, g_gf, g_sf,
    )


def solution(mesh):
    grid = mesh.devices.shape
    mesh = jax.sharding.Mesh(mesh.devices.reshape(grid[0] // 2, 2, grid[1]), ("far", "core", "tensor"))
    every = ("far", "core", "tensor")
    item = P(every, None, None)
    column, row, split, copied = P(None, "tensor"), P("tensor", None), P("tensor"), P()
    return jax.shard_map(
        per_device,
        mesh=mesh,
        in_specs=(
            item, P(every), item, column, split, column, column, split, row, copied,
            row, row, row, copied, copied, column, split, row, copied, copied, copied, item,
        ),
        out_specs=(
            item, item, column, split, column, column, split, row, copied, row, row, row,
            copied, copied, column, split, row, copied, copied, copied,
        ),
        check_vma=False,
    )
```

```python
from functools import partial
import math

import jax
import jax.numpy as jnp
from jax import lax
from jax.experimental import pallas as pl
from jax.experimental.pallas import tpu as pltpu
from jax.sharding import PartitionSpec as P

HEAD_DIM = 64
BUCKETS = 32
MAX_DIST = 128
BUCKETS_2D = 64
MAX_DIST_2D = 256
TEXT = 512
layer_eps = 1e-05

f32 = jnp.float32
bf = jnp.bfloat16
i16 = jnp.int16
PT = 256
NT = (((1,), (1,)), ((), ()))
VM = 56 << 20

USUAL = pl.CostEstimate(flops=10_000_000_000, bytes_accessed=1, transcendentals=0)


SHORT = pl.CostEstimate(flops=1, bytes_accessed=1, transcendentals=0)


def bucket_edges(buckets, farthest):
    exact=buckets//4
    r=list(range(1,exact+1))
    for k in range(1,exact):
        r.append(int(math.ceil(exact*(farthest/exact)**(k/exact)-1e-09)))
    return r
def lane_gather(table, index):
    dn=lax.GatherDimensionNumbers(offset_dims=(),collapsed_slice_dims=(1,),start_index_map=(1,),operand_batching_dims=(0,),start_indices_batching_dims=(0,))
    return lax.gather(table,index[...,None],dn,(1,1),mode=lax.GatherScatterMode.PROMISE_IN_BOUNDS)

def prep_kernel(len_ref, box_ref, own_ref, oth_ref, idx_ref, toep_ref, toep_o_ref, up_ref, bias_ref, line_ref, col_ref, *, seq):
    up_ref[...] = oth_ref[0:1, :].astype(f32)
    bias_ref[...] = oth_ref[1:2, 0:bias_ref.shape[1]].astype(f32)
    rows, lanes = idx_ref.shape[1:]
    heads = toep_ref.shape[0]
    edges = bucket_edges(BUCKETS_2D, MAX_DIST_2D)
    near = [e for e in edges if e < 128]
    far = [e for e in edges if e >= 128]
    n = len_ref[0]
    rb = 16
    line_ref[...] = jnp.zeros_like(line_ref)
    line_ref[0:2, 0:seq] = box_ref[...].astype(f32)
    col_ref[...] = line_ref[...].T
    lane = lax.broadcasted_iota(jnp.int32, (rb, 128), 1)
    tab = jnp.zeros((rb, 128), jnp.int32)
    for e in near:
        tab = tab + jnp.where(lane >= e, 1, 0)
    tab = tab.astype(i16)

    def body(i, _):
        r = pl.ds(pl.multiple_of(i * rb, rb), rb)
        place = lax.broadcasted_iota(jnp.int32, (rb, 128), 0) + i * rb
        ok = ((place < n) | (place >= TEXT)) & (place < seq)
        for ax in range(2):
            col = jnp.broadcast_to(col_ref[r, ax:ax + 1], (rb, 128))
            for c in range(lanes // 128):
                cs = slice(c * 128, (c + 1) * 128)
                d = col - line_ref[ax:ax + 1, cs]
                a = jnp.abs(d)
                b = jnp.where(d > 0, float(BUCKETS_2D // 2), 0.0)
                for e in far:
                    b = b + jnp.where(a >= e, 1.0, 0.0)
                b = b.astype(jnp.int32).astype(i16) + lane_gather(tab, jnp.minimum(a, 127.0).astype(jnp.int32).astype(i16))
                if ax == 1:
                    b = jnp.where(ok, b.astype(jnp.int32), BUCKETS_2D).astype(i16)
                idx_ref[ax, r, cs] = b
        return 0

    lax.fori_loop(0, rows // rb, body, 0, unroll=5)
    for j in range(5):
        d = lax.broadcasted_iota(jnp.int32, (128, 128), 0) - lax.broadcasted_iota(jnp.int32, (128, 128), 1) + 128 * (j - 2)
        a = jnp.abs(d)
        b = jnp.zeros_like(d)
        for e in bucket_edges(BUCKETS, MAX_DIST):
            b = b + jnp.where(a >= e, 1, 0)
        b = (b + jnp.where(d > 0, BUCKETS // 2, 0)).astype(i16)
        for src, dst in ((own_ref, toep_ref), (oth_ref, toep_o_ref)):
            for h in range(heads):
                dst[h, j * 128:(j + 1) * 128, :] = lane_gather(jnp.broadcast_to(src[2 + h:3 + h, 0:128], (128, 128)), b)


VMEM = pl.BlockSpec(memory_space=pltpu.VMEM)
SMEM = pl.BlockSpec(memory_space=pltpu.SMEM)
ANY = pl.BlockSpec(memory_space=pl.ANY)


def prep(length, box, own, oth, heads, rows, lanes):
    seq = box.shape[1]
    toep = jax.ShapeDtypeStruct((heads, 640, 128), bf)
    return pl.pallas_call(
        partial(prep_kernel, seq=seq),
        out_shape=(
            jax.ShapeDtypeStruct((2, rows, lanes), i16), toep, toep,
            jax.ShapeDtypeStruct((1, own.shape[1]), f32), jax.ShapeDtypeStruct((1, 3 * heads * HEAD_DIM), f32),
        ),
        in_specs=[SMEM, VMEM, VMEM, VMEM],
        out_specs=(VMEM,) * 5,
        scratch_shapes=[pltpu.VMEM((8, lanes), f32), pltpu.VMEM((lanes, 8), f32)],
        compiler_params=pltpu.CompilerParams(vmem_limit_bytes=VM),
        name="buckets",
        cost_estimate=USUAL,
    )(length, box, own, oth)


def pack_kernel(bq, bv, bu, ts, tx, ty, *refs):
    vectors, small_ref, up_ref, bias_ref, rows = refs[:6], refs[6], refs[7], refs[8], refs[9:]
    local = bq.shape[0]
    heads = ts.shape[0]
    hidden = bu.shape[0]
    small_ref[...] = jnp.zeros_like(small_ref)
    small_ref[0:1, 0:hidden] = bu[...][None]
    small_ref[1:2, 0:local] = bq[...][None]
    small_ref[1:2, 2 * local:3 * local] = bv[...][None]
    small_ref[2:2 + heads, 0:ts.shape[1]] = ts[...]
    small_ref[2:2 + heads, 128:128 + tx.shape[1]] = tx[...]
    small_ref[2:2 + heads, 256:384] = jnp.full((heads, 128), -1e9, bf)
    small_ref[2:2 + heads, 256:256 + ty.shape[1]] = ty[...]
    up_ref[...] = bu[...].astype(f32)[None]
    bias_ref[...] = jnp.zeros_like(bias_ref)
    bias_ref[0:1, 0:local] = bq[...].astype(f32)[None]
    bias_ref[0:1, 2 * local:3 * local] = bv[...].astype(f32)[None]
    for v, row in zip(vectors, rows):
        row[...] = v[...].astype(f32)[None]


def pack(split, copied, width, hidden):
    row = lambda n: jax.ShapeDtypeStruct((1, n), f32)
    out = pl.pallas_call(
        pack_kernel,
        out_shape=[jax.ShapeDtypeStruct((16, hidden), bf), row(hidden), row(3 * split[0].shape[0])] + [row(width)] * 6,
        in_specs=[VMEM] * 12,
        out_specs=[VMEM] * 9,
        name="pack",
        cost_estimate=USUAL,
    )(*split, *copied)
    return out[0], out[1], out[2], out[3:]


def project_kernel(core_ref, x_ref, *refs):
    weights, bias_ref, out_ref = refs[:-2], refs[-2], refs[-1]
    if len(weights) == 3:
        at = 0
        for w in weights:
            n = w.shape[1]
            part = jnp.dot(x_ref[...], w[...], preferred_element_type=f32) + bias_ref[:, at:at + n]
            out_ref[:, at:at + n] = part.astype(bf)
            at += n
        return
    n = weights[0].shape[0]
    total = bias_ref[...]
    for i, w in enumerate(weights):
        at = pl.multiple_of(jnp.bitwise_xor(core_ref[0], i) * n, n)
        total = total + jnp.dot(x_ref[:, pl.ds(at, n)], w[...], preferred_element_type=f32)
    out_ref[...] = total.astype(bf)


def project(core, x, weights, bias):
    rows, width = x.shape
    RB = rows // 3
    whole = lambda w: pl.BlockSpec(w.shape, lambda i: (0, 0))
    return pl.pallas_call(
        project_kernel,
        grid=(rows // RB,),
        in_specs=[SMEM, pl.BlockSpec((RB, width), lambda i: (i, 0))] + [whole(w) for w in weights] + [whole(bias)],
        out_specs=pl.BlockSpec((RB, bias.shape[1]), lambda i: (i, 0)),
        out_shape=jax.ShapeDtypeStruct((rows, bias.shape[1]), bf),
        compiler_params=pltpu.CompilerParams(vmem_limit_bytes=VM),
        name="project",
        cost_estimate=USUAL,
    )(core, x, *weights, bias)


def keep_rows(x,first_row,limit):
    rr=lax.broadcasted_iota(jnp.int32,(x.shape[0],1),0)+first_row
    return jnp.where(rr<limit,x,jnp.zeros_like(x))

def fwd_kernel(q_ref, k_ref, v_ref, idx_ref, toep_ref, small_ref, ctx_ref, p_ref, inv_ref, s_ref, qm_ref):
    H,rows,PT=p_ref.shape
    nch=PT//128
    tile=pl.program_id(0)
    lane=lax.broadcasted_iota(jnp.int32,(1,128),1)
    first=lane<HEAD_DIM
    for hp in range(H//2):
        hs=slice(hp*128,(hp+1)*128)
        q=keep_rows(q_ref[:,hs],tile*PT,rows)*jnp.asarray(HEAD_DIM**-0.5,bf)
        for h in range(2):
            qm=jnp.where(first if h==0 else ~first,q,jnp.zeros_like(q))
            qm_ref[2*hp+h]=qm
    tabs=[(jnp.broadcast_to(small_ref[2+h:3+h,128:256],(16,128)),jnp.broadcast_to(small_ref[2+h:3+h,256:384],(16,128))) for h in range(H)]
    cuts=[(h,c) for c in range(nch) for h in range(H)]
    BR=144
    def block1(i,ms):
        r=pl.ds(pl.multiple_of(i*BR,16),BR)
        for h in range(H):
            s_ref[h,r,:]=lax.dot_general(k_ref[r,h//2*128:(h//2+1)*128],qm_ref[h],NT,preferred_element_type=f32)
        for g in range(BR//16):
            ms=pass1(i*(BR//16)+g,ms)
        return ms
    def pass1(g,ms):
        r0=pl.multiple_of(g*16,16); r=pl.ds(r0,16)
        sb=r0//128; off=r0%128
        out=[]
        for c in range(nch):
            cs=slice(c*128,(c+1)*128)
            ix=idx_ref[0,r,cs]; iy=idx_ref[1,r,cs]
            tr=pl.ds(pl.multiple_of((jnp.clip(sb-(tile*nch+c),-2,2)+2)*128+off,16),16)
            gx=[lane_gather(tabs[h][0],ix) for h in range(H)]
            gy=[lane_gather(tabs[h][1],iy) for h in range(H)]
            for h in range(H):
                s=s_ref[h,r,cs]+gx[h].astype(f32)+gy[h].astype(f32)+toep_ref[h,tr,:].astype(f32)
                s_ref[h,r,cs]=s
                out.append(jnp.maximum(ms[c*H+h],jnp.maximum(s[:8],s[8:])))
        return tuple(out)
    ms=lax.fori_loop(0,rows//BR,block1,tuple(jnp.full((8,128),-jnp.inf,f32) for _ in cuts))
    ms=[jnp.max(m,axis=0,keepdims=True) for m in ms]
    def pass2(g,ls):
        r=pl.ds(pl.multiple_of(g*16,16),16)
        out=[]
        for i,(h,c) in enumerate(cuts):
            cs=slice(c*128,(c+1)*128)
            e=jnp.exp(s_ref[h,r,cs]-ms[i])
            p_ref[h,r,cs]=e.astype(bf)
            out.append(ls[i]+(e[:8]+e[8:]))
        return tuple(out)
    ls=lax.fori_loop(0,rows//16,pass2,tuple(jnp.zeros((8,128),f32) for _ in cuts),unroll=5)
    inv=[1.0/jnp.sum(l,axis=0,keepdims=True) for l in ls]
    for i,(h,c) in enumerate(cuts):
        inv_ref[h:h+1,c*128:(c+1)*128]=inv[i]
    for hp in range(H//2):
        hs=slice(hp*128,(hp+1)*128)
        vt=v_ref[:,hs].T
        o=[jnp.dot(vt[h*64:(h+1)*64],p_ref[2*hp+h],preferred_element_type=f32)*inv_ref[2*hp+h:2*hp+h+1,:] for h in range(2)]
        ctx_ref[:,hs]=jnp.concatenate(o,0).T.astype(bf)

def attn_fwd(q, k, v, W, idx, toep, small, after=()):
    rows = q[0].shape[0]
    H = W // HEAD_DIM
    lanes = idx.shape[2]
    whole = lambda shape: pl.BlockSpec(shape, lambda i: (0,) * len(shape))
    column = lambda at: pl.BlockSpec((rows, W), lambda i: (0, at))
    return pl.pallas_call(
        partial(skip_refs, fwd_kernel, 6, len(after)),
        grid=(lanes // PT,),
        in_specs=[pl.BlockSpec((PT, W), lambda i: (i, q[1])), column(k[1]), column(v[1]), pl.BlockSpec((2, rows, PT), lambda i: (0, 0, i)), whole(toep.shape), whole(small.shape)] + [ANY] * len(after),
        out_specs=(pl.BlockSpec((PT, W), lambda i: (i, 0)), pl.BlockSpec((H, rows, PT), lambda i: (0, 0, i)), pl.BlockSpec((H, PT), lambda i: (0, i))),
        out_shape=(jax.ShapeDtypeStruct((rows, W), bf), jax.ShapeDtypeStruct((H, rows, lanes), bf), jax.ShapeDtypeStruct((H, lanes), f32)),
        scratch_shapes=[pltpu.VMEM((H, rows, PT), f32), pltpu.VMEM((H, PT, 128), bf)],
        compiler_params=pltpu.CompilerParams(vmem_limit_bytes=VM),
        name="attn_fwd",
        cost_estimate=USUAL,
    )(q[0], k[0], v[0], idx, toep, small, *after)


def skip_refs(kernel, first, count, *refs):
    kernel(*refs[:first], *refs[first + count:])


def bwd_kernel(q_ref, k_ref, v_ref, do_ref, p_ref, inv_ref, out_ref, gs_ref, dp_ref, dka, dva, dqa):
    H,rows,PT=p_ref.shape
    nch=PT//128
    tile=pl.program_id(0); last=pl.num_programs(0)-1
    lane=lax.broadcasted_iota(jnp.int32,(1,128),1)
    first=lane<HEAD_DIM
    scale=HEAD_DIM**-0.5
    cuts=[(h,c) for c in range(nch) for h in range(H)]
    split=lambda x: (jnp.where(first,x,jnp.zeros_like(x)),jnp.where(first,jnp.zeros_like(x),x))
    for hp in range(H//2):
        hs=slice(hp*128,(hp+1)*128)
        dm=split(keep_rows(do_ref[:,hs],tile*PT,rows))
        for h in range(2):
            dp_ref[2*hp+h]=lax.dot_general(v_ref[:,hs],dm[h],NT,preferred_element_type=f32)
    def pass1(g,ds):
        r=pl.ds(pl.multiple_of(g*16,16),16)
        out=[]
        for i,(h,c) in enumerate(cuts):
            cs=slice(c*128,(c+1)*128)
            t=p_ref[h,r,cs].astype(f32)*dp_ref[h,r,cs]
            out.append(ds[i]+(t[:8]+t[8:]))
        return tuple(out)
    ds=lax.fori_loop(0,rows//16,pass1,tuple(jnp.zeros((8,128),f32) for _ in cuts),unroll=9)
    iv=[inv_ref[h:h+1,c*128:(c+1)*128] for h,c in cuts]
    ds=[jnp.sum(d,axis=0,keepdims=True)*v*v for d,v in zip(ds,iv)]
    def pass2(g,_):
        r=pl.ds(pl.multiple_of(g*16,16),16)
        for i,(h,c) in enumerate(cuts):
            cs=slice(c*128,(c+1)*128)
            gs_ref[h,r,cs]=(p_ref[h,r,cs].astype(f32)*(dp_ref[h,r,cs]*iv[i]-ds[i])).astype(bf)
        return 0
    lax.fori_loop(0,rows//16,pass2,0,unroll=9)
    @pl.when(tile==0)
    def _():
        dka[...]=jnp.zeros_like(dka); dva[...]=jnp.zeros_like(dva)
    pad=jnp.zeros((-H%8,PT),f32)
    col=jnp.concatenate([inv_ref[...],pad],0).T
    for hp in range(H//2):
        hs=slice(hp*128,(hp+1)*128)
        kt=k_ref[:,hs].T
        o=[jnp.dot(kt[h*64:(h+1)*64],gs_ref[2*hp+h],preferred_element_type=f32) for h in range(2)]
        dq=(jnp.concatenate(o,0)*scale).T.astype(bf)
        dqa[pl.ds(pl.multiple_of(tile*PT,PT),PT),hs]=dq
        qm=split(keep_rows(q_ref[:,hs],tile*PT,rows))
        dm=split(keep_rows(do_ref[:,hs],tile*PT,rows).astype(f32))
        dm=[(dm[h]*col[:,2*hp+h:2*hp+h+1]).astype(bf) for h in range(2)]
        dka[:,hs]+=jnp.dot(gs_ref[2*hp],qm[0],preferred_element_type=f32)+jnp.dot(gs_ref[2*hp+1],qm[1],preferred_element_type=f32)
        dva[:,hs]+=jnp.dot(p_ref[2*hp],dm[0],preferred_element_type=f32)+jnp.dot(p_ref[2*hp+1],dm[1],preferred_element_type=f32)
    @pl.when(tile==last)
    def _():
        W=dka.shape[1]
        out_ref[:,0:W]=dqa[0:rows,:]
        out_ref[:,W:2*W]=(dka[...]*scale).astype(bf)
        out_ref[:,2*W:]=dva[...].astype(bf)

def attn_bwd(q, k, v, W, do, p, inv, after=()):
    rows = do.shape[0]
    H = W // HEAD_DIM
    lanes = p.shape[2]
    column = lambda at: pl.BlockSpec((rows, W), lambda i: (0, at))
    big = pl.BlockSpec((H, rows, PT), lambda i: (0, 0, i))
    return pl.pallas_call(
        partial(skip_refs, bwd_kernel, 6, len(after)),
        grid=(lanes // PT,),
        in_specs=[pl.BlockSpec((PT, W), lambda i: (i, q[1])), column(k[1]), column(v[1]), pl.BlockSpec((PT, W), lambda i: (i, 0)), big, pl.BlockSpec((H, PT), lambda i: (0, i))] + [ANY] * len(after),
        out_specs=(pl.BlockSpec((rows, 3 * W), lambda i: (0, 0)), big),
        out_shape=(jax.ShapeDtypeStruct((rows, 3 * W), bf), jax.ShapeDtypeStruct((H, rows, lanes), bf)),
        scratch_shapes=[pltpu.VMEM((H, rows, PT), f32), pltpu.VMEM((rows, W), f32), pltpu.VMEM((rows, W), f32), pltpu.VMEM((lanes, W), bf)],
        compiler_params=pltpu.CompilerParams(vmem_limit_bytes=VM),
        name="attn_bwd",
        cost_estimate=SHORT,
    )(q[0], k[0], v[0], do, p, inv, *after)


def finish_kernel(info_ref, mine_ref, theirs_ref, *refs, block, widths, turned):
    rows = mine_ref.shape[0]
    count = rows // block
    n = len(widths)
    outs, wide, sems = refs[:n], refs[n:2 * n], refs[2 * n]
    copies = []
    for p, src in enumerate((mine_ref, theirs_ref)):
        for j in range(count):
            rs = slice(j * block, (j + 1) * block)
            place = pl.multiple_of((jnp.bitwise_xor(info_ref[0], p) * count + jnp.bitwise_xor(info_ref[1], j)) * block, block)
            at = 0
            for i in range(n):
                part = src[rs, at:at + widths[i]].astype(f32)
                at += widths[i]
                if turned[i]:
                    wide[i][pl.ds(place, block), :] = part
                else:
                    wide[i][p, rs, :] = part
                    copy = pltpu.make_async_copy(wide[i].at[p, rs, :], outs[i].at[pl.ds(place, block), :], sems.at[p, j, i])
                    copy.start()
                    copies.append(copy)
    for i in range(n):
        if turned[i]:
            refs[2 * n + 1][...] = wide[i][...].T
            copy = pltpu.make_async_copy(refs[2 * n + 1], outs[i], sems.at[0, 0, i])
            copy.start()
            copies.append(copy)
    for copy in copies:
        copy.wait()


def finish(mine, theirs, info, block, widths, turned):
    rows = mine.shape[0]
    return pl.pallas_call(
        partial(finish_kernel, block=block, widths=widths, turned=turned),
        in_specs=[SMEM, VMEM, VMEM],
        out_specs=[ANY] * len(widths),
        out_shape=[jax.ShapeDtypeStruct((w, 2 * rows) if t else (2 * rows, w), f32) for w, t in zip(widths, turned)],
        scratch_shapes=[pltpu.VMEM((2 * rows, w) if t else (2, rows, w), f32) for w, t in zip(widths, turned)]
        + [pltpu.SemaphoreType.DMA((2, rows // block, len(widths)))]
        + [pltpu.VMEM((w, 2 * rows), f32) for w, t in zip(widths, turned) if t],
        compiler_params=pltpu.CompilerParams(vmem_limit_bytes=VM),
        name="finish",
        cost_estimate=USUAL,
    )(info, mine, theirs)


def hist_kernel(gs_ref, go_ref, idx_ref, out_ref, toep_ref, acc, accT, *, part):
    H, rows, lanes = gs_ref.shape
    SB = 16
    heads = 2 * H
    near = BUCKETS_2D // 2
    step = pl.program_id(0)

    @pl.when(step == 0)
    def _():
        acc[...] = jnp.zeros_like(acc)
        accT[...] = jnp.zeros_like(accT)

    iota = lax.broadcasted_iota(jnp.int32, (near, lanes), 0).astype(i16)
    one = jnp.ones((near, lanes), bf)
    zero = jnp.zeros((near, lanes), bf)

    def body(i, _):
        r = pl.ds(pl.multiple_of(i * SB, SB), SB)
        s0 = (part + step) * rows + i * SB
        sb = s0 // 128
        off = pl.multiple_of(s0 % 128, SB)
        idx = [idx_ref[ax, r, :] for ax in range(2)]
        positive = [(x >= near).astype(i16).astype(jnp.int32) > 0 for x in idx]
        cols = [[], []]
        for ref in (gs_ref, go_ref):
            for h in range(H):
                full = ref[h, r, :].astype(f32)
                k = len(cols[0])
                for c in range(lanes // 128):
                    at = pl.ds(pl.multiple_of((jnp.clip(sb - c, -2, 2) + 2) * 128 + off, SB), SB)
                    accT[k, at, :] += full[:, c * 128:(c + 1) * 128]
                for ax in range(2):
                    some = jnp.where(positive[ax], full, 0.0)
                    cols[ax].append([jnp.concatenate([full[t:t + 8], some[t:t + 8]], 0).astype(bf) for t in (0, 8)])
        for ax in range(2):
            ix = jnp.bitwise_and(idx[ax], jnp.asarray(near - 1, i16))
            left = []
            right = []
            for t in range(2):
                left.append(jnp.concatenate([jnp.where(iota == ix[t * 8 + p:t * 8 + p + 1, :], one, zero) for p in range(8)], 0))
                right.append(jnp.concatenate([x[t] for x in cols[ax]], 0))
            acc[ax] += lax.dot_general(jnp.concatenate(left, 1), jnp.concatenate(right, 1), NT, preferred_element_type=f32)
        return 0

    lax.fori_loop(0, rows // SB, body, 0, unroll=3)

    @pl.when(step == pl.num_programs(0) - 1)
    def _():
        lane = lax.broadcasted_iota(jnp.int32, (near, heads * SB), 1) % 8
        for ax in range(2):
            t = jnp.zeros((near, heads * SB), f32)
            for p in range(8):
                t = t + jnp.where(lane == p, acc[ax, p * near:(p + 1) * near, :], 0.0)
            out_ref[ax] = t
        lane8 = lax.broadcasted_iota(jnp.int32, (8, 128), 1)
        row8 = lax.broadcasted_iota(jnp.int32, (8, 128), 0)
        kept = {}
        for g in range(16):
            turned = lane8 + row8 + 8 * g
            wraps = turned >= 128
            turned = jnp.where(wraps, turned - 128, turned)
            for h in range(heads):
                for j in (-1, 0, 1):
                    at = (j + 2) * 128 + 8 * g
                    x = lane_gather(accT[h, at:at + 8, :], turned)
                    for k, part_sum in enumerate((jnp.where(wraps, 0.0, x), jnp.where(wraps, x, 0.0))):
                        key = (h, 2 * (j + 1) + k)
                        kept[key] = part_sum if g == 0 else kept[key] + part_sum
        for h in range(heads):
            for k in range(6):
                toep_ref[h, k:k + 1, :] = jnp.sum(kept[h, k], axis=0, keepdims=True)
            toep_ref[h, 6:7, :] = jnp.sum(accT[h, 0:128, :], axis=0, keepdims=True)
            toep_ref[h, 7:8, :] = jnp.sum(accT[h, 512:640, :], axis=0, keepdims=True)


def hist(gs, go, idx, part, steps, after=()):
    H, rows, lanes = gs.shape
    SB = 48
    near = BUCKETS_2D // 2
    big = pl.BlockSpec((H, SB, lanes), lambda i: (0, part + i, 0))
    return pl.pallas_call(
        partial(skip_refs, partial(hist_kernel, part=part), 3, len(after)),
        grid=(steps,),
        in_specs=[big, big, pl.BlockSpec((2, SB, lanes), lambda i: (0, part + i, 0))] + [ANY] * len(after),
        out_specs=(pl.BlockSpec((2, near, 2 * H * 16), lambda i: (0, 0, 0)), pl.BlockSpec((2 * H, 8, 128), lambda i: (0, 0, 0))),
        out_shape=(jax.ShapeDtypeStruct((2, near, 2 * H * 16), f32), jax.ShapeDtypeStruct((2 * H, 8, 128), f32)),
        scratch_shapes=[pltpu.VMEM((2, 8 * near, 2 * H * 16), f32), pltpu.VMEM((2 * H, 640, 128), f32)],
        compiler_params=pltpu.CompilerParams(vmem_limit_bytes=VM),
        name="table_sums",
        cost_estimate=USUAL,
    )(gs, go, idx, *after)


def tables_kernel(*refs, parts):
    sums = refs[:2 * parts]
    dqkv, dqkv_o, up, up_o = refs[2 * parts:2 * parts + 4]
    shared = refs[2 * parts + 4:-2]
    outs = refs[-2:]
    out = sums[0][...]
    toep = sums[1][...]
    for i in range(1, parts):
        out = out + sums[2 * i][...]
        toep = toep + sums[2 * i + 1][...]
    heads = toep.shape[0] // 2
    near = out.shape[1]
    width = dqkv.shape[1] // 3
    for out_ref, d, u in zip(outs, (dqkv, dqkv_o), (up, up_o)):
        out_ref[...] = jnp.zeros_like(out_ref)
        out_ref[0:1, 0:u.shape[0]] = u[...][None]
        for at in (0, 2 * width):
            out_ref[1:2, at:at + width] = jnp.sum(d[:, at:at + width].astype(f32), axis=0, keepdims=True)
        for i, v in enumerate(shared):
            out_ref[2 + i:3 + i, 384:384 + v.shape[0]] = v[...][None]
    exact = lax.Precision.HIGHEST
    groups = lax.broadcasted_iota(jnp.int32, (4 * heads, out.shape[2]), 1) // 8
    groups = jnp.where(groups == lax.broadcasted_iota(jnp.int32, groups.shape, 0), 1.0, 0.0)
    for ax in range(2):
        t = lax.dot_general(groups, out[ax], NT, precision=exact, preferred_element_type=f32)
        for h in range(2 * heads):
            line = jnp.concatenate([t[2 * h:2 * h + 1] - t[2 * h + 1:2 * h + 2], t[2 * h + 1:2 * h + 2]], 1)
            outs[h // heads][2 + h % heads:3 + h % heads, 128 * (ax + 1):128 * (ax + 1) + 2 * near] = line
    seq = jnp.zeros((2 * heads, 128), f32)
    m = lax.broadcasted_iota(jnp.int32, (128, 128), 0)
    lane = lax.broadcasted_iota(jnp.int32, (128, 128), 1)
    for i, base in enumerate((-128, 0, 0, 128, 128, 256, -MAX_DIST - 128, MAX_DIST + 256)):
        d = base - m
        b = jnp.where(d > 0, BUCKETS // 2, 0)
        for e in bucket_edges(BUCKETS, MAX_DIST):
            b = b + jnp.where(jnp.abs(d) >= e, 1, 0)
        seq = seq + jnp.dot(toep[:, i, :], jnp.where(b == lane, 1.0, 0.0), precision=exact, preferred_element_type=f32)
    for h in range(2 * heads):
        outs[h // heads][2 + h % heads:3 + h % heads, 0:128] = seq[h:h + 1]


def pack_sums(sums, dqkv, dqkv_o, up, up_o, shared, rows, lanes, after=()):
    flat = [x for s in sums for x in s]
    return pl.pallas_call(
        partial(skip_refs, partial(tables_kernel, parts=len(sums)), len(flat) + 4 + len(shared), len(after)),
        out_shape=(jax.ShapeDtypeStruct((rows, lanes), f32),) * 2,
        in_specs=[VMEM] * (len(flat) + 4 + len(shared)) + [ANY] * len(after),
        out_specs=(VMEM, VMEM),
        compiler_params=pltpu.CompilerParams(vmem_limit_bytes=VM),
        name="pack_sums",
        cost_estimate=USUAL,
    )(*flat, dqkv, dqkv_o, up, up_o, *shared, *after)


def unpack_kernel(mine_ref, theirs_ref, *refs, width, heads):
    refs, total_ref = refs[:-1], refs[-1]
    total_ref[...] = mine_ref[...] + theirs_ref[...]
    bq, bv, bu, ts, tx, ty = refs[:6]
    bq[...] = total_ref[1, 0:width]
    bv[...] = total_ref[1, 2 * width:3 * width]
    bu[...] = total_ref[0, 0:bu.shape[0]]
    for i, t in enumerate((ts, tx, ty)):
        t[...] = total_ref[2:2 + heads, 128 * i:128 * i + t.shape[1]]
    for i, v in enumerate(refs[6:]):
        v[...] = total_ref[2 + i, 384:384 + v.shape[0]]


def unpack_sums(mine, theirs, width, heads, shapes):
    return pl.pallas_call(
        partial(unpack_kernel, width=width, heads=heads),
        out_shape=[jax.ShapeDtypeStruct(s, f32) for s in shapes],
        in_specs=[VMEM, VMEM],
        out_specs=[VMEM] * len(shapes),
        scratch_shapes=[pltpu.VMEM(mine.shape, f32)],
        name="unpack_sums",
        cost_estimate=USUAL,
    )(mine, theirs)


def tokens_kernel(core_ref, first_ref, d_ref, do_ref, wq_ref, wk_ref, wv_ref, got_ref, peer_ref, out_ref, total_ref):
    W = wq_ref.shape[1]
    total = first_ref[...]
    for i, w in enumerate((wq_ref, wk_ref, wv_ref)):
        total = total + lax.dot_general(d_ref[:, i * W:(i + 1) * W], w[...], NT, preferred_element_type=f32)
    total_ref[...] = total
    n = got_ref.shape[0]
    for i, w in enumerate((got_ref, peer_ref)):
        at = pl.ds(pl.multiple_of(jnp.bitwise_xor(core_ref[0], i) * n, n), n)
        total_ref[:, at] += lax.dot_general(do_ref[...], w[...], NT, preferred_element_type=f32)
    out_ref[...] = total_ref[...].reshape(out_ref.shape)


def grad_tokens_of(core, first, d, do, weights, seq, after=()):
    rows, width = first.shape
    RB = 240
    block = lambda n: pl.BlockSpec((RB, n), lambda i: (i, 0))
    whole = lambda w: pl.BlockSpec(w.shape, lambda i: (0, 0))
    return pl.pallas_call(
        partial(skip_refs, tokens_kernel, 9, len(after)),
        grid=(rows // RB,),
        in_specs=[SMEM, block(width), block(d.shape[1]), block(d.shape[1])] + [whole(w) for w in weights] + [ANY] * len(after),
        out_specs=pl.BlockSpec((RB, 1, width), lambda i: (i, 0, 0)),
        out_shape=jax.ShapeDtypeStruct((seq, 1, width), f32),
        scratch_shapes=[pltpu.VMEM((RB, width), f32)],
        compiler_params=pltpu.CompilerParams(vmem_limit_bytes=VM),
        name="grad_tokens",
        cost_estimate=USUAL,
    )(core, first, d, do, *weights, *after)

def swap(value, axis, bit=1):
    count = lax.axis_size(axis)
    return lax.ppermute(value, axis, [(i, i ^ bit) for i in range(count)])


def half_of(value, axis, which):
    size = value.shape[axis] // 2
    return lax.dynamic_slice_in_dim(value, which * size, size, axis)


def join(mine, theirs, which, axis=0):
    place = jnp.arange(2).reshape(2, 1, 1)
    return jnp.where(place == which, mine[None], theirs[None]).reshape(-1, mine.shape[1])


def far_bits():
    count = lax.axis_size("far")
    bits = []
    bit = 1
    while bit < count:
        bits.append(bit)
        bit *= 2
    return bits


def add_low(a, b):
    return (a.astype(f32) + b.astype(f32)).astype(bf)


def far_side(bit):
    return (lax.axis_index("far") // bit) % 2


def arrive(moment, *values):
    return lax.optimization_barrier(values + (moment,))[:-1]


def halve(parts, bit):
    at = far_side(bit)

    def pick(part, which):
        if isinstance(part, tuple):
            return jnp.concatenate([half_of(p, 0, which) for p in part], 1)
        return half_of(part, 0, which)

    add = lambda which: sum(pick(p, which).astype(f32) for p in parts).astype(bf)
    return add(at), swap(add(1 - at), "far", bit)


def double(total, got, bit, base):
    if total.shape[0] % 16:
        return join(total, got, far_side(bit), 0), base
    return jnp.concatenate([total, got], 0), base + [far_side(bit)]


def places(base):
    place = 0
    for side in base[::-1]:
        place = 2 * place + side
    return jnp.stack([lax.axis_index("core"), place]).astype(jnp.int32)


def spread(total, got, base, widths, turned, usual):
    block = total.shape[0] >> len(base)
    info = usual if len(base) == 3 else places(base)
    return finish(total, got, info, block, widths, turned)


def norm_parts(values):
    center = values - jnp.mean(values, axis=1, keepdims=True)
    inverse = lax.rsqrt(jnp.mean(center * center, axis=1, keepdims=True) + layer_eps)
    return center * inverse, inverse


def norm_back(grad_scaled, scaled, inverse):
    return inverse * (
        grad_scaled
        - jnp.mean(grad_scaled, axis=1, keepdims=True)
        - scaled * jnp.mean(grad_scaled * scaled, axis=1, keepdims=True)
    )


def gelu_parts(v):
    cdf = 0.5 * (1.0 + lax.erf(v * (0.5 ** 0.5)))
    pdf = jnp.exp(-0.5 * v * v) * (1.0 / math.sqrt(2.0 * math.pi))
    return v * cdf, cdf + v * pdf


def mm(a, b):
    return jnp.dot(a, b, preferred_element_type=f32)


def mm_nt(a, b):
    return lax.dot_general(a, b, (((1,), (1,)), ((), ())), preferred_element_type=f32)


def mm_tn(a, b):
    return lax.dot_general(a, b, (((0,), (0,)), ((), ())), preferred_element_type=f32)


def per_device(
    tokens, text_len, box_coords, w_query, b_query, w_key, w_value, b_value, w_out, b_out,
    table_seq, table_x, table_y, gain_attn, shift_attn, w_up, b_up, w_down, b_down,
    gain_ffn, shift_ffn, cotangent,
):
    seq, width = tokens.shape[1:]
    rows = -(-seq // 240) * 240
    lanes = -(-rows // PT) * PT
    local = w_query.shape[1]
    heads = local // HEAD_DIM
    hidden = w_up.shape[1]
    core = lax.axis_index("core")
    small_rows = -(-(2 + max(heads, 6)) // 8) * 8

    small, up_bias, bias, vectors = pack(
        [b_query, b_value, b_up, table_seq, table_x, table_y],
        [b_out, gain_attn, shift_attn, b_down, gain_ffn, shift_ffn], width, hidden,
    )
    small_o = swap(small, "tensor")
    halves, _ = lax.optimization_barrier((jnp.concatenate([half_of(w, 0, core) for w in (w_query, w_key, w_value)], 1), small))
    qkv_half = swap(halves, "tensor")
    b_out, gain_attn, shift_attn, b_down, gain_ffn, shift_ffn = vectors
    which = core.reshape(1).astype(jnp.int32)

    x = jnp.pad(tokens[0], ((0, rows - seq), (0, 0)))
    g = jnp.pad(cotangent[0], ((0, rows - seq), (0, 0)))
    both = project(which, x, [w_query, w_key, w_value], bias)
    q, k, v = (both, 0), (both, 1), (both, 2)
    idx, toep, toep_o, up_bias_o, bias_o = prep(text_len, box_coords[0], small, small_o, heads, rows, lanes)

    def fetched(got):
        return join(got, swap(got, "core"), core)

    qkv_half, out_half, up_half, idx, both = lax.optimization_barrier(
        (qkv_half, half_of(w_out, 0, core), half_of(w_up, 0, core), idx, both)
    )
    q, k, v = (both, 0), (both, 1), (both, 2)
    qkv_peer = swap(qkv_half, "core")
    out_half = swap(out_half, "tensor")
    up_half = swap(up_half, "tensor")
    ctx, *prob = attn_fwd(q, k, v, local, idx, toep, small, (qkv_half,))
    near = [far_side(bit) for bit in far_bits()[2::-1]]
    qkv_peer, out_half, down_half, ctx, info = arrive(ctx, qkv_peer, out_half, half_of(w_down, 0, core), ctx, places(near))
    down_half = swap(down_half, "tensor")
    both_o = project(which, x, [qkv_half, qkv_peer], bias_o)
    q_o, k_o, v_o = (both_o, 0), (both_o, 1), (both_o, 2)
    wo_o = fetched(out_half)
    ctx_o, *prob_o = attn_fwd(q_o, k_o, v_o, local, idx, toep_o, small_o, (wo_o,))
    wu_o = fetched(up_half)

    attn = mm(ctx, w_out) + mm(ctx_o, wo_o) + b_out
    n1, inv1 = norm_parts(x.astype(f32) + attn)
    normed = n1 * gain_attn + shift_attn
    low = normed.astype(bf)
    act, slope = gelu_parts(mm(low, w_up) + up_bias)
    act_o, slope_o = gelu_parts(mm(low, wu_o) + up_bias_o)
    act, act_o = act.astype(bf), act_o.astype(bf)
    down_half, act, act_o = lax.optimization_barrier((down_half, act, act_o))
    wd_o = fetched(down_half)
    slope, slope_o = slope.astype(bf), slope_o.astype(bf)
    branch = mm(act, w_down) + mm(act_o, wd_o) + b_down
    n2, inv2 = norm_parts(normed + branch)
    output = (n2 * gain_ffn + shift_ffn).astype(bf)[:seq][None]

    gf = g.astype(f32)
    grad_gain_ffn = jnp.sum(gf * n2, axis=0)
    grad_shift_ffn = jnp.sum(gf, axis=0)
    grad_mid = norm_back(gf * gain_ffn, n2, inv2)
    gb = grad_mid.astype(bf)
    grad_b_down = jnp.sum(gb.astype(f32), axis=0)

    def terms(left, right):
        sent = swap(mm_tn(half_of(left, 1, 1 - core), right).astype(bf), "core")
        return mm_tn(half_of(left, 1, core), right).astype(bf), sent

    def add_three(a, b, c):
        return (a.astype(f32) + b.astype(f32) + c.astype(f32)).astype(bf)

    bits = far_bits()
    down_o = add_low(*terms(act_o, gb))
    down_x = swap(down_o, "tensor")
    gh_o = (mm_nt(gb, wd_o) * slope_o.astype(f32)).astype(bf)
    gb, down_o = lax.optimization_barrier((gb, down_o))
    down = terms(act, gb)
    gh = (mm_nt(gb, w_down) * slope.astype(f32)).astype(bf)
    grad_b_up = jnp.sum(gh.astype(f32), axis=0)
    grad_b_up_o = jnp.sum(gh_o.astype(f32), axis=0)
    up_o = terms(low, gh_o)
    up = terms(low, gh)
    grad_normed = mm_nt(gh, w_up) + mm_nt(gh_o, wu_o) + grad_mid
    grad_gain_attn = jnp.sum(grad_normed * n1, axis=0)
    grad_shift_attn = jnp.sum(grad_normed, axis=0)
    grad_first = norm_back(grad_normed * gain_attn, n1, inv1)
    ga = grad_first.astype(bf)
    grad_b_out = jnp.sum(ga.astype(f32), axis=0)
    out_o = terms(ga, ctx_o)
    out = terms(ga, ctx)
    gc_o = mm_nt(ga, wo_o).astype(bf)
    gc = mm_nt(ga, w_out).astype(bf)
    up_o = add_low(jnp.concatenate([up_o[0], out_o[0]], 1), jnp.concatenate([up_o[1], out_o[1]], 1))
    up_x = swap(up_o, "tensor")
    up = list(zip(up, out))
    dqkv_o, gs_o = attn_bwd(q_o, k_o, v_o, local, gc_o, *prob_o, (up_o, output))
    down_x, = arrive(gs_o, down_x)
    down = halve([*down, down_x], bits[0])
    qkv_o = add_low(*terms(x, dqkv_o))
    qkv_x = swap(qkv_o, "tensor")
    dqkv, gs = attn_bwd(q, k, v, local, gc, *prob, (down[0], qkv_o))

    up_x, down_in = arrive(gs, up_x, down[1])
    down = halve([down[0], down_in], bits[1])
    up = halve([*up, up_x], bits[0])
    qkv = terms(x, dqkv)
    sums = [hist(gs, gs_o, idx, 0, 6, (up[0], down[0], qkv[0]))]

    down_in, up_in, qkv_core, qkv_x = arrive(sums[-1][0], down[1], up[1], qkv[1], qkv_x)
    down = [down[0], down_in]
    for bit in bits[3:]:
        down = halve(down, bit)
    down = halve(down, bits[2])
    up = halve([up[0], up_in], bits[1])
    qkv = halve([qkv[0], qkv_core, qkv_x], bits[0])
    sums.append(hist(gs, gs_o, idx, 6, 3, (qkv[0], up[0], down[0])))

    down_in, up_in, qkv_in = arrive(sums[-1][0], down[1], up[1], qkv[1])
    down_base, up_base, base = [], [], []
    down = add_low(down[0], down_in)
    for bit in bits[:2:-1]:
        down, down_base = double(down, swap(down, "far", bit), bit, down_base)
    down_in = swap(down, "far", bits[2])
    up = [up[0], up_in]
    for bit in bits[3:]:
        up = halve(up, bit)
    up = halve(up, bits[2])
    qkv = halve([qkv[0], qkv_in], bits[1])
    sums.append(hist(gs, gs_o, idx, 9, 3, (up[0], qkv[0], down)))

    down_in, up_in, qkv_in = arrive(sums[-1][0], down_in, up[1], qkv[1])
    down, down_base = double(down, down_in, bits[2], down_base)
    down_in = swap(down, "far", bits[1])
    up = add_low(up[0], up_in)
    for bit in bits[:2:-1]:
        up, up_base = double(up, swap(up, "far", bit), bit, up_base)
    up_in = swap(up, "far", bits[2])
    qkv = [qkv[0], qkv_in]
    for bit in bits[3:]:
        qkv = halve(qkv, bit)
    qkv = halve(qkv, bits[2])
    sums.append(hist(gs, gs_o, idx, 12, 3, (up, qkv[0], down)))

    down_in, up_in, qkv_in = arrive(sums[-1][0], down_in, up_in, qkv[1])
    qkv = add_low(qkv[0], qkv_in)
    for bit in bits[:2:-1]:
        qkv, base = double(qkv, swap(qkv, "far", bit), bit, base)
    qkv_in = swap(qkv, "far", bits[2])
    up, up_base = double(up, up_in, bits[2], up_base)
    up_in = swap(up, "far", bits[1])
    down, down_base = double(down, down_in, bits[1], down_base)
    down_in = swap(down, "far", bits[0])
    shared = [grad_b_out, grad_gain_attn, grad_shift_attn, grad_b_down, grad_gain_ffn, grad_shift_ffn]
    payload, payload_o = pack_sums(sums, dqkv, dqkv_o, grad_b_up, grad_b_up_o, shared, small_rows, hidden, (up, qkv, down))

    total, total_in = payload, swap(payload_o, "tensor")
    up_in, qkv_in = arrive(payload, up_in, qkv_in)
    qkv, base = double(qkv, qkv_in, bits[2], base)
    qkv_in = swap(qkv, "far", bits[1])
    up, up_base = double(up, up_in, bits[1], up_base)
    up_in = swap(up, "far", bits[0])
    total_in, up = arrive(up, total_in, up)
    total = total + total_in
    total_in = swap(total, "core")
    grad_tokens = grad_tokens_of(which, grad_first, dqkv, dqkv_o, [w_query, w_key, w_value, qkv_half, qkv_peer], seq, (up, qkv, total))

    qkv_in, total_in, down_in = arrive(grad_tokens, qkv_in, total_in, down_in)
    qkv, base = double(qkv, qkv_in, bits[1], base)
    qkv_in = swap(qkv, "far", bits[0])
    total = total + total_in
    total_in = swap(total, "far", bits[0])
    down, down_base = double(down, down_in, bits[0], down_base)
    down_in = swap(down, "core")
    up_in, qkv, down, total = arrive(qkv, up_in, qkv, down, total)
    up, up_base = double(up, up_in, bits[0], up_base)
    up_in = swap(up, "core")
    down_in, total_in, up = arrive(up, down_in, total_in, up)
    total = total + total_in
    total_in = swap(total, "far", bits[1])
    grad_w_down, = spread(down, down_in, down_base, (width,), (False,), info)
    total_in, up_in = arrive(grad_w_down, total_in, up_in)
    total = total + total_in
    total_in = swap(total, "far", bits[2])
    grad_w_up, grad_w_out = spread(up, up_in, up_base, (hidden, local), (False, True), info)
    total_in, qkv_in = arrive(grad_w_up, total_in, qkv_in)
    qkv, base = double(qkv, qkv_in, bits[0], base)
    qkv_in = swap(qkv, "core")
    total_last = total_in
    for bit in bits[3:]:
        total = total + total_last
        total_last = swap(total, "far", bit)
    grads_qkv = spread(qkv, qkv_in, base, (local,) * 3, (False,) * 3, info)
    grads_qkv = spread(qkv, qkv_in, base, (local,) * 3, (False,) * 3, info)
    grad_tokens = grad_tokens.reshape(1, seq, width)
    shapes = [(local,), (local,), (hidden,), table_seq.shape, table_x.shape, table_y.shape] + [(width,)] * 6
    pieces = unpack_sums(total, total_last, local, heads, shapes)
    g_bq, g_bv, g_bu, g_ts, g_tx, g_ty, g_bo, g_ga, g_sa, g_bd, g_gf, g_sf = pieces
    return (
        output, grad_tokens,
        grads_qkv[0], g_bq, grads_qkv[1], grads_qkv[2], g_bv,
        grad_w_out, g_bo, g_ts, g_tx, g_ty, g_ga, g_sa, grad_w_up, g_bu, grad_w_down, g_bd, g_gf, g_sf,
    )


def solution(mesh):
    grid = mesh.devices.shape
    mesh = jax.sharding.Mesh(mesh.devices.reshape(grid[0] // 2, 2, grid[1]), ("far", "core", "tensor"))
    every = ("far", "core", "tensor")
    item = P(every, None, None)
    column, row, split, copied = P(None, "tensor"), P("tensor", None), P("tensor"), P()
    return jax.shard_map(
        per_device,
        mesh=mesh,
        in_specs=(
            item, P(every), item, column, split, column, column, split, row, copied,
            row, row, row, copied, copied, column, split, row, copied, copied, copied, item,
        ),
        out_specs=(
            item, item, column, split, column, column, split, row, copied, row, row, row,
            copied, copied, column, split, row, copied, copied, copied,
        ),
        check_vma=False,
    )
```
